32 devices in a mesh: section: 4 (over y, x), dp: 8 (over z, core).
Axes of the slice: x: 2, y: 2, z: 4, core: 2. Of those that a mesh axis runs over, the one named last changes fastest.
Arguments:
- inputs: bfloat16 [4096, 768], P('dp'), may hold values from -6 to 6
- cotangent: bfloat16 [4096, 768], P('dp'), may hold values from -6 to 6
- long_count: int32 [8, 2], P('dp'), may hold values from 0 to 1, as said below
- timesteps: int32 [8, 2, 2], P('dp'), may hold values from 0 to 999
- w_qkv: bfloat16 [4, 768, 2304], P('section'), may hold values from -0.21875 to 0.21875
- w_out: bfloat16 [4, 768, 768], P('section'), may hold values from -0.625 to 0.625
- w_in: bfloat16 [4, 768, 3072], P('section'), may hold values from -0.21875 to 0.21875
- w_down: bfloat16 [4, 3072, 768], P('section'), may hold values from -0.109375 to 0.109375
- ada_weight: bfloat16 [4, 128, 4608], P('section'), may hold values from -0.5 to 0.5
Outputs:
- hidden_out: bfloat16 [4, 4096, 768], P('section', 'dp')
- grad_in: bfloat16 [4, 4096, 768], P('section', 'dp')
- grad_qkv: float32 [4, 768, 2304], P('section', 'dp')
- grad_out: float32 [4, 768, 768], P('section', 'dp')
- grad_up: float32 [4, 768, 3072], P('section', 'dp')
- grad_down: float32 [4, 3072, 768], P('section', 'dp')
- grad_ada: float32 [4, 128, 4608], P('section', 'dp')
The draws below stay inside these ranges and needn't reach their ends.
Inputs may be any that keep to these rules, and one draw needn't show every extreme that they name: `long_count`: 1 where the micro-batch holds one sequence of 256 tokens, 0 where it holds 2 sequences of 128; both values occur in every draw.
All inputs are finite; a program needn't handle non-finite values.
Results may differ from the reference program's by a relative error of at most 0.015.
Values may be sent and summed in bfloat16 or wider, within the bound.
A program may use at most 576 MiB of HBM per device.

```python
import math
import jax
import jax.numpy as jnp
from jax import lax

D = 768
HEADS = 12
HEAD_DIM = 64
FF = 3072
TEMB = 128
MB = 256
SHORT = 128
MICRO = 2
SLOTS = 2
LAYERS = 4
TOKENS = 4096
N_SECTION = 4
N_DP = 8


def draw_long_count(key, part):
    key = jax.random.fold_in(key, 7)
    key_flags, key_place = jax.random.split(key)
    count_all = N_DP * MICRO
    flag_values = jax.random.randint(key_flags, (count_all,), 0, 2)
    position = jax.random.randint(key_place, (), 0, count_all)
    flag_values = flag_values.at[position].set(1)
    flag_values = flag_values.at[(position + 1) % count_all].set(0)
    return flag_values.reshape(N_DP, MICRO).astype(jnp.int32)


def touch_ends(result, stream_key, low, high):
    index_at = [jax.random.randint(jax.random.fold_in(stream_key, axis), (), 0, length) for axis, length in enumerate(result.shape)]
    longest = result.shape.index(max(result.shape))
    next_to = index_at[:longest] + [(index_at[longest] + 1) % result.shape[longest]] + index_at[longest + 1:]
    return result.at[tuple(index_at)].set(low).at[tuple(next_to)].set(high)


def shard_levels(stream_key, shape, cuts, low, top_value):
    level, own = 1.0, jax.random.fold_in(stream_key, 6)
    for dim, parts in cuts:
        heights = jnp.exp(jax.random.uniform(jax.random.fold_in(own, dim), (parts,), jnp.float32, low / len(cuts), top_value / len(cuts)))
        level = level * jnp.repeat(heights, shape[dim] // parts).reshape([-1 if axis == dim else 1 for axis in range(len(shape))])
    return level


def noise(rng, dims, width, reach, shards=(), kind=jnp.bfloat16):
    gain = shard_levels(rng, dims, shards, -0.22, 0.18) if shards else 1.0
    result = jax.random.normal(rng, dims, jnp.float32) * width * gain
    return jnp.minimum(jnp.maximum(result, -reach), reach).astype(kind)


def setup_inputs(seed: int = 0) -> dict:
    key_of = jax.random.split(jax.random.key(seed), 10)
    return {
        "inputs": noise(key_of[0], (TOKENS, D), 1.0, 6.0, ((0, 8),)),
        "cotangent": noise(key_of[1], (TOKENS, D), 1.0, 6.0, ((0, 8),)),
        "long_count": draw_long_count(jax.random.fold_in(key_of[9], 71), 0),
        "timesteps": touch_ends(jax.random.randint(key_of[3], (N_DP, MICRO, SLOTS), 0, 1000), jax.random.fold_in(key_of[3], 1), 0, 999).astype(jnp.int32),
        "w_qkv": noise(key_of[4], (N_SECTION, D, 3 * D), D ** -0.5, 0.21875, ((0, 4),)),
        "w_out": noise(key_of[5], (N_SECTION, D, D), (D // 8) ** -0.5, 0.625, ((0, 4),)),
        "w_in": noise(key_of[6], (N_SECTION, D, FF), D ** -0.5, 0.21875, ((0, 4),)),
        "w_down": noise(key_of[7], (N_SECTION, FF, D), FF ** -0.5, 0.109375, ((0, 4),)),
        "ada_weight": noise(key_of[8], (N_SECTION, TEMB, 6 * D), TEMB ** -0.5, 0.5, ((0, 4),)),
    }


@jax.custom_vjp
def low(v):
    return lax.optimization_barrier(v.astype(jnp.bfloat16)).astype(jnp.float32)

@jax.custom_vjp
def low_back(v):
    return v

def low_keep(v):
    return (low(v), None)

def low_pass(kept, grad):
    return (grad,)

def back_keep(v):
    return (v, None)

def back_low(kept, grad):
    return (low(grad),)
low.defvjp(low_keep, low_pass)
low_back.defvjp(back_keep, back_low)
norm_eps = 1e-06
highest = lax.Precision.HIGHEST

def matmul(left_side, right_side):
    return jnp.dot(left_side, right_side, precision=highest)

def time_features(timestep_ids):
    half_width = TEMB // 2
    frequency = jnp.exp(-math.log(10000.0) * jnp.arange(half_width, dtype=jnp.float32) / half_width)
    angles = timestep_ids.astype(jnp.float32)[:, None] * 0.1 * frequency[None, :]
    return jnp.concatenate([jnp.sin(angles), jnp.cos(angles)], axis=1)

def normalize(values):
    centered = values - lax.optimization_barrier(jnp.mean(values, axis=-1, keepdims=True))
    variance = lax.optimization_barrier(jnp.mean(centered * centered, axis=-1, keepdims=True))
    return centered * lax.rsqrt(variance + norm_eps)

def block_forward(hidden, modulation, same_seq, w_qkv, w_out, w_in, w_down):
    shift_a, scale_a, gate_a, shift_m, scale_m, gate_m = jnp.split(modulation, 6, axis=1)
    normed = low(normalize(hidden) * (1.0 + scale_a) + shift_a)
    packed = low(low_back(matmul(normed, w_qkv)))
    queries = packed[:, :D].reshape(MB, HEADS, HEAD_DIM)
    keys_all = packed[:, D:2 * D].reshape(MB, HEADS, HEAD_DIM)
    values_all = packed[:, 2 * D:].reshape(MB, HEADS, HEAD_DIM)
    raw_scores = jnp.einsum('qhd,khd->hqk', queries, keys_all, precision=highest)
    scores = jnp.where(same_seq[None], low_back(raw_scores) * HEAD_DIM ** (-0.5), -1e+30)
    exponent = jnp.exp(scores - lax.optimization_barrier(jnp.max(scores, axis=-1, keepdims=True)))
    probability = exponent / lax.optimization_barrier(jnp.sum(exponent, axis=-1, keepdims=True))
    mixed = jnp.einsum('hqk,khd->qhd', low(probability), values_all, precision=highest).reshape(MB, D)
    mixed = low(low_back(mixed))
    branch = low_back(matmul(mixed, w_out))
    middle = hidden + gate_a * branch
    normed_m = low(normalize(middle) * (1.0 + scale_m) + shift_m)
    upward = low_back(matmul(normed_m, w_in))
    active = low(jax.nn.gelu(upward, approximate=True))
    output_branch = low_back(matmul(active, w_down))
    return middle + gate_m * output_branch

def micro_batch(item_data, weights):
    tokens, cot_rows, long_flag, timestep_ids = item_data
    positions = jnp.arange(MB, dtype=jnp.int32)
    slot_ids = jnp.where(long_flag == 1, 0, positions // SHORT).astype(jnp.int32)
    same_seq = slot_ids[:, None] == slot_ids[None, :]
    features = low(time_features(timestep_ids))

    def whole_stack(start_rows, offsets, w_qkv, w_out, w_in, w_down, ada_weight):
        hidden = start_rows + offsets[0]
        outputs = []
        for layer_index in range(LAYERS):
            if layer_index > 0:
                hidden = low_back(low(hidden)) + offsets[layer_index]
            modulation = jnp.take(matmul(features, ada_weight[layer_index]), slot_ids, axis=0)
            hidden = block_forward(hidden, modulation, same_seq, w_qkv[layer_index], w_out[layer_index], w_in[layer_index], w_down[layer_index])
            outputs.append(hidden)
        return (hidden, jnp.stack(outputs))
    start_rows = tokens.astype(jnp.float32)
    offsets = jnp.zeros((LAYERS, MB, D), jnp.float32)
    first_final, unused = whole_stack(start_rows, offsets, *weights)
    conditioned = start_rows + low(first_final)
    results, pullback = jax.vjp(whole_stack, conditioned, offsets, *weights)
    gradients = pullback((cot_rows.astype(jnp.float32), jnp.zeros_like(results[1])))
    return (results[1].astype(jnp.bfloat16), gradients[1].astype(jnp.bfloat16), tuple(gradients[2:]))

def reference(inputs, cotangent, long_count, timesteps, w_qkv, w_out, w_in, w_down, ada_weight):
    weights = tuple((matrix.astype(jnp.float32) for matrix in (w_qkv, w_out, w_in, w_down, ada_weight)))
    count_items = N_DP * MICRO
    items = (inputs.reshape(count_items, MB, D), cotangent.reshape(count_items, MB, D), long_count.reshape(count_items), timesteps.reshape(count_items, SLOTS))

    def visit_item(totals, item_data):
        hidden_rows, grad_rows, weight_terms = micro_batch(item_data, weights)
        totals = tuple((left_term + right_term for left_term, right_term in zip(totals, weight_terms)))
        return (totals, (hidden_rows, grad_rows))
    initial = tuple((jnp.zeros_like(matrix) for matrix in weights))
    totals, stacked = lax.scan(visit_item, initial, items)
    hidden_out = jnp.transpose(stacked[0], (1, 0, 2, 3)).reshape(LAYERS, TOKENS, D)
    grad_in = jnp.transpose(stacked[1], (1, 0, 2, 3)).reshape(LAYERS, TOKENS, D)
    return (hidden_out, grad_in, totals[0], totals[1], totals[2], totals[3], totals[4])
```

```python
import functools
import math

import jax
import jax.numpy as jnp
from jax import lax
from jax.experimental import pallas as pl
from jax.experimental.pallas import tpu as pltpu
from jax.sharding import PartitionSpec as P

HEADS = 12
TEMB = 128
SHORT = 128
TILE = 256
CHUNK = 32
norm_eps = 1e-06
MESH = pl.DeviceIdType.MESH
low = jnp.bfloat16
wide = jnp.float32


def dot_nn(a, b):
    return lax.dot_general(a, b, (((1,), (0,)), ((), ())), preferred_element_type=wide)


def dot_nt(a, b):
    return lax.dot_general(a, b, (((1,), (1,)), ((), ())), preferred_element_type=wide)


def dot_tn(a, b):
    return lax.dot_general(a, b, (((0,), (0,)), ((), ())), preferred_element_type=wide)


def fold(block):
    total = block[0:8]
    for start in range(8, block.shape[0], 8):
        total = total + block[start : start + 8]
    return total


GELU_C = math.sqrt(2.0 / math.pi)


def gelu(u):
    t = jnp.tanh(GELU_C * (u + 0.044715 * (u * u * u)))
    return 0.5 * u * (1.0 + t)


def gelu_slope(u):
    square = u * u
    t = jnp.tanh(GELU_C * (u + 0.044715 * (square * u)))
    return 0.5 * (1.0 + t) + 0.5 * u * (1.0 - t * t) * (GELU_C * (1.0 + (3.0 * 0.044715) * square))


def chain_kernel(
    sections,
    x_ref,
    cot_ref,
    mod_ref,
    bias_ref,
    wqkv_ref,
    wout_ref,
    win_ref,
    wdown_ref,
    fout_ref,
    gin_ref,
    dmod_ref,
    a1_ref,
    qkv_ref,
    o_ref,
    dattn_ref,
    a2_ref,
    du_ref,
    z_ref,
    dy_ref,
    h_s,
    m_s,
    t_s,
    do_s,
    n1_s,
    n2_s,
    r1_s,
    r2_s,
    y_s,
    frecv,
    brecv,
    fss,
    frs,
    bss,
    brs,
):
    micro, rows, width = x_ref.shape
    ff = win_ref.shape[1]
    half_rows = SHORT
    chunks = [(start, start // half_rows) for start in range(0, rows, CHUNK)]
    halves = rows // half_rows
    section = lax.axis_index("section")
    member = lax.axis_index("dp")
    right = lax.rem(section + 1, sections)
    left = lax.rem(section + sections - 1, sections)
    is_first = section == 0
    is_last = section == sections - 1

    barrier = pltpu.get_barrier_semaphore()
    for neighbour in (left, right):
        pl.semaphore_signal(barrier, inc=1, device_id=(neighbour, member), device_id_type=MESH)
    pl.semaphore_wait(barrier, 2)

    def forward_copy(job, slot):
        return pltpu.make_async_remote_copy(
            src_ref=fout_ref.at[job],
            dst_ref=frecv.at[slot],
            send_sem=fss.at[job],
            recv_sem=frs.at[slot],
            device_id=(right, member),
            device_id_type=MESH,
        )

    def backward_copy(job):
        return pltpu.make_async_remote_copy(
            src_ref=gin_ref.at[job],
            dst_ref=brecv.at[job],
            send_sem=bss.at[job],
            recv_sem=brs.at[job],
            device_id=(left, member),
            device_id_type=MESH,
        )

    def mod_row(mb, half, k):
        return mod_ref[mb, half, pl.ds(k, 1), :]

    lane = lax.broadcasted_iota(jnp.int32, (1, 128), 1)
    first_lanes = lane < 64
    masks = [first_lanes.astype(wide).astype(low), (1.0 - first_lanes.astype(wide)).astype(low)]
    scale = (width // HEADS) ** (-0.5)

    def norm_forward(src, mb, k_shift, k_scale, n_keep, r_keep, out):
        for start, half in chunks:
            span = pl.ds(start, CHUNK)
            v = src[span, :]
            centered = v - jnp.mean(v, axis=-1, keepdims=True)
            r = lax.rsqrt(jnp.mean(centered * centered, axis=-1, keepdims=True) + norm_eps)
            n = centered * r
            n_keep[mb, span, :] = n.astype(low)
            r_keep[mb, span, :] = r
            out[mb, span, :] = (
                n * (1.0 + mod_row(mb, half, k_scale)) + mod_row(mb, half, k_shift)
            ).astype(low)

    def forward_job(job, carry):
        mb = lax.rem(job, micro)

        @pl.when(jnp.logical_or(jnp.logical_not(is_first), job >= micro))
        def _():
            forward_copy(job, job).wait_recv()

        @pl.when(jnp.logical_and(is_first, job < micro))
        def _():
            h_s[...] = x_ref[mb].astype(wide)

        @pl.when(jnp.logical_and(is_first, job >= micro))
        def _():
            h_s[...] = x_ref[mb].astype(wide) + frecv[job].astype(wide)

        @pl.when(jnp.logical_not(is_first))
        def _():
            h_s[...] = frecv[job].astype(wide)

        norm_forward(h_s, mb, 0, 1, n1_s, r1_s, a1_ref)
        a1 = a1_ref[mb]
        for c in range(0, 3 * width, TILE):
            qkv_ref[mb, :, c : c + TILE] = dot_nn(a1, wqkv_ref[:, c : c + TILE]).astype(low)
        bias = bias_ref[mb]
        for c in range(0, width, 128):
            q = qkv_ref[mb, :, c : c + 128]
            k = qkv_ref[mb, :, width + c : width + c + 128]
            v = qkv_ref[mb, :, 2 * width + c : 2 * width + c + 128]
            outs = []
            for mask in masks:
                s = dot_nt(q * (mask * scale), k) + bias
                e = jnp.exp(s - jnp.max(s, axis=1, keepdims=True))
                p = (e * (1.0 / jnp.sum(e, axis=1, keepdims=True))).astype(low)
                outs.append(dot_nn(p, v))
            o_ref[mb, :, c : c + 128] = jnp.where(first_lanes, outs[0], outs[1]).astype(low)
        o = o_ref[mb]
        for c in range(0, width, TILE):
            t_s[:, c : c + TILE] = dot_nn(o, wout_ref[:, c : c + TILE])
        for start, half in chunks:
            span = pl.ds(start, CHUNK)
            attn = t_s[span, :]
            dattn_ref[mb, span, :] = attn.astype(low)
            m_s[span, :] = h_s[span, :] + mod_row(mb, half, 2) * attn
        norm_forward(m_s, mb, 3, 4, n2_s, r2_s, a2_ref)
        a2 = a2_ref[mb]
        for c in range(0, ff, TILE):
            u = dot_nn(a2, win_ref[:, c : c + TILE])
            du_ref[mb, :, c : c + TILE] = u.astype(low)
            z_ref[mb, :, c : c + TILE] = gelu(u).astype(low)
        z = z_ref[mb]
        for c in range(0, width, TILE):
            t_s[:, c : c + TILE] = dot_nn(z, wdown_ref[:, c : c + TILE])
        for start, half in chunks:
            span = pl.ds(start, CHUNK)
            y = t_s[span, :]
            y_s[mb, span, :] = y.astype(low)
            fout_ref[job, span, :] = (m_s[span, :] + mod_row(mb, half, 5) * y).astype(low)

        @pl.when(jnp.logical_or(jnp.logical_not(is_last), job < micro))
        def _():
            forward_copy(job, jnp.where(is_last, job + micro, job)).start()

        return carry

    lax.fori_loop(0, 2 * micro, forward_job, 0)

    def norm_backward(mb, k_scale, n_keep, r_keep, base, per_chunk):
        for half in range(halves):
            shift_sum = jnp.zeros((8, width), wide)
            scale_sum = jnp.zeros((8, width), wide)
            gate_sum = jnp.zeros((8, width), wide)
            for start in range(half * half_rows, (half + 1) * half_rows, CHUNK):
                span = pl.ds(start, CHUNK)
                da = t_s[span, :]
                n = n_keep[mb, span, :].astype(wide)
                r = r_keep[mb, span, :]
                shift_sum = shift_sum + fold(da)
                scale_sum = scale_sum + fold(da * n)
                dn = da * (1.0 + mod_row(mb, half, k_scale))
                dv = r * (
                    dn
                    - jnp.mean(dn, axis=-1, keepdims=True)
                    - n * jnp.mean(dn * n, axis=-1, keepdims=True)
                )
                extra = per_chunk(span, half, base[span, :] + dv)
                if extra is not None:
                    gate_sum = gate_sum + fold(extra)
            dmod_ref[mb, half, k_scale - 1, :] = jnp.sum(shift_sum, axis=0)
            dmod_ref[mb, half, k_scale, :] = jnp.sum(scale_sum, axis=0)
            if k_scale == 4:
                dmod_ref[mb, half, 2, :] = jnp.sum(gate_sum, axis=0)

    def backward_job(mb, carry):
        g_s = h_s

        @pl.when(is_last)
        def _():
            g_s[...] = cot_ref[mb].astype(wide)

        @pl.when(jnp.logical_not(is_last))
        def _():
            backward_copy(mb).wait_recv()
            g_s[...] = brecv[mb].astype(wide)

        for half in range(halves):
            gate_sum = jnp.zeros((8, width), wide)
            for start in range(half * half_rows, (half + 1) * half_rows, CHUNK):
                span = pl.ds(start, CHUNK)
                g = g_s[span, :]
                gate_sum = gate_sum + fold(g * y_s[mb, span, :].astype(wide))
                dy_ref[mb, span, :] = (mod_row(mb, half, 5) * g).astype(low)
            dmod_ref[mb, half, 5, :] = jnp.sum(gate_sum, axis=0)
        dy = dy_ref[mb]
        for c in range(0, ff, TILE):
            dz = dot_nt(dy, wdown_ref[c : c + TILE, :])
            u = du_ref[mb, :, c : c + TILE].astype(wide)
            du_ref[mb, :, c : c + TILE] = (gelu_slope(u) * dz).astype(low)
        du = du_ref[mb]
        for c in range(0, width, TILE):
            t_s[:, c : c + TILE] = dot_nt(du, win_ref[c : c + TILE, :])

        def after_mlp(span, half, dm):
            m_s[span, :] = dm
            extra = dm * dattn_ref[mb, span, :].astype(wide)
            dattn_ref[mb, span, :] = (mod_row(mb, half, 2) * dm).astype(low)
            return extra

        norm_backward(mb, 4, n2_s, r2_s, g_s, after_mlp)
        dattn = dattn_ref[mb]
        for c in range(0, width, TILE):
            do_s[:, c : c + TILE] = dot_nt(dattn, wout_ref[c : c + TILE, :]).astype(low)
        bias = bias_ref[mb]
        for c in range(0, width, 128):
            cols = [slice(i * width + c, i * width + c + 128) for i in range(3)]
            q, k, v = [qkv_ref[mb, :, cut] for cut in cols]
            do = do_s[:, c : c + 128]
            parts = []
            for mask in masks:
                s = dot_nt(k, q * (mask * scale)) + bias
                e = jnp.exp(s - jnp.max(s, axis=0, keepdims=True))
                p = e * (1.0 / jnp.sum(e, axis=0, keepdims=True))
                dp = dot_nt(v * mask, do)
                inner = jnp.sum(p * dp, axis=0, keepdims=True)
                ds = (p * (dp - inner) * scale).astype(low)
                parts.append((dot_tn(ds, k), dot_nn(ds, q), dot_nn(p.astype(low), do)))
            for i in range(3):
                qkv_ref[mb, :, cols[i]] = jnp.where(
                    first_lanes, parts[0][i], parts[1][i]
                ).astype(low)
        dqkv = qkv_ref[mb]
        for c in range(0, width, TILE):
            t_s[:, c : c + TILE] = dot_nt(dqkv, wqkv_ref[c : c + TILE, :])

        def after_attention(span, half, dh):
            gin_ref[mb, span, :] = dh.astype(low)

        norm_backward(mb, 1, n1_s, r1_s, m_s, after_attention)

        @pl.when(jnp.logical_not(is_first))
        def _():
            backward_copy(mb).start()

        return carry

    lax.fori_loop(0, micro, backward_job, 0)

    for job in range(2 * micro):

        @pl.when(jnp.logical_or(jnp.logical_not(is_last), job < micro))
        def _():
            forward_copy(job, job).wait_send()

    for job in range(micro):

        @pl.when(jnp.logical_not(is_first))
        def _():
            backward_copy(job).wait_send()


def run_chain(x, cot, mod, bias, w_qkv, w_out, w_in, w_down):
    micro, rows, width = x.shape
    ff = w_in.shape[1]
    sections = lax.axis_size("section")
    vmem = pl.BlockSpec(memory_space=pltpu.VMEM)

    def kept(columns):
        return jax.ShapeDtypeStruct((micro, rows, columns), low)

    out_shape = (
        jax.ShapeDtypeStruct((2 * micro, rows, width), low),
        kept(width),
        jax.ShapeDtypeStruct(mod.shape, wide),
        kept(width),
        kept(3 * width),
        kept(width),
        kept(width),
        kept(width),
        kept(ff),
        kept(ff),
        kept(width),
    )
    scratch = [
        pltpu.VMEM((rows, width), wide),
        pltpu.VMEM((rows, width), wide),
        pltpu.VMEM((rows, width), wide),
        pltpu.VMEM((rows, width), low),
        pltpu.VMEM((micro, rows, width), low),
        pltpu.VMEM((micro, rows, width), low),
        pltpu.VMEM((micro, rows, 1), wide),
        pltpu.VMEM((micro, rows, 1), wide),
        pltpu.VMEM((micro, rows, width), low),
        pltpu.VMEM((2 * micro, rows, width), low),
        pltpu.VMEM((micro, rows, width), low),
        pltpu.SemaphoreType.DMA((2 * micro,)),
        pltpu.SemaphoreType.DMA((2 * micro,)),
        pltpu.SemaphoreType.DMA((micro,)),
        pltpu.SemaphoreType.DMA((micro,)),
    ]
    return pl.pallas_call(
        functools.partial(chain_kernel, sections),
        out_shape=out_shape,
        in_specs=[vmem] * 8,
        out_specs=(vmem,) * len(out_shape),
        scratch_shapes=scratch,
        compiler_params=pltpu.CompilerParams(
            collective_id=0, has_side_effects=True, vmem_limit_bytes=60 * 1024 * 1024
        ),
    )(x, cot, mod, bias, w_qkv, w_out, w_in, w_down)


def time_features(timestep_ids):
    half_width = TEMB // 2
    frequency = jnp.exp(-math.log(10000.0) * jnp.arange(half_width, dtype=wide) / half_width)
    angles = timestep_ids.astype(wide)[:, None] * 0.1 * frequency[None, :]
    return jnp.concatenate([jnp.sin(angles), jnp.cos(angles)], axis=1)


def on_device(inputs, cotangent, long_count, timesteps, w_qkv, w_out, w_in, w_down, ada_weight):
    micro = long_count.shape[1]
    width = inputs.shape[1]
    rows = inputs.shape[0] // micro
    halves = rows // SHORT
    is_long = (long_count[0] == 1)[:, None]
    half_index = jnp.arange(halves, dtype=jnp.int32)[None, :]
    half_steps = jnp.where(is_long, timesteps[0][:, :1], timesteps[0][:, :halves])
    features = time_features(half_steps.reshape(-1)).astype(low)
    mod = jnp.dot(features, ada_weight[0], preferred_element_type=wide)
    mod = mod.reshape(micro, halves, 6, width)
    mod = jnp.pad(mod, ((0, 0), (0, 0), (0, 2), (0, 0)))
    slot_ids = jnp.where(is_long, 0, jnp.repeat(half_index, SHORT, axis=1))
    same = slot_ids[:, :, None] == slot_ids[:, None, :]
    bias = jnp.where(same, 0.0, -1e30).astype(wide)
    fout, gin, dmod, a1, dqkv, o, dattn, a2, du, z, dy = run_chain(
        inputs.reshape(micro, rows, width),
        cotangent.reshape(micro, rows, width),
        mod,
        bias,
        w_qkv[0],
        w_out[0],
        w_in[0],
        w_down[0],
    )

    def product(left, right):
        left = left.reshape(micro * rows, left.shape[2])
        right = right.reshape(micro * rows, right.shape[2])
        partial = dot_tn(left, right).astype(low)
        return lax.psum_scatter(partial, "dp", scatter_dimension=0, tiled=True).astype(wide)

    grad_down = product(z, dy)
    grad_up = product(a2, du)
    grad_out = product(o, dattn)
    grad_qkv = product(a1, dqkv)
    features_all = lax.all_gather(features.astype(wide), "dp", tiled=True)
    dmod_all = lax.all_gather(
        dmod[:, :, :6].reshape(micro * halves, 6 * width), "dp", tiled=True
    )
    share = TEMB // lax.axis_size("dp")
    mine = lax.dynamic_slice_in_dim(features_all, lax.axis_index("dp") * share, share, 1)
    grad_ada = lax.dot_general(
        mine, dmod_all, (((0,), (0,)), ((), ())), precision=lax.Precision.HIGHEST
    )
    hidden_out = fout[micro:].reshape(1, micro * rows, width)
    grad_in = gin.reshape(1, micro * rows, width)
    return (
        hidden_out,
        grad_in,
        grad_qkv[None],
        grad_out[None],
        grad_up[None],
        grad_down[None],
        grad_ada[None],
    )


def solution(mesh):
    placed = (
        P("dp", None),
        P("dp", None),
        P("dp", None),
        P("dp", None, None),
        P("section", None, None),
        P("section", None, None),
        P("section", None, None),
        P("section", None, None),
        P("section", None, None),
    )
    return jax.shard_map(
        on_device,
        mesh=mesh,
        in_specs=placed,
        out_specs=(P("section", "dp", None),) * 7,
        check_vma=False,
    )
```

```python
import functools
import math
from types import SimpleNamespace

import jax
import jax.numpy as jnp
from jax import lax
from jax.experimental import pallas as pl
from jax.experimental.pallas import tpu as pltpu
from jax.sharding import PartitionSpec as P

HEADS = 12
TEMB = 128
SHORT = 128
TILE = 256
CHUNK = 32
CORES = 2
DEEP = 4
norm_eps = 1e-06
MESH = pl.DeviceIdType.MESH
low = jnp.bfloat16
wide = jnp.float32


def dot_nn(a, b):
    return lax.dot_general(a, b, (((1,), (0,)), ((), ())), preferred_element_type=wide)


def dot_nt(a, b):
    return lax.dot_general(a, b, (((1,), (1,)), ((), ())), preferred_element_type=wide)


def dot_tn(a, b):
    return lax.dot_general(a, b, (((0,), (0,)), ((), ())), preferred_element_type=wide)


def fold(block):
    total = block[0:8]
    for start in range(8, block.shape[0], 8):
        total = total + block[start : start + 8]
    return total


GELU_C = math.sqrt(2.0 / math.pi)


def gelu(u):
    t = jnp.tanh(GELU_C * (u + 0.044715 * (u * u * u)))
    return 0.5 * u * (1.0 + t)


def gelu_both(u):
    square = u * u
    t = jnp.tanh(GELU_C * (u + 0.044715 * (square * u)))
    outer = 0.5 * (1.0 + t)
    slope = outer + 0.5 * u * (1.0 - t * t) * (GELU_C * (1.0 + (3.0 * 0.044715) * square))
    return u * outer, slope


def chain_kernel(names, sections, fused, *refs):
    r = SimpleNamespace(**dict(zip(names, refs)))
    micro, rows, width = r.x.shape
    ff = r.win.shape[1]
    qkv_width = 3 * width
    half_rows = SHORT
    chunks = [(start, start // half_rows) for start in range(0, rows, CHUNK)]
    halves = rows // half_rows
    section = lax.axis_index("section")
    member = lax.axis_index("dp")
    z_at = lax.div(member, CORES)
    core = lax.rem(member, CORES)
    own = z_at if fused else 0
    right = lax.rem(section + 1, sections)
    left = lax.rem(section + sections - 1, sections)
    is_first = section == 0
    is_last = section == sections - 1

    loads = []
    for index, (hbm, vmem) in enumerate(
        (
            (r.wqkv_h, r.wa.at[:, 0:qkv_width]),
            (r.wout_h, r.wa.at[:, qkv_width:]),
            (r.win_h, r.win),
            (r.wdown_h, r.wdown),
        )
    ):
        loads.append(pltpu.make_async_copy(hbm, vmem, r.wsem.at[index]))
        loads[index].start()

    barrier = pltpu.get_barrier_semaphore()
    greeted = [(left, member), (right, member)]
    if fused:
        greeted.append((section, z_at * CORES + 1 - core))
        for away in range(1, DEEP):
            greeted.append((section, lax.rem(z_at + away, DEEP) * CORES + core))
    for target in greeted:
        pl.semaphore_signal(barrier, inc=1, device_id=target, device_id_type=MESH)
    pl.semaphore_wait(barrier, len(greeted))

    def remote(src, dst, send_sem, recv_sem, target):
        return pltpu.make_async_remote_copy(
            src_ref=src,
            dst_ref=dst,
            send_sem=send_sem,
            recv_sem=recv_sem,
            device_id=target,
            device_id_type=MESH,
        )

    def forward_copy(job, slot):
        return remote(
            r.fout.at[job], r.frecv.at[mb_rows(slot), :], r.fss.at[job], r.frs.at[slot], (right, member)
        )

    def backward_copy(job):
        return remote(
            r.gin.at[job], r.brecv.at[job], r.bss.at[job], r.brs.at[job], (left, member)
        )

    def mod_row(mb, half, k):
        return r.mod[mb, half, pl.ds(k, 1), :]

    def mb_rows(mb):
        return pl.ds(pl.multiple_of(mb * rows, rows), rows)

    def mb_span(mb, start):
        return pl.ds(pl.multiple_of(mb * rows + start, CHUNK), CHUNK)

    lane = lax.broadcasted_iota(jnp.int32, (1, 128), 1)
    first_lanes = lane < 64
    masks = [first_lanes.astype(wide).astype(low), (1.0 - first_lanes.astype(wide)).astype(low)]
    scale = (width // HEADS) ** (-0.5)

    near = (1, 2, -1, -2)

    def spread_copy(buffer, send_sems, recv_sems, mb, k):
        target = jnp.clip(z_at + near[k], 0, DEEP - 1)
        return remote(
            buffer.at[mb, z_at],
            buffer.at[mb, z_at],
            send_sems.at[mb, k],
            recv_sems.at[mb, z_at],
            (section, target * CORES + core),
        )

    def spread(buffer, send_sems, recv_sems, mb, wait):
        for k in range(len(near)):

            @pl.when(jnp.logical_and(z_at + near[k] >= 0, z_at + near[k] < DEEP))
            def _():
                copy = spread_copy(buffer, send_sems, recv_sems, mb, k)
                copy.wait_send() if wait else copy.start()

    def relay(buffer, send_sems, recv_sems, mb, wait):
        for at, source, target in ((2, 0, 3), (1, 3, 0)):

            @pl.when(z_at == at)
            def _():
                copy = remote(
                    buffer.at[mb, source],
                    buffer.at[mb, source],
                    send_sems.at[mb, len(near)],
                    recv_sems.at[mb, source],
                    (section, target * CORES + core),
                )
                if wait:
                    copy.wait_send()
                else:
                    copy.wait_recv()
                    copy.start()

    def await_block(buffer, send_sems, recv_sems, mb, source):
        relayed = jnp.logical_or(
            jnp.logical_and(z_at == 2, source == 0), jnp.logical_and(z_at == 1, source == 3)
        )

        @pl.when(jnp.logical_and(z_at != source, jnp.logical_not(relayed)))
        def _():
            remote(
                buffer.at[mb, source],
                buffer.at[mb, source],
                send_sems.at[mb, 0],
                recv_sems.at[mb, source],
                (section, member),
            ).wait_recv()

    def norm_forward(src, mb, k_shift, k_scale, n_keep, r_keep, out):
        for start, half in chunks:
            span = pl.ds(start, CHUNK)
            v = src[span, :]
            centered = v - jnp.mean(v, axis=-1, keepdims=True)
            inverse = lax.rsqrt(jnp.mean(centered * centered, axis=-1, keepdims=True) + norm_eps)
            n = centered * inverse
            n_keep[mb_span(mb, start), :] = n.astype(low)
            r_keep[mb, span, :] = inverse
            out[span, :] = (
                n * (1.0 + mod_row(mb, half, k_scale)) + mod_row(mb, half, k_shift)
            ).astype(low)

    r.dmod[...] = jnp.zeros_like(r.dmod)

    def forward_job(job, carry):
        mb = lax.rem(job, micro)
        here = mb_rows(mb)
        z_base = 0 if fused else mb * (ff // width)

        @pl.when(jnp.logical_or(jnp.logical_not(is_first), job >= micro))
        def _():
            forward_copy(job, job).wait_recv()

        @pl.when(jnp.logical_and(is_first, job < micro))
        def _():
            r.h[...] = r.x[mb].astype(wide)

        @pl.when(jnp.logical_and(is_first, job >= micro))
        def _():
            r.h[...] = r.x[mb].astype(wide) + r.frecv[mb_rows(job), :].astype(wide)

        @pl.when(jnp.logical_not(is_first))
        def _():
            r.h[...] = r.frecv[mb_rows(job), :].astype(wide)

        norm_forward(r.h, mb, 0, 1, r.n1, r.r1, r.a1.at[mb])

        def wait_load(index):
            @pl.when(job == 0)
            def _():
                loads[index].wait()

        wait_load(0)
        a1 = r.a1[mb]
        for c in range(0, 3 * width, TILE):
            r.qkvo[here, c : c + TILE] = dot_nn(a1, r.wa[:, c : c + TILE]).astype(low)
        bias = r.bias[mb]
        for c in range(0, width, 128):
            q, k, v = [r.qkvo[here, i * width + c : i * width + c + 128] for i in range(3)]
            outs = []
            for mask in masks:
                s = dot_nt(q * (mask * scale), k) + bias
                e = jnp.exp(s - jnp.max(s, axis=1, keepdims=True))
                p = (e * (1.0 / jnp.sum(e, axis=1, keepdims=True))).astype(low)
                outs.append(dot_nn(p, v))
            r.qkvo[here, qkv_width + c : qkv_width + c + 128] = jnp.where(
                first_lanes, outs[0], outs[1]
            ).astype(low)
        wait_load(1)
        o = r.qkvo[here, qkv_width:]
        for c in range(0, width, TILE):
            r.t[:, c : c + TILE] = dot_nn(o, r.wa[:, qkv_width + c : qkv_width + c + TILE])
        for start, half in chunks:
            span = pl.ds(start, CHUNK)
            attn = r.t[span, :]
            r.dattn[mb, span, :] = attn.astype(low)
            r.m[span, :] = r.h[span, :] + mod_row(mb, half, 2) * attn
        norm_forward(r.m, mb, 3, 4, r.n2, r.r2, r.a2.at[mb, own])
        if fused:

            @pl.when(job >= micro)
            def _():
                spread(r.a2, r.a2ss, r.a2rs, mb, False)

        wait_load(2)
        a2 = r.a2[mb, own]
        for c in range(0, ff, TILE):
            u = dot_nn(a2, r.win[:, c : c + TILE])
            r.du[mb_rows(mb), c : c + TILE] = u.astype(low)
            at = c % width
            r.z[z_base + c // width, :, at : at + TILE] = gelu(u).astype(low)
        wait_load(3)
        z = [r.z[z_base + i] for i in range(ff // width)]
        for c in range(0, width, TILE):
            y = dot_nn(z[0], r.wdown[0:width, c : c + TILE])
            for i in range(1, ff // width):
                y = y + dot_nn(z[i], r.wdown[i * width : (i + 1) * width, c : c + TILE])
            r.t[:, c : c + TILE] = y
        for start, half in chunks:
            span = pl.ds(start, CHUNK)
            y = r.t[span, :]
            r.y[mb, span, :] = y.astype(low)
            r.fout[job, span, :] = (r.m[span, :] + mod_row(mb, half, 5) * y).astype(low)

        @pl.when(jnp.logical_or(jnp.logical_not(is_last), job < micro))
        def _():
            forward_copy(job, jnp.where(is_last, job + micro, job)).start()

        return carry

    lax.fori_loop(0, 2 * micro, forward_job, 0)
    if fused:
        pl.semaphore_signal(
            r.done,
            inc=1,
            device_id=(section, z_at * CORES + 1 - core),
            device_id_type=MESH,
        )

    def norm_backward(mb, k_scale, n_keep, r_keep, base, per_chunk):
        for half in range(halves):
            shift_sum = jnp.zeros((8, width), wide)
            scale_sum = jnp.zeros((8, width), wide)
            gate_sum = jnp.zeros((8, width), wide)
            for start in range(half * half_rows, (half + 1) * half_rows, CHUNK):
                span = pl.ds(start, CHUNK)
                da = r.t[span, :]
                n = n_keep[mb_span(mb, start), :].astype(wide)
                inverse = r_keep[mb, span, :]
                shift_sum = shift_sum + fold(da)
                scale_sum = scale_sum + fold(da * n)
                dn = da * (1.0 + mod_row(mb, half, k_scale))
                dv = inverse * (
                    dn
                    - jnp.mean(dn, axis=-1, keepdims=True)
                    - n * jnp.mean(dn * n, axis=-1, keepdims=True)
                )
                extra = per_chunk(span, half, base[span, :] + dv)
                if extra is not None:
                    gate_sum = gate_sum + fold(extra)
            r.dmod[mb, half, k_scale - 1, :] = jnp.sum(shift_sum, axis=0)
            r.dmod[mb, half, k_scale, :] = jnp.sum(scale_sum, axis=0)
            if k_scale == 4:
                r.dmod[mb, half, 2, :] = jnp.sum(gate_sum, axis=0)

    def backward_job(mb, carry):
        g_s = r.h
        here = mb_rows(mb)

        @pl.when(is_last)
        def _():
            g_s[...] = r.cot[mb].astype(wide)

        @pl.when(jnp.logical_not(is_last))
        def _():
            backward_copy(mb).wait_recv()
            g_s[...] = r.brecv[mb].astype(wide)

        for half in range(halves):
            gate_sum = jnp.zeros((8, width), wide)
            for start in range(half * half_rows, (half + 1) * half_rows, CHUNK):
                span = pl.ds(start, CHUNK)
                g = g_s[span, :]
                gate_sum = gate_sum + fold(g * r.y[mb, span, :].astype(wide))
                r.dy[mb, own, span, :] = (mod_row(mb, half, 5) * g).astype(low)
            r.dmod[mb, half, 5, :] = jnp.sum(gate_sum, axis=0)
        if fused:
            spread(r.dy, r.dyss, r.dyrs, mb, False)
        dy = r.dy[mb, own]
        for c in range(0, ff, TILE):
            dz = dot_nt(dy, r.wdown[c : c + TILE, :])
            u = r.du[mb_rows(mb), c : c + TILE].astype(wide)
            r.du[mb_rows(mb), c : c + TILE] = (gelu_both(u)[1] * dz).astype(low)
        du = r.du[mb_rows(mb), :]
        for c in range(0, width, TILE):
            r.t[:, c : c + TILE] = dot_nt(du, r.win[c : c + TILE, :])

        def after_mlp(span, half, dm):
            r.m[span, :] = dm
            extra = dm * r.dattn[mb, span, :].astype(wide)
            r.dattn[mb, span, :] = (mod_row(mb, half, 2) * dm).astype(low)
            return extra

        norm_backward(mb, 4, r.n2, r.r2, g_s, after_mlp)
        dattn = r.dattn[mb]
        for c in range(0, width, TILE):
            r.do[:, c : c + TILE] = dot_nt(dattn, r.wa[c : c + TILE, qkv_width:]).astype(low)
        bias = r.bias[mb]
        for c in range(0, width, 128):
            cols = [slice(i * width + c, i * width + c + 128) for i in range(3)]
            q, k, v = [r.qkvo[here, cut] for cut in cols]
            do = r.do[:, c : c + 128]
            parts = []
            for mask in masks:
                s = dot_nt(k, q * (mask * scale)) + bias
                e = jnp.exp(s - jnp.max(s, axis=0, keepdims=True))
                p = e * (1.0 / jnp.sum(e, axis=0, keepdims=True))
                dp = dot_nt(v * mask, do)
                inner = jnp.sum(p * dp, axis=0, keepdims=True)
                ds = (p * (dp - inner) * scale).astype(low)
                parts.append((dot_tn(ds, k), dot_nn(ds, q), dot_nn(p.astype(low), do)))
            for i in range(3):
                r.qkvo[here, cols[i]] = jnp.where(first_lanes, parts[0][i], parts[1][i]).astype(
                    low
                )
        dqkv = r.qkvo[here, 0:qkv_width]
        for c in range(0, width, TILE):
            r.t[:, c : c + TILE] = dot_nt(dqkv, r.wa[c : c + TILE, 0:qkv_width])

        def after_attention(span, half, dh):
            r.gin[mb, span, :] = dh.astype(low)

        norm_backward(mb, 1, r.n1, r.r1, r.m, after_attention)

        @pl.when(jnp.logical_not(is_first))
        def _():
            backward_copy(mb).start()

        return carry

    lax.fori_loop(0, micro, backward_job, 0)

    if fused:
        gradient_tail(r, section, z_at, core, member, remote, spread, relay, await_block)

    for job in range(2 * micro):

        @pl.when(jnp.logical_or(jnp.logical_not(is_last), job < micro))
        def _():
            forward_copy(job, job).wait_send()

    for job in range(micro):

        @pl.when(jnp.logical_not(is_first))
        def _():
            backward_copy(job).wait_send()


def gradient_tail(r, section, z_at, core, member, remote, spread, relay, await_block):
    micro, rows, width = r.x.shape
    ff = r.win.shape[1]
    share = width // (DEEP * CORES)
    part = ff // DEEP
    half_part = part // CORES
    other = 1 - core
    partner = (section, z_at * CORES + other)
    qkv_width = 3 * width

    def on_z(z):
        return (section, z * CORES + core)

    for step in (1, -1):

        @pl.when(jnp.logical_and(z_at + step >= 0, z_at + step < DEEP))
        def _():
            pl.semaphore_signal(
                r.free,
                inc=1,
                device_id=on_z(jnp.clip(z_at + step, 0, DEEP - 1)),
                device_id_type=MESH,
            )

    mine = r.ada.at[core, z_at]
    for mb in range(micro):
        sums = r.dmod[mb]
        mine[mb, :, 0:width] = sums.reshape(sums.shape[0] * sums.shape[1], width).astype(low)
        mine[mb, :, width:] = r.feat[mb]

    def ada_copy(away):
        target = lax.rem(z_at + away, DEEP)
        return remote(
            mine, mine, r.adass.at[away - 1], r.adars.at[z_at], (section, target * CORES + core)
        )

    for away in range(1, DEEP):
        ada_copy(away).start()

    def flat(ref):
        block = ref[...]
        return block.reshape(micro * rows, block.shape[-1])

    a1_t = flat(r.a1).T
    for c in range(0, qkv_width, TILE):
        r.wa[:, c : c + TILE] = dot_nn(a1_t, r.qkvo[:, c : c + TILE]).astype(low)
    o_t = r.qkvo[:, qkv_width:].T
    dattn = flat(r.dattn)
    for c in range(0, width, TILE):
        r.wa[:, qkv_width + c : qkv_width + c + TILE] = dot_nn(
            o_t, dattn[:, c : c + TILE]
        ).astype(low)

    def share_rows(z, of_core):
        return pl.ds(pl.multiple_of((z * CORES + of_core) * share, share), share)

    def pair_copy(z):
        return remote(
            r.wa.at[share_rows(z, other), :], r.pa.at[z], r.pss.at[z], r.prs.at[z], partner
        )

    for z in range(DEEP):
        pair_copy(z).start()

    for mb in range(micro):
        relay(r.a2, r.a2ss, r.a2rs, mb, False)
    relay(r.dy, r.dyss, r.dyrs, 0, False)

    group = 2

    def mlp_group(mb, first):
        for step in range(group):
            await_block(r.a2, r.a2ss, r.a2rs, mb, first + step)
            await_block(r.dy, r.dyss, r.dyrs, mb, first + step)
        tokens = group * rows
        a2 = r.a2[mb, pl.ds(first, group)].reshape(tokens, width)
        dy = r.dy[mb, pl.ds(first, group)].reshape(tokens, width)
        for c in range(0, part, TILE):
            at = pl.ds(pl.multiple_of(z_at * part + c, TILE), TILE)
            u = dot_nn(a2, r.win[:, at])
            dz = dot_nt(dy, r.wdown[at, :])
            active, slope = gelu_both(u)
            r.z[0:group, :, c : c + TILE] = active.astype(low).reshape(group, rows, TILE)
            r.z[group:, :, c : c + TILE] = (slope * dz).astype(low).reshape(group, rows, TILE)
        z_t = r.z[0:group].reshape(tokens, part).T
        a2_t = a2.T
        for c in range(0, width, TILE):
            r.pdown[:, c : c + TILE] += dot_nn(z_t, dy[:, c : c + TILE])
        for c in range(0, part, TILE):
            r.pin[:, c : c + TILE] += dot_nn(a2_t, r.z[group:, :, c : c + TILE].reshape(tokens, TILE))

    def sums(z):
        return r.qkvo.at[z * share : (z + 1) * share, :]

    def sum_pair():
        for z in range(DEEP):
            pair_copy(z).wait_recv()
            sums(z)[...] = (
                r.wa[share_rows(z, core), :].astype(wide) + r.pa[z].astype(wide)
            ).astype(low)

    def slot_of(z, direction):
        if direction > 0:
            return z - 1
        return DEEP - 1 + z if z < DEEP - 2 else 0

    def slot_ref(z, direction):
        return r.du.at[pl.ds(slot_of(z, direction) * share, share), :]

    def line_copy(z, direction):
        slot = slot_of(z, direction)
        return remote(
            sums(z),
            slot_ref(z, direction),
            r.lss.at[z],
            r.lrs.at[slot],
            on_z(jnp.clip(z_at + direction, 0, DEEP - 1)),
        )

    def passes(z, direction):
        return z_at < z if direction > 0 else z_at > z

    def takes(direction):
        return z_at > 0 if direction > 0 else z_at < DEEP - 1

    def add_slot(z, direction):
        line_copy(z, direction).wait_recv()
        sums(z)[...] = (
            sums(z)[...].astype(wide) + slot_ref(z, direction)[...].astype(wide)
        ).astype(low)

    def line_start(z, direction):
        @pl.when(jnp.logical_and(passes(z, direction), jnp.logical_not(takes(direction))))
        def _():
            line_copy(z, direction).start()

    def line_pass(z, direction, at):
        @pl.when(z_at == at)
        def _():
            add_slot(z, direction)
            line_copy(z, direction).start()

    def group_step(g, carry):
        @pl.when(g == 0)
        def _():
            r.pdown[...] = jnp.zeros_like(r.pdown)
            r.pin[...] = jnp.zeros_like(r.pin)

        @pl.when(g == 2)
        def _():
            sum_pair()
            for at in range(DEEP):

                @pl.when(z_at == at)
                def _():
                    pl.semaphore_wait(r.free, (at > 0) + (at < DEEP - 1))

            for z in (3, 2, 1):
                line_start(z, 1)
                line_start(DEEP - 1 - z, -1)
            relay(r.dy, r.dyss, r.dyrs, 1, False)

        mlp_group(lax.div(g, 2), lax.rem(g, 2) * group)

        @pl.when(g == 2)
        def _():
            line_pass(3, 1, 1)
            line_pass(0, -1, 2)

        @pl.when(g == 3)
        def _():
            line_pass(2, 1, 1)
            line_pass(1, -1, 2)

        return carry

    lax.fori_loop(0, micro * DEEP // group, group_step, 0)

    def down_copy():
        return remote(
            r.n1.at[pl.ds(0, half_part), :],
            r.frecv.at[pl.ds(width // CORES, half_part), :],
            r.mss.at[DEEP],
            r.mrs.at[DEEP],
            partner,
        )

    def up_copy(z):
        return remote(
            r.cols.at[z],
            r.frecv.at[pl.ds(z * share, share), :],
            r.mss.at[z],
            r.mrs.at[z],
            partner,
        )

    pl.semaphore_wait(r.done, 1)
    for z in range(DEEP):
        r.cols[z] = r.pin[share_rows(z, other), :].astype(low)
        up_copy(z).start()
    r.n1[0:half_part, :] = r.pdown[
        pl.ds(pl.multiple_of(other * half_part, half_part), half_part), :
    ].astype(low)
    down_copy().start()

    def column_copy(z):
        return remote(
            r.cols2.at[z], r.land.at[z_at], r.css.at[z], r.crs.at[z_at], on_z(z)
        )

    def part_columns(z):
        return pl.ds(pl.multiple_of(z * part, part), part)

    for z in range(DEEP):
        up_copy(z).wait_recv()
        total = r.pin[share_rows(z, core), :] + r.frecv[z * share : (z + 1) * share, :].astype(wide)

        @pl.when(z_at == z)
        def _():
            r.g_up[:, part_columns(z)] = total

        @pl.when(z_at != z)
        def _():
            r.cols2[z] = total.astype(low)
            column_copy(z).start()

    line_pass(3, 1, 2)
    line_pass(0, -1, 1)

    def ada_pair():
        return remote(
            r.ada.at[core], r.ada.at[core], r.adass.at[DEEP - 1], r.adars.at[DEEP], partner
        )

    def ada_other():
        return remote(
            r.ada.at[other], r.ada.at[other], r.adass.at[DEEP - 1], r.adars.at[DEEP], partner
        )

    for z in range(DEEP):

        @pl.when(z_at != z)
        def _():
            remote(
                r.ada.at[core, z], r.ada.at[core, z], r.adass.at[0], r.adars.at[z], partner
            ).wait_recv()

    ada_pair().start()

    down_copy().wait_recv()
    own_half = pl.ds(pl.multiple_of(core * half_part, half_part), half_part)
    r.g_down[...] = r.pdown[own_half, :] + r.frecv[
        width // CORES : width // CORES + half_part, :
    ].astype(wide)

    ada_other().wait_recv()
    entries = CORES * DEEP * micro * r.feat.shape[1]
    ada_rows = TEMB // (DEEP * CORES)
    pick = lax.broadcasted_iota(jnp.int32, (ada_rows, TEMB), 1) == (
        lax.broadcasted_iota(jnp.int32, (ada_rows, TEMB), 0) + member * ada_rows
    )
    features = r.ada[:, :, :, :, width:].reshape(entries, TEMB)
    gathered = r.ada[:, :, :, :, 0:width].reshape(entries, width)
    spreads = dot_nt(pick.astype(wide).astype(low), features)
    which = lax.rem(lax.broadcasted_iota(jnp.int32, (ada_rows, entries), 1), 8)
    for k in range(6):
        chosen = jnp.where(which == k, spreads, 0.0).astype(low)
        r.g_ada[:, k * width : (k + 1) * width] = dot_nn(chosen, gathered)

    def finish(z):
        for direction in (1, -1):

            @pl.when(takes(direction))
            def _():
                if (direction > 0 and z > 0) or (direction < 0 and z < DEEP - 1):
                    line_copy(z, direction).wait_recv()
        total = sums(z)[...].astype(wide)
        if z > 0:
            total = total + slot_ref(z, 1)[...].astype(wide)
        if z < DEEP - 1:
            total = total + slot_ref(z, -1)[...].astype(wide)
        r.g_qkv[...] = total[:, 0:qkv_width]
        r.g_out[...] = total[:, qkv_width:]

    for z in range(DEEP):

        @pl.when(z_at == z)
        def _():
            finish(z)

    for z in range(DEEP):

        @pl.when(z_at != z)
        def _():
            remote(
                r.cols2.at[z], r.land.at[z], r.css.at[z], r.crs.at[z], on_z(z)
            ).wait_recv()
            r.g_up[:, z * part : (z + 1) * part] = r.land[z].astype(wide)

    for mb in range(micro):
        spread(r.a2, r.a2ss, r.a2rs, mb, True)
        spread(r.dy, r.dyss, r.dyrs, mb, True)
        relay(r.a2, r.a2ss, r.a2rs, mb, True)
        relay(r.dy, r.dyss, r.dyrs, mb, True)
    for away in range(1, DEEP):
        ada_copy(away).wait_send()
    ada_pair().wait_send()
    for z in range(DEEP):
        pair_copy(z).wait_send()
        up_copy(z).wait_send()

        @pl.when(z_at != z)
        def _():
            column_copy(z).wait_send()
            line_copy(z, 1 if z > 0 else -1).wait_send()

    down_copy().wait_send()


def run_chain(x, cot, mod, bias, feat, w_qkv, w_out, w_in, w_down, members):
    micro, rows, width = x.shape
    ff = w_in.shape[1]
    sections = lax.axis_size("section")
    fused = members == DEEP * CORES
    vmem = pl.BlockSpec(memory_space=pltpu.VMEM)
    hbm = pl.BlockSpec(memory_space=pl.ANY)
    dma = pltpu.SemaphoreType.DMA

    def kept(*shape):
        return jax.ShapeDtypeStruct(shape, low)

    def result(*shape):
        return jax.ShapeDtypeStruct(shape, wide)

    names = ["x", "cot", "mod", "bias", "feat", "wqkv_h", "wout_h", "win_h", "wdown_h"]
    in_specs = [vmem] * 5 + [hbm] * 4
    stored = {
        "dmod": result(*mod.shape),
        "a1": kept(micro, rows, width),
        "qkvo": kept(micro * rows, 4 * width),
        "dattn": kept(micro, rows, width),
        "a2": kept(micro, DEEP if fused else 1, rows, width),
        "du": kept(micro * rows, ff),
        "z": kept((1 if fused else micro) * (ff // width), rows, width),
        "dy": kept(micro, DEEP if fused else 1, rows, width),
    }
    outs = {"fout": kept(2 * micro, rows, width), "gin": kept(micro, rows, width)}
    share = width // members
    if fused:
        outs["g_qkv"] = result(share, 3 * width)
        outs["g_out"] = result(share, width)
        outs["g_up"] = result(share, ff)
        outs["g_down"] = result(ff // members, width)
        outs["g_ada"] = result(TEMB // members, 6 * width)
    else:
        outs.update(stored)
    scratch = {
        "wa": pltpu.VMEM((width, 4 * width), low),
        "win": pltpu.VMEM((width, ff), low),
        "wdown": pltpu.VMEM((ff, width), low),
        "h": pltpu.VMEM((rows, width), wide),
        "m": pltpu.VMEM((rows, width), wide),
        "t": pltpu.VMEM((rows, width), wide),
        "do": pltpu.VMEM((rows, width), low),
        "n1": pltpu.VMEM((micro * rows, width), low),
        "n2": pltpu.VMEM((micro * rows, width), low),
        "r1": pltpu.VMEM((micro, rows, 1), wide),
        "r2": pltpu.VMEM((micro, rows, 1), wide),
        "y": pltpu.VMEM((micro, rows, width), low),
        "frecv": pltpu.VMEM((2 * micro * rows, width), low),
        "brecv": pltpu.VMEM((micro, rows, width), low),
        "wsem": dma((4,)),
        "fss": dma((2 * micro,)),
        "frs": dma((2 * micro,)),
        "bss": dma((micro,)),
        "brs": dma((micro,)),
    }
    if fused:
        part = ff // DEEP
        for name, value in stored.items():
            scratch[name] = pltpu.VMEM(value.shape, value.dtype)
        scratch.update(
            {
                "pa": pltpu.VMEM((DEEP, share, 4 * width), low),
                "pdown": pltpu.VMEM((part, width), wide),
                "pin": pltpu.VMEM((width, part), wide),
                "cols": pltpu.VMEM((DEEP, share, part), low),
                "cols2": pltpu.VMEM((DEEP, share, part), low),
                "land": pltpu.VMEM((DEEP, share, part), low),
                "ada": pltpu.VMEM((CORES, DEEP, micro, feat.shape[1], width + TEMB), low),
                "free": pltpu.SemaphoreType.REGULAR,
                "done": pltpu.SemaphoreType.REGULAR,
                "a2ss": dma((micro, 5)),
                "a2rs": dma((micro, DEEP)),
                "dyss": dma((micro, 5)),
                "dyrs": dma((micro, DEEP)),
                "adass": dma((DEEP,)),
                "adars": dma((DEEP + 1,)),
                "pss": dma((DEEP,)),
                "prs": dma((DEEP,)),
                "lss": dma((DEEP,)),
                "lrs": dma((5,)),
                "mss": dma((DEEP + 1,)),
                "mrs": dma((DEEP + 1,)),
                "css": dma((DEEP,)),
                "crs": dma((DEEP,)),
            }
        )
    names = names + list(outs) + list(scratch)
    values = pl.pallas_call(
        functools.partial(chain_kernel, names, sections, fused),
        out_shape=tuple(outs.values()),
        in_specs=in_specs,
        out_specs=(vmem,) * len(outs),
        scratch_shapes=list(scratch.values()),
        compiler_params=pltpu.CompilerParams(
            collective_id=0, has_side_effects=True, vmem_limit_bytes=60 * 1024 * 1024
        ),
    )(x, cot, mod, bias, feat, w_qkv, w_out, w_in, w_down)
    return SimpleNamespace(**dict(zip(outs, values)))


def time_features(timestep_ids):
    half_width = TEMB // 2
    frequency = jnp.exp(-math.log(10000.0) * jnp.arange(half_width, dtype=wide) / half_width)
    angles = timestep_ids.astype(wide)[:, None] * 0.1 * frequency[None, :]
    return jnp.concatenate([jnp.sin(angles), jnp.cos(angles)], axis=1)


def summed_apart(kept, features, micro, rows, width):
    def product(left, right):
        left = left.reshape(micro * rows, -1)
        right = right.reshape(micro * rows, -1)
        partial = dot_tn(left, right).astype(low)
        return lax.psum_scatter(partial, "dp", scatter_dimension=0, tiled=True).astype(wide)

    sums = kept.dmod[:, :, :6].reshape(features.shape[0], 6 * width)
    features_all = lax.all_gather(features.astype(wide), "dp", tiled=True)
    sums_all = lax.all_gather(sums, "dp", tiled=True)
    share = TEMB // lax.axis_size("dp")
    mine = lax.dynamic_slice_in_dim(features_all, lax.axis_index("dp") * share, share, 1)
    grad_ada = lax.dot_general(
        mine, sums_all, (((0,), (0,)), ((), ())), precision=lax.Precision.HIGHEST
    )
    return (
        product(kept.a1, kept.qkvo[:, : 3 * width]),
        product(kept.qkvo[:, 3 * width :], kept.dattn),
        product(kept.a2, kept.du),
        product(jnp.swapaxes(kept.z.reshape(micro, -1, rows, width), 1, 2), kept.dy),
        grad_ada,
    )


def on_device(inputs, cotangent, long_count, timesteps, w_qkv, w_out, w_in, w_down, ada_weight):
    micro = long_count.shape[1]
    width = inputs.shape[1]
    rows = inputs.shape[0] // micro
    halves = rows // SHORT
    members = lax.axis_size("dp")
    is_long = (long_count[0] == 1)[:, None]
    half_index = jnp.arange(halves, dtype=jnp.int32)[None, :]
    half_steps = jnp.where(is_long, timesteps[0][:, :1], timesteps[0][:, :halves])
    features = time_features(half_steps.reshape(-1)).astype(low)
    mod = jnp.dot(features, ada_weight[0], preferred_element_type=wide)
    mod = mod.reshape(micro, halves, 6, width)
    mod = jnp.pad(mod, ((0, 0), (0, 0), (0, 2), (0, 0)))
    feat = jnp.repeat(features.reshape(micro, halves, TEMB), 8, axis=1)
    slot_ids = jnp.where(is_long, 0, jnp.repeat(half_index, SHORT, axis=1))
    same = slot_ids[:, :, None] == slot_ids[:, None, :]
    bias = jnp.where(same, 0.0, -1e30).astype(wide)
    kept = run_chain(
        inputs.reshape(micro, rows, width),
        cotangent.reshape(micro, rows, width),
        mod,
        bias,
        feat,
        w_qkv[0],
        w_out[0],
        w_in[0],
        w_down[0],
        members,
    )
    if members == DEEP * CORES:
        grads = (kept.g_qkv, kept.g_out, kept.g_up, kept.g_down, kept.g_ada)
    else:
        grads = summed_apart(kept, features, micro, rows, width)
    hidden_out = kept.fout[micro:].reshape(1, micro * rows, width)
    grad_in = kept.gin.reshape(1, micro * rows, width)
    return (hidden_out, grad_in) + tuple(grad[None] for grad in grads)


def solution(mesh):
    placed = (
        P("dp", None),
        P("dp", None),
        P("dp", None),
        P("dp", None, None),
        P("section", None, None),
        P("section", None, None),
        P("section", None, None),
        P("section", None, None),
        P("section", None, None),
    )
    return jax.shard_map(
        on_device,
        mesh=mesh,
        in_specs=placed,
        out_specs=(P("section", "dp", None),) * 7,
        check_vma=False,
    )
```

```python
import functools
import math
from types import SimpleNamespace

import jax
import jax.numpy as jnp
from jax import lax
from jax.experimental import pallas as pl
from jax.experimental.pallas import tpu as pltpu
from jax.sharding import PartitionSpec as P

HEADS = 12
TEMB = 128
SHORT = 128
TILE = 256
CHUNK = 32
CORES = 2
DEEP = 4
norm_eps = 1e-06
MESH = pl.DeviceIdType.MESH
low = jnp.bfloat16
wide = jnp.float32


def dot_nn(a, b):
    return lax.dot_general(a, b, (((1,), (0,)), ((), ())), preferred_element_type=wide)


def dot_nt(a, b):
    return lax.dot_general(a, b, (((1,), (1,)), ((), ())), preferred_element_type=wide)


def dot_tn(a, b):
    return lax.dot_general(a, b, (((0,), (0,)), ((), ())), preferred_element_type=wide)


def fold(block):
    total = block[0:8]
    for start in range(8, block.shape[0], 8):
        total = total + block[start : start + 8]
    return total


GELU_C = math.sqrt(2.0 / math.pi)


def gelu(u):
    t = jnp.tanh(GELU_C * (u + 0.044715 * (u * u * u)))
    return 0.5 * u * (1.0 + t)


def gelu_both(u):
    square = u * u
    t = jnp.tanh(GELU_C * (u + 0.044715 * (square * u)))
    outer = 0.5 * (1.0 + t)
    slope = outer + 0.5 * u * (1.0 - t * t) * (GELU_C * (1.0 + (3.0 * 0.044715) * square))
    return u * outer, slope


def chain_kernel(names, sections, fused, *refs):
    r = SimpleNamespace(**dict(zip(names, refs)))
    micro, rows, width = r.x.shape
    ff = r.win.shape[1]
    qkv_width = 3 * width
    half_rows = SHORT

    def half_chunks(half):
        return range(half * half_rows, (half + 1) * half_rows, CHUNK)

    halves = rows // half_rows
    section = lax.axis_index("section")
    member = lax.axis_index("dp")
    z_at = lax.div(member, CORES)
    core = lax.rem(member, CORES)
    own = z_at if fused else 0
    right = lax.rem(section + 1, sections)
    left = lax.rem(section + sections - 1, sections)
    is_first = section == 0
    is_last = section == sections - 1

    loads = []
    for index, (hbm, vmem) in enumerate(
        (
            (r.wqkv_h, r.wa.at[:, 0:qkv_width]),
            (r.wout_h, r.wa.at[:, qkv_width:]),
            (r.win_h, r.win),
            (r.wdown_h, r.wdown),
        )
    ):
        loads.append(pltpu.make_async_copy(hbm, vmem, r.wsem.at[index]))
        loads[index].start()

    barrier = pltpu.get_barrier_semaphore()
    greeted = [(left, member), (right, member)]
    if fused:
        greeted.append((section, z_at * CORES + 1 - core))
        for away in range(1, DEEP):
            greeted.append((section, lax.rem(z_at + away, DEEP) * CORES + core))
    for target in greeted:
        pl.semaphore_signal(barrier, inc=1, device_id=target, device_id_type=MESH)
    pl.semaphore_wait(barrier, len(greeted))

    def remote(src, dst, send_sem, recv_sem, target):
        return pltpu.make_async_remote_copy(
            src_ref=src,
            dst_ref=dst,
            send_sem=send_sem,
            recv_sem=recv_sem,
            device_id=target,
            device_id_type=MESH,
        )

    def forward_copy(job, slot, half):
        span = pl.ds(half * half_rows, half_rows)
        landing = pl.ds(
            pl.multiple_of(slot * rows + half * half_rows, half_rows), half_rows
        )
        return remote(
            r.fout.at[job, span, :],
            r.frecv.at[landing, :],
            r.fss.at[job, half],
            r.frs.at[slot, half],
            (right, member),
        )

    def backward_copy(job, half):
        span = pl.ds(half * half_rows, half_rows)
        return remote(
            r.gin.at[job, span, :],
            r.brecv.at[job, span, :],
            r.bss.at[job, half],
            r.brs.at[job, half],
            (left, member),
        )

    def mod_row(mb, half, k):
        return r.mod[mb, half, pl.ds(k, 1), :]

    def mb_rows(mb):
        return pl.ds(pl.multiple_of(mb * rows, rows), rows)

    def mb_span(mb, start):
        return pl.ds(pl.multiple_of(mb * rows + start, CHUNK), CHUNK)

    lane = lax.broadcasted_iota(jnp.int32, (1, 128), 1)
    first_lanes = lane < 64
    masks = [first_lanes.astype(wide).astype(low), (1.0 - first_lanes.astype(wide)).astype(low)]
    scale = (width // HEADS) ** (-0.5)
    ones = jnp.ones((rows, 128), low)

    near = (1, 2, -1, -2)

    def spread_copy(buffer, send_sems, recv_sems, mb, k):
        target = jnp.clip(z_at + near[k], 0, DEEP - 1)
        return remote(
            buffer.at[mb, z_at],
            buffer.at[mb, z_at],
            send_sems.at[mb, k],
            recv_sems.at[mb, z_at],
            (section, target * CORES + core),
        )

    def spread(buffer, send_sems, recv_sems, mb, wait):
        for k in range(len(near)):

            @pl.when(jnp.logical_and(z_at + near[k] >= 0, z_at + near[k] < DEEP))
            def _():
                copy = spread_copy(buffer, send_sems, recv_sems, mb, k)
                copy.wait_send() if wait else copy.start()

    def relay(buffer, send_sems, recv_sems, mb, wait):
        for at, source, target in ((2, 0, 3), (1, 3, 0)):

            @pl.when(z_at == at)
            def _():
                copy = remote(
                    buffer.at[mb, source],
                    buffer.at[mb, source],
                    send_sems.at[mb, len(near)],
                    recv_sems.at[mb, source],
                    (section, target * CORES + core),
                )
                if wait:
                    copy.wait_send()
                else:
                    copy.wait_recv()
                    copy.start()

    def await_block(buffer, send_sems, recv_sems, mb, source):
        relayed = jnp.logical_or(
            jnp.logical_and(z_at == 2, source == 0), jnp.logical_and(z_at == 1, source == 3)
        )

        @pl.when(jnp.logical_and(z_at != source, jnp.logical_not(relayed)))
        def _():
            remote(
                buffer.at[mb, source],
                buffer.at[mb, source],
                send_sems.at[mb, 0],
                recv_sems.at[mb, source],
                (section, member),
            ).wait_recv()

    def norm_forward(src, mb, half, k_shift, k_scale, n_keep, r_keep, out):
        for start in half_chunks(half):
            span = pl.ds(start, CHUNK)
            v = src[span, :]
            centered = v - jnp.mean(v, axis=-1, keepdims=True)
            inverse = lax.rsqrt(jnp.mean(centered * centered, axis=-1, keepdims=True) + norm_eps)
            n = centered * inverse
            n_keep[mb_span(mb, start), :] = n.astype(low)
            r_keep[mb, span, :] = inverse
            out[span, :] = (
                n * (1.0 + mod_row(mb, half, k_scale)) + mod_row(mb, half, k_shift)
            ).astype(low)

    r.dmod[...] = jnp.zeros_like(r.dmod)

    def forward_job(job, carry):
        mb = lax.rem(job, micro)
        here = mb_rows(mb)
        z_base = 0 if fused else mb * (ff // width)

        def wait_load(index):
            @pl.when(job == 0)
            def _():
                loads[index].wait()

        for half in range(halves):
            span = pl.ds(half * half_rows, half_rows)
            arrived = pl.ds(
                pl.multiple_of(job * rows + half * half_rows, half_rows), half_rows
            )

            @pl.when(jnp.logical_or(jnp.logical_not(is_first), job >= micro))
            def _():
                forward_copy(job, job, half).wait_recv()

            @pl.when(jnp.logical_and(is_first, job < micro))
            def _():
                r.h[span, :] = r.x[mb, span, :].astype(wide)

            @pl.when(jnp.logical_and(is_first, job >= micro))
            def _():
                r.h[span, :] = r.x[mb, span, :].astype(wide) + r.frecv[arrived, :].astype(wide)

            @pl.when(jnp.logical_not(is_first))
            def _():
                r.h[span, :] = r.frecv[arrived, :].astype(wide)

            norm_forward(r.h, mb, half, 0, 1, r.n1, r.r1, r.a1.at[mb])
            if half == 0:
                wait_load(0)
            a1 = r.a1[mb, span, :]
            to = pl.ds(pl.multiple_of(mb * rows + half * half_rows, half_rows), half_rows)
            for c in range(0, qkv_width, TILE):
                r.qkvo[to, c : c + TILE] = dot_nn(a1, r.wa[:, c : c + TILE]).astype(low)

        q_tag = r.tags[0, mb]
        k_tag = r.tags[1, mb]

        def scores(c):
            q, k, v = [r.qkvo[here, i * width + c : i * width + c + 128] for i in range(3)]
            k_wide = jnp.concatenate([k, k_tag], axis=1)
            found = [
                dot_nt(jnp.concatenate([q * (mask * scale), q_tag], axis=1), k_wide)
                for mask in masks
            ]
            return found, jnp.concatenate([v, ones], axis=1)

        def mix(c, found, v_wide):
            weights = [jnp.exp(s - jnp.max(s, axis=1, keepdims=True)).astype(low) for s in found]
            mixed = [dot_nn(e, v_wide) for e in weights]
            top = jnp.where(first_lanes, mixed[0][:, 0:128], mixed[1][:, 0:128])
            total = jnp.where(first_lanes, mixed[0][:, 128:], mixed[1][:, 128:])
            r.do[:, c : c + 128] = (top * (1.0 / total)).astype(low)

        ahead = scores(0)
        for c in range(0, width, 128):
            current = ahead
            if c + 128 < width:
                ahead = scores(c + 128)
            mix(c, *current)
        wait_load(1)
        wait_load(2)
        wait_load(3)
        r.qkvo[here, qkv_width:] = r.do[...]
        for half in range(halves):
            span = pl.ds(half * half_rows, half_rows)
            to = pl.ds(pl.multiple_of(mb * rows + half * half_rows, half_rows), half_rows)
            o = r.do[span, :]
            for c in range(0, width, TILE):
                r.t[span, c : c + TILE] = dot_nn(o, r.wa[:, qkv_width + c : qkv_width + c + TILE])
            for start in half_chunks(half):
                part = pl.ds(start, CHUNK)
                attn = r.t[part, :]
                r.dattn[mb, part, :] = attn.astype(low)
                r.m[part, :] = r.h[part, :] + mod_row(mb, half, 2) * attn
            norm_forward(r.m, mb, half, 3, 4, r.n2, r.r2, r.a2.at[mb, own])
            a2 = r.a2[mb, own, span, :]
            for c in range(0, ff, TILE):
                u = dot_nn(a2, r.win[:, c : c + TILE])
                r.du[to, c : c + TILE] = u.astype(low)
                at = c % width
                r.z[z_base + c // width, span, at : at + TILE] = gelu(u).astype(low)
            z = [r.z[z_base + i, span, :] for i in range(ff // width)]
            for c in range(0, width, TILE):
                y = dot_nn(z[0], r.wdown[0:width, c : c + TILE])
                for i in range(1, ff // width):
                    y = y + dot_nn(z[i], r.wdown[i * width : (i + 1) * width, c : c + TILE])
                r.t[span, c : c + TILE] = y
            for start in half_chunks(half):
                part = pl.ds(start, CHUNK)
                y = r.t[part, :]
                r.y[mb, part, :] = y.astype(low)
                r.fout[job, part, :] = (r.m[part, :] + mod_row(mb, half, 5) * y).astype(low)

            @pl.when(jnp.logical_or(jnp.logical_not(is_last), job < micro))
            def _():
                forward_copy(job, jnp.where(is_last, job + micro, job), half).start()

        if fused:

            @pl.when(job >= micro)
            def _():
                spread(r.a2, r.a2ss, r.a2rs, mb, False)

        return carry

    lax.fori_loop(0, 2 * micro, forward_job, 0)
    if fused:
        pl.semaphore_signal(
            r.done,
            inc=1,
            device_id=(section, z_at * CORES + 1 - core),
            device_id_type=MESH,
        )

    def norm_backward(mb, k_scale, n_keep, r_keep, base, per_chunk):
        for half in range(halves):
            shift_sum = jnp.zeros((8, width), wide)
            scale_sum = jnp.zeros((8, width), wide)
            gate_sum = jnp.zeros((8, width), wide)
            for start in half_chunks(half):
                span = pl.ds(start, CHUNK)
                da = r.t[span, :]
                n = n_keep[mb_span(mb, start), :].astype(wide)
                inverse = r_keep[mb, span, :]
                shift_sum = shift_sum + fold(da)
                scale_sum = scale_sum + fold(da * n)
                dn = da * (1.0 + mod_row(mb, half, k_scale))
                dv = inverse * (
                    dn
                    - jnp.mean(dn, axis=-1, keepdims=True)
                    - n * jnp.mean(dn * n, axis=-1, keepdims=True)
                )
                extra = per_chunk(span, half, base[span, :] + dv)
                if extra is not None:
                    gate_sum = gate_sum + fold(extra)
            r.dmod[mb, half, k_scale - 1, :] = jnp.sum(shift_sum, axis=0)
            r.dmod[mb, half, k_scale, :] = jnp.sum(scale_sum, axis=0)
            if k_scale == 4:
                r.dmod[mb, half, 2, :] = jnp.sum(gate_sum, axis=0)
            else:

                @pl.when(jnp.logical_not(is_first))
                def _():
                    backward_copy(mb, half).start()

    def backward_job(mb, carry):
        g_s = r.h
        here = mb_rows(mb)
        z_base = 0 if fused else micro * (ff // width)

        for half in range(halves):
            rows_of = pl.ds(half * half_rows, half_rows)

            @pl.when(is_last)
            def _():
                g_s[rows_of, :] = r.cot[mb, rows_of, :].astype(wide)

            @pl.when(jnp.logical_not(is_last))
            def _():
                backward_copy(mb, half).wait_recv()
                g_s[rows_of, :] = r.brecv[mb, rows_of, :].astype(wide)

            gate_sum = jnp.zeros((8, width), wide)
            for start in half_chunks(half):
                span = pl.ds(start, CHUNK)
                g = g_s[span, :]
                gate_sum = gate_sum + fold(g * r.y[mb, span, :].astype(wide))
                r.dy[mb, own, span, :] = (mod_row(mb, half, 5) * g).astype(low)
            r.dmod[mb, half, 5, :] = jnp.sum(gate_sum, axis=0)
        if fused:
            spread(r.dy, r.dyss, r.dyrs, mb, False)
        dy = r.dy[mb, own]
        for c in range(0, ff, TILE):
            dz = dot_nt(dy, r.wdown[c : c + TILE, :])
            u = r.du[mb_rows(mb), c : c + TILE].astype(wide)
            r.du[mb_rows(mb), c : c + TILE] = (gelu_both(u)[1] * dz).astype(low)
        du = r.du[mb_rows(mb), :]
        for c in range(0, width, TILE):
            r.t[:, c : c + TILE] = dot_nt(du, r.win[c : c + TILE, :])

        def after_mlp(span, half, dm):
            r.m[span, :] = dm
            extra = dm * r.dattn[mb, span, :].astype(wide)
            r.dattn[mb, span, :] = (mod_row(mb, half, 2) * dm).astype(low)
            return extra

        norm_backward(mb, 4, r.n2, r.r2, g_s, after_mlp)
        dattn = r.dattn[mb]
        for c in range(0, width, TILE):
            r.do[:, c : c + TILE] = dot_nt(dattn, r.wa[c : c + TILE, qkv_width:]).astype(low)
        q_tag = r.tags[0, mb]
        k_tag = r.tags[1, mb]

        def pulls(c):
            q, k, v = [r.qkvo[here, i * width + c : i * width + c + 128] for i in range(3)]
            do = r.do[:, c : c + 128]
            k_wide = jnp.concatenate([k, k_tag], axis=1)
            found = []
            for mask in masks:
                s = dot_nt(k_wide, jnp.concatenate([q * (mask * scale), q_tag], axis=1))
                found.append((s, dot_nt(v * mask, do)))
            return found, q, k, do

        def push(c, found, q, k, do):
            parts = []
            for s, dp in found:
                e = jnp.exp(s - jnp.max(s, axis=0, keepdims=True))
                p = e * (1.0 / jnp.sum(e, axis=0, keepdims=True))
                inner = jnp.sum(p * dp, axis=0, keepdims=True)
                ds = (p * (dp - inner)).astype(low)
                parts.append((dot_tn(ds, k), dot_nn(ds, q), dot_nn(p.astype(low), do)))
            for i, factor in enumerate((scale, scale, 1.0)):
                both = jnp.where(first_lanes, parts[0][i], parts[1][i])
                r.z[z_base + i, :, c : c + 128] = (both * factor).astype(low)

        ahead = pulls(0)
        for c in range(0, width, 128):
            current = ahead
            if c + 128 < width:
                ahead = pulls(c + 128)
            push(c, *current)
        dqkv = [r.z[z_base + i] for i in range(3)]
        for i in range(3):
            r.qkvo[here, i * width : (i + 1) * width] = dqkv[i]
        for c in range(0, width, TILE):
            pulled = dot_nt(dqkv[0], r.wa[c : c + TILE, 0:width])
            for i in range(1, 3):
                pulled = pulled + dot_nt(
                    dqkv[i], r.wa[c : c + TILE, i * width : (i + 1) * width]
                )
            r.t[:, c : c + TILE] = pulled

        def after_attention(span, half, dh):
            r.gin[mb, span, :] = dh.astype(low)

        norm_backward(mb, 1, r.n1, r.r1, r.m, after_attention)
        return carry

    lax.fori_loop(0, micro, backward_job, 0)

    if fused:
        gradient_tail(r, section, z_at, core, member, remote, spread, relay, await_block)

    for half in range(halves):
        for job in range(2 * micro):

            @pl.when(jnp.logical_or(jnp.logical_not(is_last), job < micro))
            def _():
                forward_copy(job, job, half).wait_send()

        for job in range(micro):

            @pl.when(jnp.logical_not(is_first))
            def _():
                backward_copy(job, half).wait_send()


def gradient_tail(r, section, z_at, core, member, remote, spread, relay, await_block):
    micro, rows, width = r.x.shape
    ff = r.win.shape[1]
    share = width // (DEEP * CORES)
    part = ff // DEEP
    half_part = part // CORES
    other = 1 - core
    partner = (section, z_at * CORES + other)
    qkv_width = 3 * width

    def on_z(z):
        return (section, z * CORES + core)

    for step in (1, -1):

        @pl.when(jnp.logical_and(z_at + step >= 0, z_at + step < DEEP))
        def _():
            pl.semaphore_signal(
                r.free,
                inc=1,
                device_id=on_z(jnp.clip(z_at + step, 0, DEEP - 1)),
                device_id_type=MESH,
            )

    mine = r.ada.at[core, z_at]
    for mb in range(micro):
        sums = r.dmod[mb]
        mine[mb, :, 0:width] = sums.reshape(sums.shape[0] * sums.shape[1], width).astype(low)
        mine[mb, :, width:] = r.feat[mb]

    def ada_copy(away):
        target = lax.rem(z_at + away, DEEP)
        return remote(
            mine, mine, r.adass.at[away - 1], r.adars.at[z_at], (section, target * CORES + core)
        )

    for away in range(1, DEEP):
        ada_copy(away).start()

    def flat(ref):
        block = ref[...]
        return block.reshape(micro * rows, block.shape[-1])

    a1_t = flat(r.a1).T
    for c in range(0, qkv_width, TILE):
        r.wa[:, c : c + TILE] = dot_nn(a1_t, r.qkvo[:, c : c + TILE]).astype(low)
    o_t = r.qkvo[:, qkv_width:].T
    dattn = flat(r.dattn)
    for c in range(0, width, TILE):
        r.wa[:, qkv_width + c : qkv_width + c + TILE] = dot_nn(
            o_t, dattn[:, c : c + TILE]
        ).astype(low)

    def share_rows(z, of_core):
        return pl.ds(pl.multiple_of((z * CORES + of_core) * share, share), share)

    def pair_copy(z):
        return remote(
            r.wa.at[share_rows(z, other), :], r.pa.at[z], r.pss.at[z], r.prs.at[z], partner
        )

    for z in (0, DEEP - 1, 1, DEEP - 2):
        pair_copy(z).start()

    r.pdown[...] = jnp.zeros_like(r.pdown)
    r.pin[...] = jnp.zeros_like(r.pin)
    for mb in range(micro):
        relay(r.a2, r.a2ss, r.a2rs, mb, False)

    group = 2

    def mlp_group(mb, first):
        for step in range(group):
            await_block(r.a2, r.a2ss, r.a2rs, mb, first + step)
            await_block(r.dy, r.dyss, r.dyrs, mb, first + step)
        tokens = group * rows
        a2 = r.a2[mb, pl.ds(first, group)].reshape(tokens, width)
        dy = r.dy[mb, pl.ds(first, group)].reshape(tokens, width)
        for c in range(0, part, TILE):
            at = pl.ds(pl.multiple_of(z_at * part + c, TILE), TILE)
            u = dot_nn(a2, r.win[:, at])
            dz = dot_nt(dy, r.wdown[at, :])
            active, slope = gelu_both(u)
            r.z[0:group, :, c : c + TILE] = active.astype(low).reshape(group, rows, TILE)
            r.z[group:, :, c : c + TILE] = (slope * dz).astype(low).reshape(group, rows, TILE)
        z_t = r.z[0:group].reshape(tokens, part).T
        a2_t = a2.T
        for c in range(0, width, TILE):
            r.pdown[:, c : c + TILE] += dot_nn(z_t, dy[:, c : c + TILE])
        for c in range(0, part, TILE):
            r.pin[:, c : c + TILE] += dot_nn(a2_t, r.z[group:, :, c : c + TILE].reshape(tokens, TILE))

    def sums(z):
        return r.qkvo.at[z * share : (z + 1) * share, :]

    def sum_pair(z):
        pair_copy(z).wait_recv()
        sums(z)[...] = (r.wa[share_rows(z, core), :].astype(wide) + r.pa[z].astype(wide)).astype(
            low
        )

    def slot_of(z, direction):
        if direction > 0:
            return z - 1
        return DEEP - 1 + z if z < DEEP - 2 else 0

    def slot_ref(z, direction):
        return r.du.at[pl.ds(slot_of(z, direction) * share, share), :]

    def line_copy(z, direction):
        slot = slot_of(z, direction)
        return remote(
            sums(z),
            slot_ref(z, direction),
            r.lss.at[z],
            r.lrs.at[slot],
            on_z(jnp.clip(z_at + direction, 0, DEEP - 1)),
        )

    def passes(z, direction):
        return z_at < z if direction > 0 else z_at > z

    def takes(direction):
        return z_at > 0 if direction > 0 else z_at < DEEP - 1

    def add_slot(z, direction):
        line_copy(z, direction).wait_recv()
        sums(z)[...] = (
            sums(z)[...].astype(wide) + slot_ref(z, direction)[...].astype(wide)
        ).astype(low)

    def line_start(z, direction):
        @pl.when(jnp.logical_and(passes(z, direction), jnp.logical_not(takes(direction))))
        def _():
            line_copy(z, direction).start()

    def line_pass(z, direction, at):
        @pl.when(z_at == at)
        def _():
            add_slot(z, direction)
            line_copy(z, direction).start()

    for at in range(DEEP):

        @pl.when(z_at == at)
        def _():
            pl.semaphore_wait(r.free, (at > 0) + (at < DEEP - 1))

    for z in (0, DEEP - 1, 1, DEEP - 2):
        sum_pair(z)
        if z > 0:
            line_start(z, 1)
        if z < DEEP - 1:
            line_start(z, -1)

    def group_step(g, carry):
        @pl.when(g == 0)
        def _():
            relay(r.dy, r.dyss, r.dyrs, 0, False)

        @pl.when(g == 2)
        def _():
            line_pass(3, 1, 1)
            line_pass(0, -1, 2)
            relay(r.dy, r.dyss, r.dyrs, 1, False)

        @pl.when(g == 3)
        def _():
            line_pass(2, 1, 1)
            line_pass(1, -1, 2)
            line_pass(3, 1, 2)
            line_pass(0, -1, 1)

        mlp_group(lax.div(g, 2), lax.rem(g, 2) * group)
        return carry

    lax.fori_loop(0, micro * DEEP // group, group_step, 0)

    def down_copy():
        return remote(
            r.n1.at[pl.ds(0, half_part), :],
            r.frecv.at[pl.ds(width // CORES, half_part), :],
            r.mss.at[DEEP],
            r.mrs.at[DEEP],
            partner,
        )

    def up_copy(z):
        return remote(
            r.cols.at[z],
            r.frecv.at[pl.ds(z * share, share), :],
            r.mss.at[z],
            r.mrs.at[z],
            partner,
        )

    pl.semaphore_wait(r.done, 1)
    for z in range(DEEP):
        r.cols[z] = r.pin[share_rows(z, other), :].astype(low)
        up_copy(z).start()
    r.n1[0:half_part, :] = r.pdown[
        pl.ds(pl.multiple_of(other * half_part, half_part), half_part), :
    ].astype(low)
    down_copy().start()

    def column_copy(z):
        return remote(
            r.cols2.at[z], r.land.at[z_at], r.css.at[z], r.crs.at[z_at], on_z(z)
        )

    def part_columns(z):
        return pl.ds(pl.multiple_of(z * part, part), part)

    for z in range(DEEP):
        up_copy(z).wait_recv()
        total = r.pin[share_rows(z, core), :] + r.frecv[z * share : (z + 1) * share, :].astype(wide)

        @pl.when(z_at == z)
        def _():
            r.g_up[:, part_columns(z)] = total

        @pl.when(z_at != z)
        def _():
            r.cols2[z] = total.astype(low)
            column_copy(z).start()

    def ada_pair():
        return remote(
            r.ada.at[core], r.ada.at[core], r.adass.at[DEEP - 1], r.adars.at[DEEP], partner
        )

    def ada_other():
        return remote(
            r.ada.at[other], r.ada.at[other], r.adass.at[DEEP - 1], r.adars.at[DEEP], partner
        )

    for z in range(DEEP):

        @pl.when(z_at != z)
        def _():
            remote(
                r.ada.at[core, z], r.ada.at[core, z], r.adass.at[0], r.adars.at[z], partner
            ).wait_recv()

    ada_pair().start()

    down_copy().wait_recv()
    own_half = pl.ds(pl.multiple_of(core * half_part, half_part), half_part)
    r.g_down[...] = r.pdown[own_half, :] + r.frecv[
        width // CORES : width // CORES + half_part, :
    ].astype(wide)

    ada_other().wait_recv()
    entries = CORES * DEEP * micro * r.feat.shape[1]
    ada_rows = TEMB // (DEEP * CORES)
    pick = lax.broadcasted_iota(jnp.int32, (ada_rows, TEMB), 1) == (
        lax.broadcasted_iota(jnp.int32, (ada_rows, TEMB), 0) + member * ada_rows
    )
    features = r.ada[:, :, :, :, width:].reshape(entries, TEMB)
    gathered = r.ada[:, :, :, :, 0:width].reshape(entries, width)
    spreads = dot_nt(pick.astype(wide).astype(low), features)
    which = lax.rem(lax.broadcasted_iota(jnp.int32, (ada_rows, entries), 1), 8)
    for k in range(6):
        chosen = jnp.where(which == k, spreads, 0.0).astype(low)
        r.g_ada[:, k * width : (k + 1) * width] = dot_nn(chosen, gathered)

    def finish(z):
        for direction in (1, -1):

            @pl.when(takes(direction))
            def _():
                if (direction > 0 and z > 0) or (direction < 0 and z < DEEP - 1):
                    line_copy(z, direction).wait_recv()
        total = sums(z)[...].astype(wide)
        if z > 0:
            total = total + slot_ref(z, 1)[...].astype(wide)
        if z < DEEP - 1:
            total = total + slot_ref(z, -1)[...].astype(wide)
        r.g_qkv[...] = total[:, 0:qkv_width]
        r.g_out[...] = total[:, qkv_width:]

    for z in range(DEEP):

        @pl.when(z_at == z)
        def _():
            finish(z)

    for z in range(DEEP):

        @pl.when(z_at != z)
        def _():
            remote(
                r.cols2.at[z], r.land.at[z], r.css.at[z], r.crs.at[z], on_z(z)
            ).wait_recv()
            r.g_up[:, z * part : (z + 1) * part] = r.land[z].astype(wide)

    for mb in range(micro):
        spread(r.a2, r.a2ss, r.a2rs, mb, True)
        spread(r.dy, r.dyss, r.dyrs, mb, True)
        relay(r.a2, r.a2ss, r.a2rs, mb, True)
        relay(r.dy, r.dyss, r.dyrs, mb, True)
    for away in range(1, DEEP):
        ada_copy(away).wait_send()
    ada_pair().wait_send()
    for z in range(DEEP):
        pair_copy(z).wait_send()
        up_copy(z).wait_send()

        @pl.when(z_at != z)
        def _():
            column_copy(z).wait_send()
            line_copy(z, 1 if z > 0 else -1).wait_send()

    down_copy().wait_send()


def run_chain(x, cot, mod, tags, feat, w_qkv, w_out, w_in, w_down, members):
    micro, rows, width = x.shape
    ff = w_in.shape[1]
    sections = lax.axis_size("section")
    fused = members == DEEP * CORES
    vmem = pl.BlockSpec(memory_space=pltpu.VMEM)
    hbm = pl.BlockSpec(memory_space=pl.ANY)
    dma = pltpu.SemaphoreType.DMA

    def kept(*shape):
        return jax.ShapeDtypeStruct(shape, low)

    def result(*shape):
        return jax.ShapeDtypeStruct(shape, wide)

    names = ["x", "cot", "mod", "tags", "feat", "wqkv_h", "wout_h", "win_h", "wdown_h"]
    in_specs = [vmem] * 5 + [hbm] * 4
    stored = {
        "dmod": result(*mod.shape),
        "a1": kept(micro, rows, width),
        "qkvo": kept(micro * rows, 4 * width),
        "dattn": kept(micro, rows, width),
        "a2": kept(micro, DEEP if fused else 1, rows, width),
        "du": kept(micro * rows, ff),
        "z": kept((1 if fused else micro + 1) * (ff // width), rows, width),
        "dy": kept(micro, DEEP if fused else 1, rows, width),
    }
    outs = {"fout": kept(2 * micro, rows, width), "gin": kept(micro, rows, width)}
    share = width // members
    if fused:
        outs["g_qkv"] = result(share, 3 * width)
        outs["g_out"] = result(share, width)
        outs["g_up"] = result(share, ff)
        outs["g_down"] = result(ff // members, width)
        outs["g_ada"] = result(TEMB // members, 6 * width)
    else:
        outs.update(stored)
    scratch = {
        "wa": pltpu.VMEM((width, 4 * width), low),
        "win": pltpu.VMEM((width, ff), low),
        "wdown": pltpu.VMEM((ff, width), low),
        "h": pltpu.VMEM((rows, width), wide),
        "m": pltpu.VMEM((rows, width), wide),
        "t": pltpu.VMEM((rows, width), wide),
        "do": pltpu.VMEM((rows, width), low),
        "n1": pltpu.VMEM((micro * rows, width), low),
        "n2": pltpu.VMEM((micro * rows, width), low),
        "r1": pltpu.VMEM((micro, rows, 1), wide),
        "r2": pltpu.VMEM((micro, rows, 1), wide),
        "y": pltpu.VMEM((micro, rows, width), low),
        "frecv": pltpu.VMEM((2 * micro * rows, width), low),
        "brecv": pltpu.VMEM((micro, rows, width), low),
        "wsem": dma((4,)),
        "fss": dma((2 * micro, rows // SHORT)),
        "frs": dma((2 * micro, rows // SHORT)),
        "bss": dma((micro, rows // SHORT)),
        "brs": dma((micro, rows // SHORT)),
    }
    if fused:
        part = ff // DEEP
        for name, value in stored.items():
            scratch[name] = pltpu.VMEM(value.shape, value.dtype)
        scratch.update(
            {
                "pa": pltpu.VMEM((DEEP, share, 4 * width), low),
                "pdown": pltpu.VMEM((part, width), wide),
                "pin": pltpu.VMEM((width, part), wide),
                "cols": pltpu.VMEM((DEEP, share, part), low),
                "cols2": pltpu.VMEM((DEEP, share, part), low),
                "land": pltpu.VMEM((DEEP, share, part), low),
                "ada": pltpu.VMEM((CORES, DEEP, micro, feat.shape[1], width + TEMB), low),
                "free": pltpu.SemaphoreType.REGULAR,
                "done": pltpu.SemaphoreType.REGULAR,
                "a2ss": dma((micro, 5)),
                "a2rs": dma((micro, DEEP)),
                "dyss": dma((micro, 5)),
                "dyrs": dma((micro, DEEP)),
                "adass": dma((DEEP,)),
                "adars": dma((DEEP + 1,)),
                "pss": dma((DEEP,)),
                "prs": dma((DEEP,)),
                "lss": dma((DEEP,)),
                "lrs": dma((5,)),
                "mss": dma((DEEP + 1,)),
                "mrs": dma((DEEP + 1,)),
                "css": dma((DEEP,)),
                "crs": dma((DEEP,)),
            }
        )
    names = names + list(outs) + list(scratch)
    values = pl.pallas_call(
        functools.partial(chain_kernel, names, sections, fused),
        out_shape=tuple(outs.values()),
        in_specs=in_specs,
        out_specs=(vmem,) * len(outs),
        scratch_shapes=list(scratch.values()),
        compiler_params=pltpu.CompilerParams(
            collective_id=0, has_side_effects=True, vmem_limit_bytes=60 * 1024 * 1024
        ),
    )(x, cot, mod, tags, feat, w_qkv, w_out, w_in, w_down)
    return SimpleNamespace(**dict(zip(outs, values)))


def time_features(timestep_ids):
    half_width = TEMB // 2
    frequency = jnp.exp(-math.log(10000.0) * jnp.arange(half_width, dtype=wide) / half_width)
    angles = timestep_ids.astype(wide)[:, None] * 0.1 * frequency[None, :]
    return jnp.concatenate([jnp.sin(angles), jnp.cos(angles)], axis=1)


def summed_apart(kept, features, micro, rows, width):
    def product(left, right):
        left = left.reshape(micro * rows, -1)
        right = right.reshape(micro * rows, -1)
        partial = dot_tn(left, right).astype(low)
        return lax.psum_scatter(partial, "dp", scatter_dimension=0, tiled=True).astype(wide)

    sums = kept.dmod[:, :, :6].reshape(features.shape[0], 6 * width)
    features_all = lax.all_gather(features.astype(wide), "dp", tiled=True)
    sums_all = lax.all_gather(sums, "dp", tiled=True)
    share = TEMB // lax.axis_size("dp")
    mine = lax.dynamic_slice_in_dim(features_all, lax.axis_index("dp") * share, share, 1)
    grad_ada = lax.dot_general(
        mine, sums_all, (((0,), (0,)), ((), ())), precision=lax.Precision.HIGHEST
    )
    return (
        product(kept.a1, kept.qkvo[:, : 3 * width]),
        product(kept.qkvo[:, 3 * width :], kept.dattn),
        product(kept.a2, kept.du),
        product(jnp.swapaxes(kept.z.reshape(micro + 1, -1, rows, width)[:micro], 1, 2), kept.dy),
        grad_ada,
    )


def on_device(inputs, cotangent, long_count, timesteps, w_qkv, w_out, w_in, w_down, ada_weight):
    micro = long_count.shape[1]
    width = inputs.shape[1]
    rows = inputs.shape[0] // micro
    halves = rows // SHORT
    members = lax.axis_size("dp")
    is_long = (long_count[0] == 1)[:, None]
    half_index = jnp.arange(halves, dtype=jnp.int32)[None, :]
    half_steps = jnp.where(is_long, timesteps[0][:, :1], timesteps[0][:, :halves])
    features = time_features(half_steps.reshape(-1)).astype(low)
    mod = jnp.dot(features, ada_weight[0], preferred_element_type=wide)
    mod = mod.reshape(micro, halves, 6, width)
    mod = jnp.pad(mod, ((0, 0), (0, 0), (0, 2), (0, 0)))
    feat = jnp.repeat(features.reshape(micro, halves, TEMB), 8, axis=1)
    slot_ids = jnp.where(is_long, 0, jnp.repeat(half_index, SHORT, axis=1))
    spots = jnp.arange(128, dtype=jnp.int32)[None, None, :]
    in_slot = slot_ids[:, :, None] == spots
    barred = jnp.where(jnp.logical_or(in_slot, spots >= halves), 0.0, -1e30)
    tags = jnp.stack([in_slot.astype(wide), barred]).astype(low)
    kept = run_chain(
        inputs.reshape(micro, rows, width),
        cotangent.reshape(micro, rows, width),
        mod,
        tags,
        feat,
        w_qkv[0],
        w_out[0],
        w_in[0],
        w_down[0],
        members,
    )
    if members == DEEP * CORES:
        grads = (kept.g_qkv, kept.g_out, kept.g_up, kept.g_down, kept.g_ada)
    else:
        grads = summed_apart(kept, features, micro, rows, width)
    hidden_out = kept.fout[micro:].reshape(1, micro * rows, width)
    grad_in = kept.gin.reshape(1, micro * rows, width)
    return (hidden_out, grad_in) + tuple(grad[None] for grad in grads)


def solution(mesh):
    placed = (
        P("dp", None),
        P("dp", None),
        P("dp", None),
        P("dp", None, None),
        P("section", None, None),
        P("section", None, None),
        P("section", None, None),
        P("section", None, None),
        P("section", None, None),
    )
    return jax.shard_map(
        on_device,
        mesh=mesh,
        in_specs=placed,
        out_specs=(P("section", "dp", None),) * 7,
        check_vma=False,
    )
```

```python
import functools
import math
from types import SimpleNamespace

import jax
import jax.numpy as jnp
from jax import lax
from jax.experimental import pallas as pl
from jax.experimental.pallas import tpu as pltpu
from jax.sharding import PartitionSpec as P

HEADS = 12
TEMB = 128
SHORT = 128
TILE = 256
CHUNK = 32
CORES = 2
DEEP = 4
INNER = (1, 2)
norm_eps = 1e-06
MESH = pl.DeviceIdType.MESH
low = jnp.bfloat16
wide = jnp.float32


def dot_nn(a, b):
    return lax.dot_general(a, b, (((1,), (0,)), ((), ())), preferred_element_type=wide)


def dot_nt(a, b):
    return lax.dot_general(a, b, (((1,), (1,)), ((), ())), preferred_element_type=wide)


def dot_tn(a, b):
    return lax.dot_general(a, b, (((0,), (0,)), ((), ())), preferred_element_type=wide)


def fold(block):
    total = block[0:8]
    for start in range(8, block.shape[0], 8):
        total = total + block[start : start + 8]
    return total


GELU_C = math.sqrt(2.0 / math.pi)


def gelu(u):
    t = jnp.tanh(GELU_C * (u + 0.044715 * (u * u * u)))
    return 0.5 * u * (1.0 + t)


def gelu_both(u):
    square = u * u
    t = jnp.tanh(GELU_C * (u + 0.044715 * (square * u)))
    outer = 0.5 * (1.0 + t)
    slope = outer + 0.5 * u * (1.0 - t * t) * (GELU_C * (1.0 + (3.0 * 0.044715) * square))
    return u * outer, slope


def chain_kernel(names, sections, fused, *refs):
    r = SimpleNamespace(**dict(zip(names, refs)))
    micro, rows, width = r.x.shape
    ff = r.win.shape[1]
    qkv_width = 3 * width
    half_rows = SHORT

    def half_chunks(half):
        return range(half * half_rows, (half + 1) * half_rows, CHUNK)

    halves = rows // half_rows
    section = lax.axis_index("section")
    member = lax.axis_index("dp")
    z_at = lax.div(member, CORES)
    core = lax.rem(member, CORES)
    own = z_at if fused else 0
    right = lax.rem(section + 1, sections)
    left = lax.rem(section + sections - 1, sections)
    is_first = section == 0
    is_last = section == sections - 1

    maps = []
    for k in range(6):
        spot = pl.ds(k % 2 * TEMB, TEMB)
        copy = pltpu.make_async_copy(
            r.ada_h.at[:, pl.ds(k * width, width)], r.z.at[k // 2, spot, :], r.msem.at[k]
        )
        copy.start()
        maps.append(copy)

    loads = []
    for index, (hbm, vmem) in enumerate(
        (
            (r.wqkv_h, r.wa.at[:, 0:qkv_width]),
            (r.wout_h, r.wa.at[:, qkv_width:]),
            (r.win_h, r.win),
            (r.wdown_h, r.wdown),
        )
    ):
        loads.append(pltpu.make_async_copy(hbm, vmem, r.wsem.at[index]))
        if index == 0:
            loads[index].start()

    barrier = pltpu.get_barrier_semaphore()
    greeted = [(left, member), (right, member)]
    if fused:
        greeted.append((section, z_at * CORES + 1 - core))
        for away in range(1, DEEP):
            greeted.append((section, lax.rem(z_at + away, DEEP) * CORES + core))
    for target in greeted:
        pl.semaphore_signal(barrier, inc=1, device_id=target, device_id_type=MESH)
    pl.semaphore_wait(barrier, len(greeted))

    def remote(src, dst, send_sem, recv_sem, target):
        return pltpu.make_async_remote_copy(
            src_ref=src,
            dst_ref=dst,
            send_sem=send_sem,
            recv_sem=recv_sem,
            device_id=target,
            device_id_type=MESH,
        )

    def forward_copy(job, slot, half):
        span = pl.ds(half * half_rows, half_rows)
        landing = pl.ds(
            pl.multiple_of(slot * rows + half * half_rows, half_rows), half_rows
        )
        return remote(
            r.fout.at[job, span, :],
            r.frecv.at[landing, :],
            r.fss.at[job, half],
            r.frs.at[slot, half],
            (right, member),
        )

    def backward_copy(job, half):
        span = pl.ds(half * half_rows, half_rows)
        return remote(
            r.gin.at[job, span, :],
            r.brecv.at[job, span, :],
            r.bss.at[job, half],
            r.brs.at[job, half],
            (left, member),
        )

    def mod_row(mb, half, k):
        return r.mod[mb, half, pl.ds(k, 1), :]

    def mb_rows(mb):
        return pl.ds(pl.multiple_of(mb * rows, rows), rows)

    def mb_span(mb, start):
        return pl.ds(pl.multiple_of(mb * rows + start, CHUNK), CHUNK)

    lane = lax.broadcasted_iota(jnp.int32, (1, 128), 1)
    first_lanes = lane < 64
    masks = [first_lanes.astype(wide).astype(low), (1.0 - first_lanes.astype(wide)).astype(low)]
    scale = (width // HEADS) ** (-0.5)
    ones = jnp.ones((rows, 128), low)

    def spread(buffer, send_sems, recv_sems, mb, wait):
        for k, target in enumerate(INNER):

            @pl.when(z_at != target)
            def _():
                copy = remote(
                    buffer.at[mb, z_at],
                    buffer.at[mb, z_at],
                    send_sems.at[mb, k],
                    recv_sems.at[mb, z_at],
                    (section, target * CORES + core),
                )
                copy.wait_send() if wait else copy.start()

    def await_block(buffer, send_sems, recv_sems, mb, source):
        @pl.when(z_at != source)
        def _():
            remote(
                buffer.at[mb, source],
                buffer.at[mb, source],
                send_sems.at[mb, 0],
                recv_sems.at[mb, source],
                (section, member),
            ).wait_recv()

    def norm_forward(src, mb, half, k_shift, k_scale, n_keep, r_keep, out):
        for start in half_chunks(half):
            span = pl.ds(start, CHUNK)
            v = src[span, :]
            centered = v - jnp.mean(v, axis=-1, keepdims=True)
            inverse = lax.rsqrt(jnp.mean(centered * centered, axis=-1, keepdims=True) + norm_eps)
            n = centered * inverse
            n_keep[mb_span(mb, start), :] = n.astype(low)
            r_keep[mb, span, :] = inverse
            out[span, :] = (
                n * (1.0 + mod_row(mb, half, k_scale)) + mod_row(mb, half, k_shift)
            ).astype(low)

    r.dmod[...] = jnp.zeros_like(r.dmod)

    for mb in range(micro):
        long_row = (lane * 0 + r.long[0, mb]).astype(wide)
        for half in range(halves):
            here = (lane == 0).astype(wide)
            there = (lane == half).astype(wide)
            in_slot = long_row * here + (1.0 - long_row) * there
            barred = (lane < halves).astype(wide) * (1.0 - in_slot) * -1e30
            span = pl.ds(half * half_rows, half_rows)
            r.tags[0, mb, span, :] = jnp.broadcast_to(in_slot, (half_rows, 128)).astype(low)
            r.tags[1, mb, span, :] = jnp.broadcast_to(barred, (half_rows, 128)).astype(low)

    pairs = [(mb, half) for mb in range(micro) for half in range(halves)]
    row = lax.broadcasted_iota(jnp.int32, (8 * len(pairs), TEMB), 0)
    steps = jnp.zeros((8 * len(pairs), TEMB), jnp.int32)
    for i, (mb, half) in enumerate(pairs):
        flag = r.long[0, mb]
        chosen = flag * r.steps[0, mb, 0] + (1 - flag) * r.steps[0, mb, half]
        steps = jnp.where(row // 8 == i, chosen, steps)
    feature = lax.broadcasted_iota(jnp.int32, (8 * len(pairs), TEMB), 1)
    half_width = TEMB // 2
    position = lax.rem(feature, half_width).astype(wide)
    angles = steps.astype(wide) * 0.1 * jnp.exp(position * (-math.log(10000.0) / half_width))
    features = jnp.where(feature < half_width, jnp.sin(angles), jnp.cos(angles)).astype(low)
    r.feat[...] = features.reshape(micro, 8 * halves, TEMB)
    for copy in maps:
        copy.wait()
    for copy in loads[1:]:
        copy.start()
    for k in range(6):
        spot = pl.ds(k % 2 * TEMB, TEMB)
        found = dot_nn(features, r.z[k // 2, spot, :])
        for i, (mb, half) in enumerate(pairs):
            r.mod[mb, half, k : k + 1, :] = found[8 * i : 8 * i + 1, :]

    def forward_job(job, carry):
        mb = lax.rem(job, micro)
        here = mb_rows(mb)
        z_base = 0 if fused else mb * (ff // width)

        def wait_load(index):
            @pl.when(job == 0)
            def _():
                loads[index].wait()

        for half in range(halves):
            span = pl.ds(half * half_rows, half_rows)
            arrived = pl.ds(
                pl.multiple_of(job * rows + half * half_rows, half_rows), half_rows
            )

            @pl.when(jnp.logical_or(jnp.logical_not(is_first), job >= micro))
            def _():
                forward_copy(job, job, half).wait_recv()

            @pl.when(jnp.logical_and(is_first, job < micro))
            def _():
                r.h[span, :] = r.x[mb, span, :].astype(wide)

            @pl.when(jnp.logical_and(is_first, job >= micro))
            def _():
                r.h[span, :] = r.x[mb, span, :].astype(wide) + r.frecv[arrived, :].astype(wide)

            @pl.when(jnp.logical_not(is_first))
            def _():
                r.h[span, :] = r.frecv[arrived, :].astype(wide)

            norm_forward(r.h, mb, half, 0, 1, r.n1, r.r1, r.a1.at[mb])
            if half == 0:
                wait_load(0)
            a1 = r.a1[mb, span, :]
            to = pl.ds(pl.multiple_of(mb * rows + half * half_rows, half_rows), half_rows)
            for c in range(0, qkv_width, TILE):
                r.qkvo[to, c : c + TILE] = dot_nn(a1, r.wa[:, c : c + TILE]).astype(low)

        q_tag = r.tags[0, mb]
        k_tag = r.tags[1, mb]

        def scores(c):
            q, k, v = [r.qkvo[here, i * width + c : i * width + c + 128] for i in range(3)]
            k_wide = jnp.concatenate([k, k_tag], axis=1)
            found = [
                dot_nt(jnp.concatenate([q * (mask * scale), q_tag], axis=1), k_wide)
                for mask in masks
            ]
            return found, jnp.concatenate([v, ones], axis=1)

        def mix(c, found, v_wide):
            weights = [jnp.exp(s - jnp.max(s, axis=1, keepdims=True)).astype(low) for s in found]
            mixed = [dot_nn(e, v_wide) for e in weights]
            top = jnp.where(first_lanes, mixed[0][:, 0:128], mixed[1][:, 0:128])
            total = jnp.where(first_lanes, mixed[0][:, 128:], mixed[1][:, 128:])
            r.do[:, c : c + 128] = (top * (1.0 / total)).astype(low)

        ahead = scores(0)
        for c in range(0, width, 128):
            current = ahead
            if c + 128 < width:
                ahead = scores(c + 128)
            mix(c, *current)
        wait_load(1)
        wait_load(2)
        wait_load(3)
        r.qkvo[here, qkv_width:] = r.do[...]
        for half in range(halves):
            span = pl.ds(half * half_rows, half_rows)
            to = pl.ds(pl.multiple_of(mb * rows + half * half_rows, half_rows), half_rows)
            o = r.do[span, :]
            for c in range(0, width, TILE):
                r.t[span, c : c + TILE] = dot_nn(o, r.wa[:, qkv_width + c : qkv_width + c + TILE])
            for start in half_chunks(half):
                part = pl.ds(start, CHUNK)
                attn = r.t[part, :]
                r.dattn[mb, part, :] = attn.astype(low)
                r.m[part, :] = r.h[part, :] + mod_row(mb, half, 2) * attn
            norm_forward(r.m, mb, half, 3, 4, r.n2, r.r2, r.a2.at[mb, own])
            a2 = r.a2[mb, own, span, :]
            for c in range(0, ff, TILE):
                u = dot_nn(a2, r.win[:, c : c + TILE])
                r.du[to, c : c + TILE] = u.astype(low)
                at = c % width
                r.z[z_base + c // width, span, at : at + TILE] = gelu(u).astype(low)
            z = [r.z[z_base + i, span, :] for i in range(ff // width)]
            for c in range(0, width, TILE):
                y = dot_nn(z[0], r.wdown[0:width, c : c + TILE])
                for i in range(1, ff // width):
                    y = y + dot_nn(z[i], r.wdown[i * width : (i + 1) * width, c : c + TILE])
                r.t[span, c : c + TILE] = y
            for start in half_chunks(half):
                part = pl.ds(start, CHUNK)
                y = r.t[part, :]
                r.y[mb, part, :] = y.astype(low)
                r.fout[job, part, :] = (r.m[part, :] + mod_row(mb, half, 5) * y).astype(low)

            @pl.when(jnp.logical_or(jnp.logical_not(is_last), job < micro))
            def _():
                forward_copy(job, jnp.where(is_last, job + micro, job), half).start()

        if fused:

            @pl.when(job >= micro)
            def _():
                spread(r.a2, r.a2ss, r.a2rs, mb, False)

        return carry

    lax.fori_loop(0, 2 * micro, forward_job, 0)
    if fused:
        pl.semaphore_signal(
            r.done,
            inc=1,
            device_id=(section, z_at * CORES + 1 - core),
            device_id_type=MESH,
        )

    def norm_backward(mb, k_scale, n_keep, r_keep, base, per_chunk):
        for half in range(halves):
            shift_sum = jnp.zeros((8, width), wide)
            scale_sum = jnp.zeros((8, width), wide)
            gate_sum = jnp.zeros((8, width), wide)
            for start in half_chunks(half):
                span = pl.ds(start, CHUNK)
                da = r.t[span, :]
                n = n_keep[mb_span(mb, start), :].astype(wide)
                inverse = r_keep[mb, span, :]
                shift_sum = shift_sum + fold(da)
                scale_sum = scale_sum + fold(da * n)
                dn = da * (1.0 + mod_row(mb, half, k_scale))
                dv = inverse * (
                    dn
                    - jnp.mean(dn, axis=-1, keepdims=True)
                    - n * jnp.mean(dn * n, axis=-1, keepdims=True)
                )
                extra = per_chunk(span, half, base[span, :] + dv)
                if extra is not None:
                    gate_sum = gate_sum + fold(extra)
            r.dmod[mb, half, k_scale - 1, :] = jnp.sum(shift_sum, axis=0)
            r.dmod[mb, half, k_scale, :] = jnp.sum(scale_sum, axis=0)
            if k_scale == 4:
                r.dmod[mb, half, 2, :] = jnp.sum(gate_sum, axis=0)
            else:

                @pl.when(jnp.logical_not(is_first))
                def _():
                    backward_copy(mb, half).start()

    def backward_job(mb, carry):
        g_s = r.h
        here = mb_rows(mb)
        z_base = 0 if fused else micro * (ff // width)

        for half in range(halves):
            rows_of = pl.ds(half * half_rows, half_rows)

            @pl.when(is_last)
            def _():
                g_s[rows_of, :] = r.cot[mb, rows_of, :].astype(wide)

            @pl.when(jnp.logical_not(is_last))
            def _():
                backward_copy(mb, half).wait_recv()
                g_s[rows_of, :] = r.brecv[mb, rows_of, :].astype(wide)

            gate_sum = jnp.zeros((8, width), wide)
            for start in half_chunks(half):
                span = pl.ds(start, CHUNK)
                g = g_s[span, :]
                gate_sum = gate_sum + fold(g * r.y[mb, span, :].astype(wide))
                r.dy[mb, own, span, :] = (mod_row(mb, half, 5) * g).astype(low)
            r.dmod[mb, half, 5, :] = jnp.sum(gate_sum, axis=0)
        if fused:
            spread(r.dy, r.dyss, r.dyrs, mb, False)
        dy = r.dy[mb, own]
        for c in range(0, ff, TILE):
            dz = dot_nt(dy, r.wdown[c : c + TILE, :])
            u = r.du[mb_rows(mb), c : c + TILE].astype(wide)
            r.du[mb_rows(mb), c : c + TILE] = (gelu_both(u)[1] * dz).astype(low)
        du = r.du[mb_rows(mb), :]
        for c in range(0, width, TILE):
            r.t[:, c : c + TILE] = dot_nt(du, r.win[c : c + TILE, :])

        def after_mlp(span, half, dm):
            r.m[span, :] = dm
            extra = dm * r.dattn[mb, span, :].astype(wide)
            r.dattn[mb, span, :] = (mod_row(mb, half, 2) * dm).astype(low)
            return extra

        norm_backward(mb, 4, r.n2, r.r2, g_s, after_mlp)
        dattn = r.dattn[mb]
        for c in range(0, width, TILE):
            r.do[:, c : c + TILE] = dot_nt(dattn, r.wa[c : c + TILE, qkv_width:]).astype(low)
        q_tag = r.tags[0, mb]
        k_tag = r.tags[1, mb]

        def pulls(c):
            q, k, v = [r.qkvo[here, i * width + c : i * width + c + 128] for i in range(3)]
            do = r.do[:, c : c + 128]
            k_wide = jnp.concatenate([k, k_tag], axis=1)
            found = []
            for mask in masks:
                s = dot_nt(k_wide, jnp.concatenate([q * (mask * scale), q_tag], axis=1))
                found.append((s, dot_nt(v * mask, do)))
            return found, q, k, do

        def push(c, found, q, k, do):
            parts = []
            for s, dp in found:
                e = jnp.exp(s - jnp.max(s, axis=0, keepdims=True))
                p = e * (1.0 / jnp.sum(e, axis=0, keepdims=True))
                inner = jnp.sum(p * dp, axis=0, keepdims=True)
                ds = (p * (dp - inner)).astype(low)
                parts.append((dot_tn(ds, k), dot_nn(ds, q), dot_nn(p.astype(low), do)))
            for i, factor in enumerate((scale, scale, 1.0)):
                both = jnp.where(first_lanes, parts[0][i], parts[1][i])
                r.z[z_base + i, :, c : c + 128] = (both * factor).astype(low)

        ahead = pulls(0)
        for c in range(0, width, 128):
            current = ahead
            if c + 128 < width:
                ahead = pulls(c + 128)
            push(c, *current)
        dqkv = [r.z[z_base + i] for i in range(3)]
        for i in range(3):
            r.qkvo[here, i * width : (i + 1) * width] = dqkv[i]
        for c in range(0, width, TILE):
            pulled = dot_nt(dqkv[0], r.wa[c : c + TILE, 0:width])
            for i in range(1, 3):
                pulled = pulled + dot_nt(
                    dqkv[i], r.wa[c : c + TILE, i * width : (i + 1) * width]
                )
            r.t[:, c : c + TILE] = pulled

        def after_attention(span, half, dh):
            r.gin[mb, span, :] = dh.astype(low)

        norm_backward(mb, 1, r.n1, r.r1, r.m, after_attention)
        return carry

    lax.fori_loop(0, micro, backward_job, 0)

    if fused:
        gradient_tail(r, section, z_at, core, member, remote, spread, await_block)

    for half in range(halves):
        for job in range(2 * micro):

            @pl.when(jnp.logical_or(jnp.logical_not(is_last), job < micro))
            def _():
                forward_copy(job, job, half).wait_send()

        for job in range(micro):

            @pl.when(jnp.logical_not(is_first))
            def _():
                backward_copy(job, half).wait_send()


def gradient_tail(r, section, z_at, core, member, remote, spread, await_block):
    micro, rows, width = r.x.shape
    ff = r.win.shape[1]
    share = width // (DEEP * CORES)
    part = ff // DEEP
    half_part = part // CORES
    other = 1 - core
    partner = (section, z_at * CORES + other)
    qkv_width = 3 * width

    def on_z(z):
        return (section, z * CORES + core)

    for step in (1, -1):

        @pl.when(jnp.logical_and(z_at + step >= 0, z_at + step < DEEP))
        def _():
            pl.semaphore_signal(
                r.free,
                inc=1,
                device_id=on_z(jnp.clip(z_at + step, 0, DEEP - 1)),
                device_id_type=MESH,
            )

    mine = r.ada.at[core, z_at]
    for mb in range(micro):
        sums = r.dmod[mb]
        mine[mb, :, 0:width] = sums.reshape(sums.shape[0] * sums.shape[1], width).astype(low)
        mine[mb, :, width:] = r.feat[mb]

    def ada_copy(away):
        target = lax.rem(z_at + away, DEEP)
        return remote(
            mine, mine, r.adass.at[away - 1], r.adars.at[z_at], (section, target * CORES + core)
        )

    for away in range(1, DEEP):
        ada_copy(away).start()

    def flat(ref):
        block = ref[...]
        return block.reshape(micro * rows, block.shape[-1])

    def share_rows(z, of_core):
        return pl.ds(pl.multiple_of((z * CORES + of_core) * share, share), share)

    def pair_copy(z):
        return remote(
            r.wa.at[share_rows(z, other), :], r.pa.at[z], r.pss.at[z], r.prs.at[z], partner
        )

    a1_t = flat(r.a1).T
    o_t = r.qkvo[:, qkv_width:].T
    dattn = flat(r.dattn)
    both = CORES * share
    for pair in ((0, DEEP - 1), (1, DEEP - 2)):
        a1_rows, o_rows = [
            jnp.concatenate([side[z * both : (z + 1) * both] for z in pair], axis=0)
            for side in (a1_t, o_t)
        ]
        for c in range(0, 4 * width, TILE):
            if c < qkv_width:
                found = dot_nn(a1_rows, r.qkvo[:, c : c + TILE])
            else:
                found = dot_nn(o_rows, dattn[:, c - qkv_width : c - qkv_width + TILE])
            for i, z in enumerate(pair):
                r.wa[z * both : (z + 1) * both, c : c + TILE] = found[
                    i * both : (i + 1) * both
                ].astype(low)
        for z in pair:
            pair_copy(z).start()

    inner = jnp.logical_or(z_at == INNER[0], z_at == INNER[1])
    edge = jnp.where(z_at == INNER[0], 0, DEEP - 1)
    group = 2

    def quarter(turn):
        return jnp.where(turn == 0, edge, z_at)

    def mlp_group(turn, mb, first):
        for step in range(group):

            @pl.when(turn == 0)
            def _():
                await_block(r.a2, r.a2ss, r.a2rs, mb, first + step)
                await_block(r.dy, r.dyss, r.dyrs, mb, first + step)

        tokens = group * rows
        a2 = r.a2[mb, pl.ds(first, group)].reshape(tokens, width)
        dy = r.dy[mb, pl.ds(first, group)].reshape(tokens, width)
        for c in range(0, part, TILE):
            at = pl.ds(pl.multiple_of(quarter(turn) * part + c, TILE), TILE)
            u = dot_nn(a2, r.win[:, at])
            dz = dot_nt(dy, r.wdown[at, :])
            active, slope = gelu_both(u)
            r.z[0:group, :, c : c + TILE] = active.astype(low).reshape(group, rows, TILE)
            r.z[group:, :, c : c + TILE] = (slope * dz).astype(low).reshape(group, rows, TILE)
        z_t = r.z[0:group].reshape(tokens, part).T
        a2_t = a2.T
        for c in range(0, width, TILE):
            r.pdown[:, c : c + TILE] += dot_nn(z_t, dy[:, c : c + TILE])
        for c in range(0, part, TILE):
            up = dot_nn(a2_t, r.z[group:, :, c : c + TILE].reshape(tokens, TILE))
            r.pin[:, c : c + TILE] += up

    def sums(z):
        return r.qkvo.at[z * share : (z + 1) * share, :]

    def sum_pair(z):
        pair_copy(z).wait_recv()
        sums(z)[...] = (r.wa[share_rows(z, core), :].astype(wide) + r.pa[z].astype(wide)).astype(
            low
        )

    def slot_of(z, direction):
        if direction > 0:
            return z - 1
        return DEEP - 1 + z if z < DEEP - 2 else 0

    def slot_ref(z, direction):
        return r.du.at[pl.ds(slot_of(z, direction) * share, share), :]

    def line_copy(z, direction, piece):
        slot = slot_of(z, direction)
        columns = pl.ds(piece * 2 * width, 2 * width)
        return remote(
            sums(z).at[:, columns],
            slot_ref(z, direction).at[:, columns],
            r.lss.at[z, piece],
            r.lrs.at[slot, piece],
            on_z(jnp.clip(z_at + direction, 0, DEEP - 1)),
        )

    def line_pass(z, direction, at, piece):
        @pl.when(z_at == at)
        def _():
            line_copy(z, direction, piece).wait_recv()
            columns = slice(piece * 2 * width, (piece + 1) * 2 * width)
            sums(z)[:, columns] = (
                sums(z)[:, columns].astype(wide)
                + slot_ref(z, direction)[:, columns].astype(wide)
            ).astype(low)
            line_copy(z, direction, piece).start()

    for at in range(DEEP):

        @pl.when(z_at == at)
        def _():
            pl.semaphore_wait(r.free, (at > 0) + (at < DEEP - 1))

    far_first = (0, DEEP - 1, 1, DEEP - 2)

    @pl.when(jnp.logical_not(inner))
    def _():
        for z in far_first:
            sum_pair(z)

        def queue(direction):
            order = [(z, piece) for z in (3, 2, 1) for piece in range(2)]
            if direction < 0:
                order = [(DEEP - 1 - z, piece) for z, piece in order]
            for i, (z, piece) in enumerate(order):
                if i >= 2:
                    before, half = order[i - 2]
                    line_copy(before, direction, half).wait_send()
                line_copy(z, direction, piece).start()

        @pl.when(z_at == 0)
        def _():
            queue(1)

        @pl.when(z_at == DEEP - 1)
        def _():
            queue(-1)

    pl.semaphore_wait(r.done, 1)

    def staged(kind, turn):
        return pl.ds((kind * 2 + turn) * part, part)

    def landing(turn):
        return r.frecv if turn == 0 else r.land2

    def down_copy(turn):
        return remote(
            (r.n1, r.n2)[turn].at[pl.ds(0, half_part), :],
            landing(turn).at[pl.ds(DEEP * share, half_part), :],
            r.mss.at[turn, DEEP],
            r.mrs.at[turn, DEEP],
            partner,
        )

    def up_copy(turn, z):
        return remote(
            r.pa.at[z, :, staged(0, turn)],
            landing(turn).at[pl.ds(z * share, share), :],
            r.mss.at[turn, z],
            r.mrs.at[turn, z],
            partner,
        )

    def column_copy(turn, z):
        return remote(
            r.pa.at[z, :, staged(1, turn)],
            r.land.at[quarter(turn)],
            r.css.at[turn, z],
            r.crs.at[quarter(turn)],
            on_z(z),
        )

    def edge_copy():
        return remote(
            r.slice, r.frecv.at[pl.ds(0, half_part), :], r.ess.at[0], r.ers.at[0], on_z(edge)
        )

    def half_rows_of(which):
        return pl.ds(pl.multiple_of(which * half_part, half_part), half_part)

    def down_rows(z):
        return pl.ds(pl.multiple_of(core * half_part + z * share, share), share)

    def exchange(turn):
        for z in range(DEEP):
            r.pa[z, :, staged(0, turn)] = r.pin[share_rows(z, other), :].astype(low)
            up_copy(turn, z).start()
        (r.n1, r.n2)[turn][0:half_part, :] = r.pdown[half_rows_of(other), :].astype(low)
        down_copy(turn).start()
        for z in range(DEEP):
            r.wa[share_rows(z, core), 0:part] = r.pin[share_rows(z, core), :].astype(low)
            r.wa[share_rows(z, core), part : 2 * part] = r.pdown[down_rows(z), :].astype(low)

    def finish_quarter(turn):
        for z in range(DEEP):
            up_copy(turn, z).wait_recv()
            arrived = landing(turn)[z * share : (z + 1) * share, :].astype(wide)
            total = r.wa[share_rows(z, core), 0:part].astype(wide) + arrived

            @pl.when(z_at == z)
            def _():
                to = pl.ds(pl.multiple_of(quarter(turn) * part, part), part)
                r.g_up[:, to] = total

            @pl.when(z_at != z)
            def _():
                r.pa[z, :, staged(1, turn)] = total.astype(low)
                column_copy(turn, z).start()

        down_copy(turn).wait_recv()
        for z in range(DEEP):
            arrived = landing(turn)[(DEEP + z) * share : (DEEP + z + 1) * share, :].astype(wide)
            total = r.wa[share_rows(z, core), part : 2 * part].astype(wide) + arrived
            if turn == 0:
                r.slice[z * share : (z + 1) * share, :] = total.astype(low)
            else:
                r.g_down[z * share : (z + 1) * share, :] = total
        if turn == 0:
            edge_copy().start()

    def clear():
        r.pdown[...] = jnp.zeros_like(r.pdown)
        r.pin[...] = jnp.zeros_like(r.pin)

    groups = micro * DEEP // group

    def group_step(step, carry):
        turn = lax.div(step, groups)
        at = lax.rem(step, groups)

        @pl.when(step == DEEP // group)
        def _():
            for z in far_first:
                sum_pair(z)

        @pl.when(step == groups)
        def _():
            exchange(0)
            clear()
            line_pass(3, 1, 1, 0)
            line_pass(0, -1, 2, 0)

        @pl.when(step == groups + 1)
        def _():
            finish_quarter(0)
            line_pass(3, 1, 1, 1)
            line_pass(0, -1, 2, 1)

        @pl.when(step == groups + 2)
        def _():
            line_pass(3, 1, 2, 0)
            line_pass(0, -1, 1, 0)
            line_pass(2, 1, 1, 0)
            line_pass(1, -1, 2, 0)

        @pl.when(step == groups + 3)
        def _():
            line_pass(3, 1, 2, 1)
            line_pass(0, -1, 1, 1)
            line_pass(2, 1, 1, 1)
            line_pass(1, -1, 2, 1)

        place = lax.rem(at, DEEP // group) * group
        mlp_group(turn, lax.div(at, DEEP // group), jnp.where(z_at == INNER[0], place, group - place))
        return carry

    @pl.when(inner)
    def _():
        clear()
        lax.fori_loop(0, 2 * groups, group_step, 0)
        exchange(1)

    def ada_pair():
        return remote(
            r.ada.at[core], r.ada.at[core], r.adass.at[DEEP - 1], r.adars.at[DEEP], partner
        )

    def ada_other():
        return remote(
            r.ada.at[other], r.ada.at[other], r.adass.at[DEEP - 1], r.adars.at[DEEP], partner
        )

    for z in range(DEEP):

        @pl.when(z_at != z)
        def _():
            remote(
                r.ada.at[core, z], r.ada.at[core, z], r.adass.at[0], r.adars.at[z], partner
            ).wait_recv()

    ada_pair().start()

    ada_other().wait_recv()
    entries = CORES * DEEP * micro * r.feat.shape[1]
    ada_rows = TEMB // (DEEP * CORES)
    pick = lax.broadcasted_iota(jnp.int32, (ada_rows, TEMB), 1) == (
        lax.broadcasted_iota(jnp.int32, (ada_rows, TEMB), 0) + member * ada_rows
    )
    features = r.ada[:, :, :, :, width:].reshape(entries, TEMB)
    gathered = r.ada[:, :, :, :, 0:width].reshape(entries, width)
    spreads = dot_nt(pick.astype(wide).astype(low), features)
    which = lax.rem(lax.broadcasted_iota(jnp.int32, (ada_rows, entries), 1), 8)
    for k in range(6):
        chosen = jnp.where(which == k, spreads, 0.0).astype(low)
        r.g_ada[:, k * width : (k + 1) * width] = dot_nn(chosen, gathered)

    @pl.when(inner)
    def _():
        finish_quarter(1)

    def finish(z):
        for piece in range(2):
            if z > 0:
                line_copy(z, 1, piece).wait_recv()
            if z < DEEP - 1:
                line_copy(z, -1, piece).wait_recv()
        total = sums(z)[...].astype(wide)
        if z > 0:
            total = total + slot_ref(z, 1)[...].astype(wide)
        if z < DEEP - 1:
            total = total + slot_ref(z, -1)[...].astype(wide)
        r.g_qkv[...] = total[:, 0:qkv_width]
        r.g_out[...] = total[:, qkv_width:]

    for z in range(DEEP):

        @pl.when(z_at == z)
        def _():
            finish(z)

    for q in range(DEEP):

        @pl.when(z_at != INNER[q // 2])
        def _():
            remote(
                r.pa.at[0, :, staged(1, 0)], r.land.at[q], r.css.at[0, 0], r.crs.at[q], partner
            ).wait_recv()
            r.g_up[:, q * part : (q + 1) * part] = r.land[q].astype(wide)

    @pl.when(jnp.logical_not(inner))
    def _():
        edge_copy().wait_recv()
        r.g_down[...] = r.frecv[0:half_part, :].astype(wide)

    for mb in range(micro):
        spread(r.a2, r.a2ss, r.a2rs, mb, True)
        spread(r.dy, r.dyss, r.dyrs, mb, True)
    for away in range(1, DEEP):
        ada_copy(away).wait_send()
    ada_pair().wait_send()
    for z in range(DEEP):
        pair_copy(z).wait_send()

        unsent = inner
        if z in (1, 2):
            unsent = jnp.logical_or(inner, z_at == (0 if z == 1 else DEEP - 1))

        @pl.when(jnp.logical_and(unsent, z_at != z))
        def _():
            for piece in range(2):
                line_copy(z, 1 if z > 0 else -1, piece).wait_send()

    @pl.when(inner)
    def _():
        edge_copy().wait_send()
        for turn in range(2):
            down_copy(turn).wait_send()
            for z in range(DEEP):
                up_copy(turn, z).wait_send()

                @pl.when(z_at != z)
                def _():
                    column_copy(turn, z).wait_send()


def run_chain(x, cot, long_count, timesteps, ada_weight, w_qkv, w_out, w_in, w_down, members):
    micro, rows, width = x.shape
    ff = w_in.shape[1]
    sections = lax.axis_size("section")
    fused = members == DEEP * CORES
    vmem = pl.BlockSpec(memory_space=pltpu.VMEM)
    hbm = pl.BlockSpec(memory_space=pl.ANY)
    dma = pltpu.SemaphoreType.DMA

    def kept(*shape):
        return jax.ShapeDtypeStruct(shape, low)

    def result(*shape):
        return jax.ShapeDtypeStruct(shape, wide)

    halves = rows // SHORT
    smem = pl.BlockSpec(memory_space=pltpu.SMEM)
    names = ["long", "steps", "x", "cot", "ada_h", "wqkv_h", "wout_h", "win_h", "wdown_h"]
    in_specs = [smem] * 2 + [vmem] * 2 + [hbm] * 5
    stored = {
        "dmod": result(micro, halves, 8, width),
        "a1": kept(micro, rows, width),
        "qkvo": kept(micro * rows, 4 * width),
        "dattn": kept(micro, rows, width),
        "a2": kept(micro, DEEP if fused else 1, rows, width),
        "du": kept(micro * rows, ff),
        "z": kept((1 if fused else micro + 1) * (ff // width), rows, width),
        "dy": kept(micro, DEEP if fused else 1, rows, width),
    }
    outs = {"fout": kept(2 * micro, rows, width), "gin": kept(micro, rows, width)}
    share = width // members
    if fused:
        outs["g_qkv"] = result(share, 3 * width)
        outs["g_out"] = result(share, width)
        outs["g_up"] = result(share, ff)
        outs["g_down"] = result(ff // members, width)
        outs["g_ada"] = result(TEMB // members, 6 * width)
    else:
        outs.update(stored)
    scratch = {
        "wa": pltpu.VMEM((width, 4 * width), low),
        "win": pltpu.VMEM((width, ff), low),
        "wdown": pltpu.VMEM((ff, width), low),
        "mod": pltpu.VMEM((micro, halves, 8, width), wide),
        "tags": pltpu.VMEM((2, micro, rows, 128), low),
        "feat": pltpu.VMEM((micro, 8 * halves, TEMB), low),
        "msem": dma((6,)),
        "h": pltpu.VMEM((rows, width), wide),
        "m": pltpu.VMEM((rows, width), wide),
        "t": pltpu.VMEM((rows, width), wide),
        "do": pltpu.VMEM((rows, width), low),
        "n1": pltpu.VMEM((micro * rows, width), low),
        "n2": pltpu.VMEM((micro * rows, width), low),
        "r1": pltpu.VMEM((micro, rows, 1), wide),
        "r2": pltpu.VMEM((micro, rows, 1), wide),
        "y": pltpu.VMEM((micro, rows, width), low),
        "frecv": pltpu.VMEM((2 * micro * rows, width), low),
        "brecv": pltpu.VMEM((micro, rows, width), low),
        "wsem": dma((4,)),
        "fss": dma((2 * micro, rows // SHORT)),
        "frs": dma((2 * micro, rows // SHORT)),
        "bss": dma((micro, rows // SHORT)),
        "brs": dma((micro, rows // SHORT)),
    }
    if fused:
        part = ff // DEEP
        for name, value in stored.items():
            scratch[name] = pltpu.VMEM(value.shape, value.dtype)
        scratch.update(
            {
                "pa": pltpu.VMEM((DEEP, share, 4 * width), low),
                "pdown": pltpu.VMEM((part, width), wide),
                "pin": pltpu.VMEM((width, part), wide),
                "land2": pltpu.VMEM((DEEP * share + part // CORES, part), low),
                "slice": pltpu.VMEM((part // CORES, width), low),
                "land": pltpu.VMEM((DEEP, share, part), low),
                "ada": pltpu.VMEM((CORES, DEEP, micro, 8 * halves, width + TEMB), low),
                "free": pltpu.SemaphoreType.REGULAR,
                "done": pltpu.SemaphoreType.REGULAR,
                "a2ss": dma((micro, len(INNER))),
                "a2rs": dma((micro, DEEP)),
                "dyss": dma((micro, len(INNER))),
                "dyrs": dma((micro, DEEP)),
                "adass": dma((DEEP,)),
                "adars": dma((DEEP + 1,)),
                "pss": dma((DEEP,)),
                "prs": dma((DEEP,)),
                "lss": dma((DEEP, 2)),
                "lrs": dma((5, 2)),
                "mss": dma((2, DEEP + 1)),
                "mrs": dma((2, DEEP + 1)),
                "ess": dma((1,)),
                "ers": dma((1,)),
                "css": dma((2, DEEP)),
                "crs": dma((DEEP,)),
            }
        )
    names = names + list(outs) + list(scratch)
    values = pl.pallas_call(
        functools.partial(chain_kernel, names, sections, fused),
        out_shape=tuple(outs.values()),
        in_specs=in_specs,
        out_specs=(vmem,) * len(outs),
        scratch_shapes=list(scratch.values()),
        compiler_params=pltpu.CompilerParams(
            collective_id=0, has_side_effects=True, vmem_limit_bytes=60 * 1024 * 1024
        ),
    )(long_count, timesteps, x, cot, ada_weight, w_qkv, w_out, w_in, w_down)
    return SimpleNamespace(**dict(zip(outs, values)))


def time_features(timestep_ids):
    half_width = TEMB // 2
    frequency = jnp.exp(-math.log(10000.0) * jnp.arange(half_width, dtype=wide) / half_width)
    angles = timestep_ids.astype(wide)[:, None] * 0.1 * frequency[None, :]
    return jnp.concatenate([jnp.sin(angles), jnp.cos(angles)], axis=1)


def summed_apart(kept, features, micro, rows, width):
    def product(left, right):
        left = left.reshape(micro * rows, -1)
        right = right.reshape(micro * rows, -1)
        partial = dot_tn(left, right).astype(low)
        return lax.psum_scatter(partial, "dp", scatter_dimension=0, tiled=True).astype(wide)

    sums = kept.dmod[:, :, :6].reshape(features.shape[0], 6 * width)
    features_all = lax.all_gather(features.astype(wide), "dp", tiled=True)
    sums_all = lax.all_gather(sums, "dp", tiled=True)
    share = TEMB // lax.axis_size("dp")
    mine = lax.dynamic_slice_in_dim(features_all, lax.axis_index("dp") * share, share, 1)
    grad_ada = lax.dot_general(
        mine, sums_all, (((0,), (0,)), ((), ())), precision=lax.Precision.HIGHEST
    )
    return (
        product(kept.a1, kept.qkvo[:, : 3 * width]),
        product(kept.qkvo[:, 3 * width :], kept.dattn),
        product(kept.a2, kept.du),
        product(jnp.swapaxes(kept.z.reshape(micro + 1, -1, rows, width)[:micro], 1, 2), kept.dy),
        grad_ada,
    )


def on_device(inputs, cotangent, long_count, timesteps, w_qkv, w_out, w_in, w_down, ada_weight):
    micro = long_count.shape[1]
    width = inputs.shape[1]
    rows = inputs.shape[0] // micro
    halves = rows // SHORT
    members = lax.axis_size("dp")
    kept = run_chain(
        inputs.reshape(micro, rows, width),
        cotangent.reshape(micro, rows, width),
        long_count,
        timesteps,
        ada_weight[0],
        w_qkv[0],
        w_out[0],
        w_in[0],
        w_down[0],
        members,
    )
    if members == DEEP * CORES:
        hidden, grad_in, *grads = handed_over(
            (kept.fout, kept.gin, kept.g_qkv, kept.g_out, kept.g_up, kept.g_down, kept.g_ada)
        )
    else:
        is_long = (long_count[0] == 1)[:, None]
        half_steps = jnp.where(is_long, timesteps[0][:, :1], timesteps[0][:, :halves])
        features = time_features(half_steps.reshape(-1)).astype(low)
        grads = summed_apart(kept, features, micro, rows, width)
        hidden, grad_in = kept.fout[micro:], kept.gin
    hidden_out = hidden.reshape(1, micro * rows, width)
    grad_in = grad_in.reshape(1, micro * rows, width)
    return (hidden_out, grad_in) + tuple(grad[None] for grad in grads)


def handed_over(results):
    micro = results[1].shape[0]

    def kernel(*refs):
        count = len(results)
        sources, targets, holds = [refs[i * count : (i + 1) * count] for i in range(3)]
        sems = refs[-1]
        arrivals, departures = [], []
        for i in range(count):
            source = sources[i].at[pl.ds(micro, micro)] if i == 0 else sources[i]
            arrivals.append(pltpu.make_async_copy(source, holds[i], sems.at[0, i]))
            departures.append(pltpu.make_async_copy(holds[i], targets[i], sems.at[1, i]))
            arrivals[i].start()
        for i in range(count):
            arrivals[i].wait()
            departures[i].start()
        for copy in departures:
            copy.wait()

    shapes = [jax.ShapeDtypeStruct(value.shape, value.dtype) for value in results]
    shapes[0] = jax.ShapeDtypeStruct((micro,) + results[0].shape[1:], results[0].dtype)
    anywhere = pl.BlockSpec(memory_space=pl.ANY)
    return pl.pallas_call(
        kernel,
        out_shape=tuple(shapes),
        in_specs=[anywhere] * len(results),
        out_specs=[anywhere] * len(results),
        scratch_shapes=[pltpu.VMEM(shape.shape, shape.dtype) for shape in shapes]
        + [pltpu.SemaphoreType.DMA((2, len(results)))],
        compiler_params=pltpu.CompilerParams(vmem_limit_bytes=60 * 1024 * 1024),
    )(*results)


def solution(mesh):
    placed = (
        P("dp", None),
        P("dp", None),
        P("dp", None),
        P("dp", None, None),
        P("section", None, None),
        P("section", None, None),
        P("section", None, None),
        P("section", None, None),
        P("section", None, None),
    )
    return jax.shard_map(
        on_device,
        mesh=mesh,
        in_specs=placed,
        out_specs=(P("section", "dp", None),) * 7,
        check_vma=False,
    )
```

```python
import functools
import math
from types import SimpleNamespace

import jax
import jax.numpy as jnp
from jax import lax
from jax.experimental import pallas as pl
from jax.experimental.pallas import tpu as pltpu
from jax.sharding import PartitionSpec as P

HEADS = 12
TEMB = 128
SHORT = 128
TILE = 256
CHUNK = 32
CORES = 2
DEEP = 4
INNER = (1, 2)
norm_eps = 1e-06
MESH = pl.DeviceIdType.MESH
low = jnp.bfloat16
wide = jnp.float32


def dot_nn(a, b):
    return lax.dot_general(a, b, (((1,), (0,)), ((), ())), preferred_element_type=wide)


def dot_nt(a, b):
    return lax.dot_general(a, b, (((1,), (1,)), ((), ())), preferred_element_type=wide)


def dot_tn(a, b):
    return lax.dot_general(a, b, (((0,), (0,)), ((), ())), preferred_element_type=wide)


def fold(block):
    total = block[0:8]
    for start in range(8, block.shape[0], 8):
        total = total + block[start : start + 8]
    return total


GELU_C = math.sqrt(2.0 / math.pi)


def gelu(u):
    t = jnp.tanh(GELU_C * (u + 0.044715 * (u * u * u)))
    return 0.5 * u * (1.0 + t)


def gelu_both(u):
    square = u * u
    t = jnp.tanh(GELU_C * (u + 0.044715 * (square * u)))
    outer = 0.5 * (1.0 + t)
    slope = outer + 0.5 * u * (1.0 - t * t) * (GELU_C * (1.0 + (3.0 * 0.044715) * square))
    return u * outer, slope


def chain_kernel(names, sections, fused, *refs):
    r = SimpleNamespace(**dict(zip(names, refs)))
    micro, rows, width = r.x.shape
    ff = r.win.shape[1]
    qkv_width = 3 * width
    half_rows = SHORT

    def half_chunks(half):
        return range(half * half_rows, (half + 1) * half_rows, CHUNK)

    halves = rows // half_rows
    section = lax.axis_index("section")
    member = lax.axis_index("dp")
    z_at = lax.div(member, CORES)
    core = lax.rem(member, CORES)
    own = z_at if fused else 0
    right = lax.rem(section + 1, sections)
    left = lax.rem(section + sections - 1, sections)
    is_first = section == 0
    is_last = section == sections - 1

    maps = []
    for k in range(6):
        spot = pl.ds(k % 2 * TEMB, TEMB)
        copy = pltpu.make_async_copy(
            r.ada_h.at[:, pl.ds(k * width, width)], r.z.at[k // 2, spot, :], r.msem.at[k]
        )
        copy.start()
        maps.append(copy)

    loads = []
    for index, (hbm, vmem) in enumerate(
        (
            (r.wqkv_h, r.wa.at[:, 0:qkv_width]),
            (r.wout_h, r.wa.at[:, qkv_width:]),
            (r.win_h, r.win),
            (r.wdown_h, r.wdown),
        )
    ):
        loads.append(pltpu.make_async_copy(hbm, vmem, r.wsem.at[index]))
        if index == 0:
            loads[index].start()

    barrier = pltpu.get_barrier_semaphore()
    partner = (section, z_at * CORES + 1 - core)
    greeted = [(left, member), (right, member), partner]
    if fused:
        for away in range(1, DEEP):
            greeted.append((section, lax.rem(z_at + away, DEEP) * CORES + core))
    for target in greeted:
        pl.semaphore_signal(barrier, inc=1, device_id=target, device_id_type=MESH)
    pl.semaphore_wait(barrier, len(greeted))

    def remote(src, dst, send_sem, recv_sem, target):
        return pltpu.make_async_remote_copy(
            src_ref=src,
            dst_ref=dst,
            send_sem=send_sem,
            recv_sem=recv_sem,
            device_id=target,
            device_id_type=MESH,
        )

    def forward_copy(job, slot, half):
        span = pl.ds(half * half_rows, half_rows)
        landing = pl.ds(
            pl.multiple_of(slot * rows + half * half_rows, half_rows), half_rows
        )
        return remote(
            r.fout.at[job, span, :],
            r.frecv.at[landing, :],
            r.fss.at[job, half],
            r.frs.at[slot, half],
            (right, member),
        )

    def backward_copy(job, half):
        span = pl.ds(half * half_rows, half_rows)
        return remote(
            r.gin.at[job, span, :],
            r.brecv.at[job, span, :],
            r.bss.at[job, half],
            r.brs.at[job, half],
            (left, member),
        )

    def mod_row(mb, half, k):
        return r.mod[mb, half, pl.ds(k, 1), :]

    def mb_rows(mb):
        return pl.ds(pl.multiple_of(mb * rows, rows), rows)

    def mb_span(mb, start):
        return pl.ds(pl.multiple_of(mb * rows + start, CHUNK), CHUNK)

    lane = lax.broadcasted_iota(jnp.int32, (1, 128), 1)
    first_lanes = lane < 64
    masks = [first_lanes.astype(wide).astype(low), (1.0 - first_lanes.astype(wide)).astype(low)]
    scale = (width // HEADS) ** (-0.5)
    ones = jnp.ones((rows, 128), low)

    def spread(buffer, send_sems, recv_sems, mb, wait):
        for k, target in enumerate(INNER):

            @pl.when(z_at != target)
            def _():
                copy = remote(
                    buffer.at[mb, z_at],
                    buffer.at[mb, z_at],
                    send_sems.at[mb, k],
                    recv_sems.at[mb, z_at],
                    (section, target * CORES + core),
                )
                copy.wait_send() if wait else copy.start()

    def await_block(buffer, send_sems, recv_sems, mb, source):
        @pl.when(z_at != source)
        def _():
            remote(
                buffer.at[mb, source],
                buffer.at[mb, source],
                send_sems.at[mb, 0],
                recv_sems.at[mb, source],
                (section, member),
            ).wait_recv()

    def norm_forward(src, mb, half, k_shift, k_scale, n_keep, r_keep, out):
        for start in half_chunks(half):
            span = pl.ds(start, CHUNK)
            v = src[span, :]
            centered = v - jnp.mean(v, axis=-1, keepdims=True)
            inverse = lax.rsqrt(jnp.mean(centered * centered, axis=-1, keepdims=True) + norm_eps)
            n = centered * inverse
            n_keep[mb_span(mb, start), :] = n.astype(low)
            r_keep[mb, span, :] = inverse
            out[span, :] = (
                n * (1.0 + mod_row(mb, half, k_scale)) + mod_row(mb, half, k_shift)
            ).astype(low)

    r.dmod[...] = jnp.zeros_like(r.dmod)

    for mb in range(micro):
        long_row = (lane * 0 + r.long[0, mb]).astype(wide)
        for half in range(halves):
            here = (lane == 0).astype(wide)
            there = (lane == half).astype(wide)
            in_slot = long_row * here + (1.0 - long_row) * there
            barred = (lane < halves).astype(wide) * (1.0 - in_slot) * -1e30
            span = pl.ds(half * half_rows, half_rows)
            r.tags[0, mb, span, :] = jnp.broadcast_to(in_slot, (half_rows, 128)).astype(low)
            r.tags[1, mb, span, :] = jnp.broadcast_to(barred, (half_rows, 128)).astype(low)

    pairs = [(mb, half) for mb in range(micro) for half in range(halves)]
    row = lax.broadcasted_iota(jnp.int32, (8 * len(pairs), TEMB), 0)
    steps = jnp.zeros((8 * len(pairs), TEMB), jnp.int32)
    for i, (mb, half) in enumerate(pairs):
        flag = r.long[0, mb]
        chosen = flag * r.steps[0, mb, 0] + (1 - flag) * r.steps[0, mb, half]
        steps = jnp.where(row // 8 == i, chosen, steps)
    feature = lax.broadcasted_iota(jnp.int32, (8 * len(pairs), TEMB), 1)
    half_width = TEMB // 2
    position = lax.rem(feature, half_width).astype(wide)
    angles = steps.astype(wide) * 0.1 * jnp.exp(position * (-math.log(10000.0) / half_width))
    features = jnp.where(feature < half_width, jnp.sin(angles), jnp.cos(angles)).astype(low)
    r.feat[...] = features.reshape(micro, 8 * halves, TEMB)
    for copy in maps:
        copy.wait()
    for copy in loads[1:]:
        copy.start()
    for k in range(6):
        spot = pl.ds(k % 2 * TEMB, TEMB)
        found = dot_nn(features, r.z[k // 2, spot, :])
        for i, (mb, half) in enumerate(pairs):
            r.mod[mb, half, k : k + 1, :] = found[8 * i : 8 * i + 1, :]

    def forward_job(job, carry):
        mb = lax.rem(job, micro)
        here = mb_rows(mb)
        opening = jnp.logical_and(is_first, job == 0)

        @pl.when(jnp.logical_and(opening, core == 0))
        def _():
            pl.semaphore_wait(r.turn, 1)

        z_base = 0 if fused else mb * (ff // width)

        def wait_load(index):
            @pl.when(job == 0)
            def _():
                loads[index].wait()

        for half in range(halves):
            span = pl.ds(half * half_rows, half_rows)
            arrived = pl.ds(
                pl.multiple_of(job * rows + half * half_rows, half_rows), half_rows
            )

            @pl.when(jnp.logical_or(jnp.logical_not(is_first), job >= micro))
            def _():
                forward_copy(job, job, half).wait_recv()

            @pl.when(jnp.logical_and(is_first, job < micro))
            def _():
                r.h[span, :] = r.x[mb, span, :].astype(wide)

            @pl.when(jnp.logical_and(is_first, job >= micro))
            def _():
                r.h[span, :] = r.x[mb, span, :].astype(wide) + r.frecv[arrived, :].astype(wide)

            @pl.when(jnp.logical_not(is_first))
            def _():
                r.h[span, :] = r.frecv[arrived, :].astype(wide)

            norm_forward(r.h, mb, half, 0, 1, r.n1, r.r1, r.a1.at[mb])
            if half == 0:
                wait_load(0)
            a1 = r.a1[mb, span, :]
            to = pl.ds(pl.multiple_of(mb * rows + half * half_rows, half_rows), half_rows)
            for c in range(0, qkv_width, TILE):
                r.qkvo[to, c : c + TILE] = dot_nn(a1, r.wa[:, c : c + TILE]).astype(low)

        q_tag = r.tags[0, mb]
        k_tag = r.tags[1, mb]

        def scores(c):
            q, k, v = [r.qkvo[here, i * width + c : i * width + c + 128] for i in range(3)]
            k_wide = jnp.concatenate([k, k_tag], axis=1)
            found = [
                dot_nt(jnp.concatenate([q * (mask * scale), q_tag], axis=1), k_wide)
                for mask in masks
            ]
            return found, jnp.concatenate([v, ones], axis=1)

        def mix(c, found, v_wide):
            weights = [jnp.exp(s - jnp.max(s, axis=1, keepdims=True)).astype(low) for s in found]
            mixed = [dot_nn(e, v_wide) for e in weights]
            top = jnp.where(first_lanes, mixed[0][:, 0:128], mixed[1][:, 0:128])
            total = jnp.where(first_lanes, mixed[0][:, 128:], mixed[1][:, 128:])
            r.do[:, c : c + 128] = (top * (1.0 / total)).astype(low)

        ahead = scores(0)
        for c in range(0, width, 128):
            current = ahead
            if c + 128 < width:
                ahead = scores(c + 128)
            mix(c, *current)
        @pl.when(jnp.logical_and(opening, core == 1))
        def _():
            pl.semaphore_signal(r.turn, inc=1, device_id=partner, device_id_type=MESH)

        wait_load(1)
        wait_load(2)
        wait_load(3)
        r.qkvo[here, qkv_width:] = r.do[...]
        for half in range(halves):
            span = pl.ds(half * half_rows, half_rows)
            to = pl.ds(pl.multiple_of(mb * rows + half * half_rows, half_rows), half_rows)
            o = r.do[span, :]
            for c in range(0, width, TILE):
                r.t[span, c : c + TILE] = dot_nn(o, r.wa[:, qkv_width + c : qkv_width + c + TILE])
            for start in half_chunks(half):
                part = pl.ds(start, CHUNK)
                attn = r.t[part, :]
                r.dattn[mb, part, :] = attn.astype(low)
                r.m[part, :] = r.h[part, :] + mod_row(mb, half, 2) * attn
            norm_forward(r.m, mb, half, 3, 4, r.n2, r.r2, r.a2.at[mb, own])
            a2 = r.a2[mb, own, span, :]
            for c in range(0, ff, TILE):
                u = dot_nn(a2, r.win[:, c : c + TILE])
                r.du[to, c : c + TILE] = u.astype(low)
                at = c % width
                r.z[z_base + c // width, span, at : at + TILE] = gelu(u).astype(low)
            z = [r.z[z_base + i, span, :] for i in range(ff // width)]
            for c in range(0, width, TILE):
                y = dot_nn(z[0], r.wdown[0:width, c : c + TILE])
                for i in range(1, ff // width):
                    y = y + dot_nn(z[i], r.wdown[i * width : (i + 1) * width, c : c + TILE])
                r.t[span, c : c + TILE] = y
            for start in half_chunks(half):
                part = pl.ds(start, CHUNK)
                y = r.t[part, :]
                r.y[mb, part, :] = y.astype(low)
                r.fout[job, part, :] = (r.m[part, :] + mod_row(mb, half, 5) * y).astype(low)

            @pl.when(jnp.logical_or(jnp.logical_not(is_last), job < micro))
            def _():
                forward_copy(job, jnp.where(is_last, job + micro, job), half).start()


        if fused:

            @pl.when(job >= micro)
            def _():
                spread(r.a2, r.a2ss, r.a2rs, mb, False)

        return carry

    lax.fori_loop(0, 2 * micro, forward_job, 0)
    if fused:
        pl.semaphore_signal(
            r.done,
            inc=1,
            device_id=partner,
            device_id_type=MESH,
        )

    def norm_backward(mb, k_scale, n_keep, r_keep, base, per_chunk):
        for half in range(halves):
            shift_sum = jnp.zeros((8, width), wide)
            scale_sum = jnp.zeros((8, width), wide)
            gate_sum = jnp.zeros((8, width), wide)
            for start in half_chunks(half):
                span = pl.ds(start, CHUNK)
                da = r.t[span, :]
                n = n_keep[mb_span(mb, start), :].astype(wide)
                inverse = r_keep[mb, span, :]
                shift_sum = shift_sum + fold(da)
                scale_sum = scale_sum + fold(da * n)
                dn = da * (1.0 + mod_row(mb, half, k_scale))
                dv = inverse * (
                    dn
                    - jnp.mean(dn, axis=-1, keepdims=True)
                    - n * jnp.mean(dn * n, axis=-1, keepdims=True)
                )
                extra = per_chunk(span, half, base[span, :] + dv)
                if extra is not None:
                    gate_sum = gate_sum + fold(extra)
            r.dmod[mb, half, k_scale - 1, :] = jnp.sum(shift_sum, axis=0)
            r.dmod[mb, half, k_scale, :] = jnp.sum(scale_sum, axis=0)
            if k_scale == 4:
                r.dmod[mb, half, 2, :] = jnp.sum(gate_sum, axis=0)
            else:

                @pl.when(jnp.logical_not(is_first))
                def _():
                    backward_copy(mb, half).start()

    def backward_job(mb, carry):
        g_s = r.h
        here = mb_rows(mb)
        z_base = 0 if fused else micro * (ff // width)

        for half in range(halves):
            rows_of = pl.ds(half * half_rows, half_rows)

            @pl.when(is_last)
            def _():
                g_s[rows_of, :] = r.cot[mb, rows_of, :].astype(wide)

            @pl.when(jnp.logical_not(is_last))
            def _():
                backward_copy(mb, half).wait_recv()
                g_s[rows_of, :] = r.brecv[mb, rows_of, :].astype(wide)

            gate_sum = jnp.zeros((8, width), wide)
            for start in half_chunks(half):
                span = pl.ds(start, CHUNK)
                g = g_s[span, :]
                gate_sum = gate_sum + fold(g * r.y[mb, span, :].astype(wide))
                r.dy[mb, own, span, :] = (mod_row(mb, half, 5) * g).astype(low)
            r.dmod[mb, half, 5, :] = jnp.sum(gate_sum, axis=0)
        if fused:
            spread(r.dy, r.dyss, r.dyrs, mb, False)
        dy = r.dy[mb, own]
        for c in range(0, ff, TILE):
            dz = dot_nt(dy, r.wdown[c : c + TILE, :])
            u = r.du[mb_rows(mb), c : c + TILE].astype(wide)
            r.du[mb_rows(mb), c : c + TILE] = (gelu_both(u)[1] * dz).astype(low)
        du = r.du[mb_rows(mb), :]
        for c in range(0, width, TILE):
            r.t[:, c : c + TILE] = dot_nt(du, r.win[c : c + TILE, :])

        def after_mlp(span, half, dm):
            r.m[span, :] = dm
            extra = dm * r.dattn[mb, span, :].astype(wide)
            r.dattn[mb, span, :] = (mod_row(mb, half, 2) * dm).astype(low)
            return extra

        norm_backward(mb, 4, r.n2, r.r2, g_s, after_mlp)
        dattn = r.dattn[mb]
        for c in range(0, width, TILE):
            r.do[:, c : c + TILE] = dot_nt(dattn, r.wa[c : c + TILE, qkv_width:]).astype(low)
        q_tag = r.tags[0, mb]
        k_tag = r.tags[1, mb]

        def pulls(c):
            q, k, v = [r.qkvo[here, i * width + c : i * width + c + 128] for i in range(3)]
            do = r.do[:, c : c + 128]
            k_wide = jnp.concatenate([k, k_tag], axis=1)
            found = []
            for mask in masks:
                s = dot_nt(k_wide, jnp.concatenate([q * (mask * scale), q_tag], axis=1))
                found.append((s, dot_nt(v * mask, do)))
            return found, q, k, do

        def push(c, found, q, k, do):
            parts = []
            for s, dp in found:
                e = jnp.exp(s - jnp.max(s, axis=0, keepdims=True))
                p = e * (1.0 / jnp.sum(e, axis=0, keepdims=True))
                inner = jnp.sum(p * dp, axis=0, keepdims=True)
                ds = (p * (dp - inner)).astype(low)
                parts.append((dot_tn(ds, k), dot_nn(ds, q), dot_nn(p.astype(low), do)))
            for i, factor in enumerate((scale, scale, 1.0)):
                both = jnp.where(first_lanes, parts[0][i], parts[1][i])
                r.z[z_base + i, :, c : c + 128] = (both * factor).astype(low)

        ahead = pulls(0)
        for c in range(0, width, 128):
            current = ahead
            if c + 128 < width:
                ahead = pulls(c + 128)
            push(c, *current)
        dqkv = [r.z[z_base + i] for i in range(3)]
        for i in range(3):
            r.qkvo[here, i * width : (i + 1) * width] = dqkv[i]
        for c in range(0, width, TILE):
            pulled = dot_nt(dqkv[0], r.wa[c : c + TILE, 0:width])
            for i in range(1, 3):
                pulled = pulled + dot_nt(
                    dqkv[i], r.wa[c : c + TILE, i * width : (i + 1) * width]
                )
            r.t[:, c : c + TILE] = pulled

        def after_attention(span, half, dh):
            r.gin[mb, span, :] = dh.astype(low)

        norm_backward(mb, 1, r.n1, r.r1, r.m, after_attention)
        return carry

    lax.fori_loop(0, micro, backward_job, 0)

    if fused:
        gradient_tail(r, section, z_at, core, member, remote, spread, await_block)

    for half in range(halves):
        for job in range(2 * micro):

            @pl.when(jnp.logical_or(jnp.logical_not(is_last), job < micro))
            def _():
                forward_copy(job, job, half).wait_send()

        for job in range(micro):

            @pl.when(jnp.logical_not(is_first))
            def _():
                backward_copy(job, half).wait_send()


def gradient_tail(r, section, z_at, core, member, remote, spread, await_block):
    micro, rows, width = r.x.shape
    ff = r.win.shape[1]
    share = width // (DEEP * CORES)
    part = ff // DEEP
    half_part = part // CORES
    other = 1 - core
    partner = (section, z_at * CORES + other)
    qkv_width = 3 * width

    def on_z(z):
        return (section, z * CORES + core)

    for step in (1, -1):

        @pl.when(jnp.logical_and(z_at + step >= 0, z_at + step < DEEP))
        def _():
            pl.semaphore_signal(
                r.free,
                inc=1,
                device_id=on_z(jnp.clip(z_at + step, 0, DEEP - 1)),
                device_id_type=MESH,
            )

    mine = r.ada.at[core, z_at]
    for mb in range(micro):
        sums = r.dmod[mb]
        mine[mb, :, 0:width] = sums.reshape(sums.shape[0] * sums.shape[1], width).astype(low)
        mine[mb, :, width:] = r.feat[mb]

    def ada_copy(away):
        target = lax.rem(z_at + away, DEEP)
        return remote(
            mine, mine, r.adass.at[away - 1], r.adars.at[z_at], (section, target * CORES + core)
        )

    for away in range(1, DEEP):
        ada_copy(away).start()

    def flat(ref):
        block = ref[...]
        return block.reshape(micro * rows, block.shape[-1])

    def share_rows(z, of_core):
        return pl.ds(pl.multiple_of((z * CORES + of_core) * share, share), share)

    def pair_copy(z):
        return remote(
            r.wa.at[share_rows(z, other), :], r.pa.at[z], r.pss.at[z], r.prs.at[z], partner
        )

    a1_t = flat(r.a1).T
    o_t = r.qkvo[:, qkv_width:].T
    dattn = flat(r.dattn)
    both = CORES * share
    for pair in ((0, DEEP - 1), (1, DEEP - 2)):
        a1_rows, o_rows = [
            jnp.concatenate([side[z * both : (z + 1) * both] for z in pair], axis=0)
            for side in (a1_t, o_t)
        ]
        for c in range(0, 4 * width, TILE):
            if c < qkv_width:
                found = dot_nn(a1_rows, r.qkvo[:, c : c + TILE])
            else:
                found = dot_nn(o_rows, dattn[:, c - qkv_width : c - qkv_width + TILE])
            for i, z in enumerate(pair):
                r.wa[z * both : (z + 1) * both, c : c + TILE] = found[
                    i * both : (i + 1) * both
                ].astype(low)
        for z in pair:
            pair_copy(z).start()

    inner = jnp.logical_or(z_at == INNER[0], z_at == INNER[1])
    edge = jnp.where(z_at == INNER[0], 0, DEEP - 1)
    group = 2

    def quarter(turn):
        return jnp.where(turn == 0, edge, z_at)

    def mlp_group(turn, mb, first):
        for step in range(group):

            @pl.when(turn == 0)
            def _():
                await_block(r.a2, r.a2ss, r.a2rs, mb, first + step)
                await_block(r.dy, r.dyss, r.dyrs, mb, first + step)

        tokens = group * rows
        a2 = r.a2[mb, pl.ds(first, group)].reshape(tokens, width)
        dy = r.dy[mb, pl.ds(first, group)].reshape(tokens, width)
        for c in range(0, part, TILE):
            at = pl.ds(pl.multiple_of(quarter(turn) * part + c, TILE), TILE)
            u = dot_nn(a2, r.win[:, at])
            dz = dot_nt(dy, r.wdown[at, :])
            active, slope = gelu_both(u)
            r.z[0:group, :, c : c + TILE] = active.astype(low).reshape(group, rows, TILE)
            r.z[group:, :, c : c + TILE] = (slope * dz).astype(low).reshape(group, rows, TILE)
        z_t = r.z[0:group].reshape(tokens, part).T
        a2_t = a2.T
        for c in range(0, width, TILE):
            r.pdown[:, c : c + TILE] += dot_nn(z_t, dy[:, c : c + TILE])
        for c in range(0, part, TILE):
            up = dot_nn(a2_t, r.z[group:, :, c : c + TILE].reshape(tokens, TILE))
            r.pin[:, c : c + TILE] += up

    def sums(z):
        return r.qkvo.at[z * share : (z + 1) * share, :]

    def sum_pair(z):
        pair_copy(z).wait_recv()
        sums(z)[...] = (r.wa[share_rows(z, core), :].astype(wide) + r.pa[z].astype(wide)).astype(
            low
        )

    def slot_of(z, direction):
        if direction > 0:
            return z - 1
        return DEEP - 1 + z if z < DEEP - 2 else 0

    def slot_ref(z, direction):
        return r.du.at[pl.ds(slot_of(z, direction) * share, share), :]

    def line_copy(z, direction, piece):
        slot = slot_of(z, direction)
        columns = pl.ds(piece * 2 * width, 2 * width)
        return remote(
            sums(z).at[:, columns],
            slot_ref(z, direction).at[:, columns],
            r.lss.at[z, piece],
            r.lrs.at[slot, piece],
            on_z(jnp.clip(z_at + direction, 0, DEEP - 1)),
        )

    def line_pass(z, direction, at, piece):
        @pl.when(z_at == at)
        def _():
            line_copy(z, direction, piece).wait_recv()
            columns = slice(piece * 2 * width, (piece + 1) * 2 * width)
            sums(z)[:, columns] = (
                sums(z)[:, columns].astype(wide)
                + slot_ref(z, direction)[:, columns].astype(wide)
            ).astype(low)
            line_copy(z, direction, piece).start()

    for at in range(DEEP):

        @pl.when(z_at == at)
        def _():
            pl.semaphore_wait(r.free, (at > 0) + (at < DEEP - 1))

    far_first = (0, DEEP - 1, 1, DEEP - 2)

    @pl.when(jnp.logical_not(inner))
    def _():
        for z in far_first:
            sum_pair(z)

        def queue(direction):
            order = [(z, piece) for z in (3, 2, 1) for piece in range(2)]
            if direction < 0:
                order = [(DEEP - 1 - z, piece) for z, piece in order]
            for i, (z, piece) in enumerate(order):
                if i >= 2:
                    before, half = order[i - 2]
                    line_copy(before, direction, half).wait_send()
                line_copy(z, direction, piece).start()

        @pl.when(z_at == 0)
        def _():
            queue(1)

        @pl.when(z_at == DEEP - 1)
        def _():
            queue(-1)

    pl.semaphore_wait(r.done, 1)

    def staged(kind, turn):
        return pl.ds((kind * 2 + turn) * part, part)

    def landing(turn):
        return r.frecv if turn == 0 else r.land2

    def down_copy(turn):
        return remote(
            (r.n1, r.n2)[turn].at[pl.ds(0, half_part), :],
            landing(turn).at[pl.ds(DEEP * share, half_part), :],
            r.mss.at[turn, DEEP],
            r.mrs.at[turn, DEEP],
            partner,
        )

    def up_copy(turn, z):
        return remote(
            r.pa.at[z, :, staged(0, turn)],
            landing(turn).at[pl.ds(z * share, share), :],
            r.mss.at[turn, z],
            r.mrs.at[turn, z],
            partner,
        )

    def column_copy(turn, z):
        return remote(
            r.pa.at[z, :, staged(1, turn)],
            r.land.at[quarter(turn)],
            r.css.at[turn, z],
            r.crs.at[quarter(turn)],
            on_z(z),
        )

    def edge_copy():
        return remote(
            r.slice, r.frecv.at[pl.ds(0, half_part), :], r.ess.at[0], r.ers.at[0], on_z(edge)
        )

    def half_rows_of(which):
        return pl.ds(pl.multiple_of(which * half_part, half_part), half_part)

    def down_rows(z):
        return pl.ds(pl.multiple_of(core * half_part + z * share, share), share)

    def exchange(turn):
        for z in range(DEEP):
            r.pa[z, :, staged(0, turn)] = r.pin[share_rows(z, other), :].astype(low)
            up_copy(turn, z).start()
        (r.n1, r.n2)[turn][0:half_part, :] = r.pdown[half_rows_of(other), :].astype(low)
        down_copy(turn).start()
        for z in range(DEEP):
            r.wa[share_rows(z, core), 0:part] = r.pin[share_rows(z, core), :].astype(low)
            r.wa[share_rows(z, core), part : 2 * part] = r.pdown[down_rows(z), :].astype(low)

    def finish_quarter(turn):
        for z in range(DEEP):
            up_copy(turn, z).wait_recv()
            arrived = landing(turn)[z * share : (z + 1) * share, :].astype(wide)
            total = r.wa[share_rows(z, core), 0:part].astype(wide) + arrived

            @pl.when(z_at == z)
            def _():
                to = pl.ds(pl.multiple_of(quarter(turn) * part, part), part)
                r.g_up[:, to] = total

            @pl.when(z_at != z)
            def _():
                r.pa[z, :, staged(1, turn)] = total.astype(low)
                column_copy(turn, z).start()

        down_copy(turn).wait_recv()
        for z in range(DEEP):
            arrived = landing(turn)[(DEEP + z) * share : (DEEP + z + 1) * share, :].astype(wide)
            total = r.wa[share_rows(z, core), part : 2 * part].astype(wide) + arrived
            if turn == 0:
                r.slice[z * share : (z + 1) * share, :] = total.astype(low)
            else:
                r.g_down[z * share : (z + 1) * share, :] = total
        if turn == 0:
            edge_copy().start()

    def clear():
        r.pdown[...] = jnp.zeros_like(r.pdown)
        r.pin[...] = jnp.zeros_like(r.pin)

    groups = micro * DEEP // group

    def group_step(step, carry):
        turn = lax.div(step, groups)
        at = lax.rem(step, groups)

        @pl.when(step == DEEP // group)
        def _():
            for z in far_first:
                sum_pair(z)

        @pl.when(step == groups)
        def _():
            exchange(0)
            clear()
            line_pass(3, 1, 1, 0)
            line_pass(0, -1, 2, 0)

        @pl.when(step == groups + 1)
        def _():
            finish_quarter(0)
            line_pass(3, 1, 1, 1)
            line_pass(0, -1, 2, 1)

        @pl.when(step == groups + 2)
        def _():
            line_pass(3, 1, 2, 0)
            line_pass(0, -1, 1, 0)
            line_pass(2, 1, 1, 0)
            line_pass(1, -1, 2, 0)

        @pl.when(step == groups + 3)
        def _():
            line_pass(3, 1, 2, 1)
            line_pass(0, -1, 1, 1)
            line_pass(2, 1, 1, 1)
            line_pass(1, -1, 2, 1)

        place = lax.rem(at, DEEP // group) * group
        mlp_group(turn, lax.div(at, DEEP // group), jnp.where(z_at == INNER[0], place, group - place))
        return carry

    @pl.when(inner)
    def _():
        clear()
        lax.fori_loop(0, 2 * groups, group_step, 0)
        exchange(1)

    def ada_pair():
        return remote(
            r.ada.at[core], r.ada.at[core], r.adass.at[DEEP - 1], r.adars.at[DEEP], partner
        )

    def ada_other():
        return remote(
            r.ada.at[other], r.ada.at[other], r.adass.at[DEEP - 1], r.adars.at[DEEP], partner
        )

    for z in range(DEEP):

        @pl.when(z_at != z)
        def _():
            remote(
                r.ada.at[core, z], r.ada.at[core, z], r.adass.at[0], r.adars.at[z], partner
            ).wait_recv()

    ada_pair().start()

    ada_other().wait_recv()
    entries = CORES * DEEP * micro * r.feat.shape[1]
    ada_rows = TEMB // (DEEP * CORES)
    pick = lax.broadcasted_iota(jnp.int32, (ada_rows, TEMB), 1) == (
        lax.broadcasted_iota(jnp.int32, (ada_rows, TEMB), 0) + member * ada_rows
    )
    features = r.ada[:, :, :, :, width:].reshape(entries, TEMB)
    gathered = r.ada[:, :, :, :, 0:width].reshape(entries, width)
    spreads = dot_nt(pick.astype(wide).astype(low), features)
    which = lax.rem(lax.broadcasted_iota(jnp.int32, (ada_rows, entries), 1), 8)
    for k in range(6):
        chosen = jnp.where(which == k, spreads, 0.0).astype(low)
        r.g_ada[:, k * width : (k + 1) * width] = dot_nn(chosen, gathered)

    @pl.when(inner)
    def _():
        finish_quarter(1)

    def finish(z):
        for piece in range(2):
            if z > 0:
                line_copy(z, 1, piece).wait_recv()
            if z < DEEP - 1:
                line_copy(z, -1, piece).wait_recv()
        total = sums(z)[...].astype(wide)
        if z > 0:
            total = total + slot_ref(z, 1)[...].astype(wide)
        if z < DEEP - 1:
            total = total + slot_ref(z, -1)[...].astype(wide)
        r.g_qkv[...] = total[:, 0:qkv_width]
        r.g_out[...] = total[:, qkv_width:]

    for z in range(DEEP):

        @pl.when(z_at == z)
        def _():
            finish(z)

    for q in range(DEEP):

        @pl.when(z_at != INNER[q // 2])
        def _():
            remote(
                r.pa.at[0, :, staged(1, 0)], r.land.at[q], r.css.at[0, 0], r.crs.at[q], partner
            ).wait_recv()
            r.g_up[:, q * part : (q + 1) * part] = r.land[q].astype(wide)

    @pl.when(jnp.logical_not(inner))
    def _():
        edge_copy().wait_recv()
        r.g_down[...] = r.frecv[0:half_part, :].astype(wide)

    for mb in range(micro):
        spread(r.a2, r.a2ss, r.a2rs, mb, True)
        spread(r.dy, r.dyss, r.dyrs, mb, True)
    for away in range(1, DEEP):
        ada_copy(away).wait_send()
    ada_pair().wait_send()
    for z in range(DEEP):
        pair_copy(z).wait_send()

        unsent = inner
        if z in (1, 2):
            unsent = jnp.logical_or(inner, z_at == (0 if z == 1 else DEEP - 1))

        @pl.when(jnp.logical_and(unsent, z_at != z))
        def _():
            for piece in range(2):
                line_copy(z, 1 if z > 0 else -1, piece).wait_send()

    @pl.when(inner)
    def _():
        edge_copy().wait_send()
        for turn in range(2):
            down_copy(turn).wait_send()
            for z in range(DEEP):
                up_copy(turn, z).wait_send()

                @pl.when(z_at != z)
                def _():
                    column_copy(turn, z).wait_send()


def run_chain(x, cot, long_count, timesteps, ada_weight, w_qkv, w_out, w_in, w_down, members):
    micro, rows, width = x.shape
    ff = w_in.shape[1]
    sections = lax.axis_size("section")
    fused = members == DEEP * CORES
    vmem = pl.BlockSpec(memory_space=pltpu.VMEM)
    hbm = pl.BlockSpec(memory_space=pl.ANY)
    dma = pltpu.SemaphoreType.DMA

    def kept(*shape):
        return jax.ShapeDtypeStruct(shape, low)

    def result(*shape):
        return jax.ShapeDtypeStruct(shape, wide)

    halves = rows // SHORT
    smem = pl.BlockSpec(memory_space=pltpu.SMEM)
    names = ["long", "steps", "x", "cot", "ada_h", "wqkv_h", "wout_h", "win_h", "wdown_h"]
    in_specs = [smem] * 2 + [vmem] * 2 + [hbm] * 5
    stored = {
        "dmod": result(micro, halves, 8, width),
        "a1": kept(micro, rows, width),
        "qkvo": kept(micro * rows, 4 * width),
        "dattn": kept(micro, rows, width),
        "a2": kept(micro, DEEP if fused else 1, rows, width),
        "du": kept(micro * rows, ff),
        "z": kept((1 if fused else micro + 1) * (ff // width), rows, width),
        "dy": kept(micro, DEEP if fused else 1, rows, width),
    }
    outs = {"fout": kept(2 * micro, rows, width), "gin": kept(micro, rows, width)}
    share = width // members
    if fused:
        outs["g_qkv"] = result(share, 3 * width)
        outs["g_out"] = result(share, width)
        outs["g_up"] = result(share, ff)
        outs["g_down"] = result(ff // members, width)
        outs["g_ada"] = result(TEMB // members, 6 * width)
    else:
        outs.update(stored)
    scratch = {
        "wa": pltpu.VMEM((width, 4 * width), low),
        "win": pltpu.VMEM((width, ff), low),
        "wdown": pltpu.VMEM((ff, width), low),
        "mod": pltpu.VMEM((micro, halves, 8, width), wide),
        "tags": pltpu.VMEM((2, micro, rows, 128), low),
        "feat": pltpu.VMEM((micro, 8 * halves, TEMB), low),
        "turn": pltpu.SemaphoreType.REGULAR,
        "msem": dma((6,)),
        "h": pltpu.VMEM((rows, width), wide),
        "m": pltpu.VMEM((rows, width), wide),
        "t": pltpu.VMEM((rows, width), wide),
        "do": pltpu.VMEM((rows, width), low),
        "n1": pltpu.VMEM((micro * rows, width), low),
        "n2": pltpu.VMEM((micro * rows, width), low),
        "r1": pltpu.VMEM((micro, rows, 1), wide),
        "r2": pltpu.VMEM((micro, rows, 1), wide),
        "y": pltpu.VMEM((micro, rows, width), low),
        "frecv": pltpu.VMEM((2 * micro * rows, width), low),
        "brecv": pltpu.VMEM((micro, rows, width), low),
        "wsem": dma((4,)),
        "fss": dma((2 * micro, rows // SHORT)),
        "frs": dma((2 * micro, rows // SHORT)),
        "bss": dma((micro, rows // SHORT)),
        "brs": dma((micro, rows // SHORT)),
    }
    if fused:
        part = ff // DEEP
        for name, value in stored.items():
            scratch[name] = pltpu.VMEM(value.shape, value.dtype)
        scratch.update(
            {
                "pa": pltpu.VMEM((DEEP, share, 4 * width), low),
                "pdown": pltpu.VMEM((part, width), wide),
                "pin": pltpu.VMEM((width, part), wide),
                "land2": pltpu.VMEM((DEEP * share + part // CORES, part), low),
                "slice": pltpu.VMEM((part // CORES, width), low),
                "land": pltpu.VMEM((DEEP, share, part), low),
                "ada": pltpu.VMEM((CORES, DEEP, micro, 8 * halves, width + TEMB), low),
                "free": pltpu.SemaphoreType.REGULAR,
                "done": pltpu.SemaphoreType.REGULAR,
                "a2ss": dma((micro, len(INNER))),
                "a2rs": dma((micro, DEEP)),
                "dyss": dma((micro, len(INNER))),
                "dyrs": dma((micro, DEEP)),
                "adass": dma((DEEP,)),
                "adars": dma((DEEP + 1,)),
                "pss": dma((DEEP,)),
                "prs": dma((DEEP,)),
                "lss": dma((DEEP, 2)),
                "lrs": dma((5, 2)),
                "mss": dma((2, DEEP + 1)),
                "mrs": dma((2, DEEP + 1)),
                "ess": dma((1,)),
                "ers": dma((1,)),
                "css": dma((2, DEEP)),
                "crs": dma((DEEP,)),
            }
        )
    names = names + list(outs) + list(scratch)
    values = pl.pallas_call(
        functools.partial(chain_kernel, names, sections, fused),
        out_shape=tuple(outs.values()),
        in_specs=in_specs,
        out_specs=(vmem,) * len(outs),
        scratch_shapes=list(scratch.values()),
        compiler_params=pltpu.CompilerParams(
            collective_id=0, has_side_effects=True, vmem_limit_bytes=60 * 1024 * 1024
        ),
    )(long_count, timesteps, x, cot, ada_weight, w_qkv, w_out, w_in, w_down)
    return SimpleNamespace(**dict(zip(outs, values)))


def time_features(timestep_ids):
    half_width = TEMB // 2
    frequency = jnp.exp(-math.log(10000.0) * jnp.arange(half_width, dtype=wide) / half_width)
    angles = timestep_ids.astype(wide)[:, None] * 0.1 * frequency[None, :]
    return jnp.concatenate([jnp.sin(angles), jnp.cos(angles)], axis=1)


def summed_apart(kept, features, micro, rows, width):
    def product(left, right):
        left = left.reshape(micro * rows, -1)
        right = right.reshape(micro * rows, -1)
        partial = dot_tn(left, right).astype(low)
        return lax.psum_scatter(partial, "dp", scatter_dimension=0, tiled=True).astype(wide)

    sums = kept.dmod[:, :, :6].reshape(features.shape[0], 6 * width)
    features_all = lax.all_gather(features.astype(wide), "dp", tiled=True)
    sums_all = lax.all_gather(sums, "dp", tiled=True)
    share = TEMB // lax.axis_size("dp")
    mine = lax.dynamic_slice_in_dim(features_all, lax.axis_index("dp") * share, share, 1)
    grad_ada = lax.dot_general(
        mine, sums_all, (((0,), (0,)), ((), ())), precision=lax.Precision.HIGHEST
    )
    return (
        product(kept.a1, kept.qkvo[:, : 3 * width]),
        product(kept.qkvo[:, 3 * width :], kept.dattn),
        product(kept.a2, kept.du),
        product(jnp.swapaxes(kept.z.reshape(micro + 1, -1, rows, width)[:micro], 1, 2), kept.dy),
        grad_ada,
    )


def on_device(inputs, cotangent, long_count, timesteps, w_qkv, w_out, w_in, w_down, ada_weight):
    micro = long_count.shape[1]
    width = inputs.shape[1]
    rows = inputs.shape[0] // micro
    halves = rows // SHORT
    members = lax.axis_size("dp")
    kept = run_chain(
        inputs.reshape(micro, rows, width),
        cotangent.reshape(micro, rows, width),
        long_count,
        timesteps,
        ada_weight[0],
        w_qkv[0],
        w_out[0],
        w_in[0],
        w_down[0],
        members,
    )
    if members == DEEP * CORES:
        hidden, grad_in, *grads = handed_over(
            (kept.fout, kept.gin, kept.g_qkv, kept.g_out, kept.g_up, kept.g_down, kept.g_ada)
        )
    else:
        is_long = (long_count[0] == 1)[:, None]
        half_steps = jnp.where(is_long, timesteps[0][:, :1], timesteps[0][:, :halves])
        features = time_features(half_steps.reshape(-1)).astype(low)
        grads = summed_apart(kept, features, micro, rows, width)
        hidden, grad_in = kept.fout[micro:], kept.gin
    hidden_out = hidden.reshape(1, micro * rows, width)
    grad_in = grad_in.reshape(1, micro * rows, width)
    return (hidden_out, grad_in) + tuple(grad[None] for grad in grads)


def handed_over(results):
    micro = results[1].shape[0]

    def kernel(*refs):
        count = len(results)
        sources, targets, holds = [refs[i * count : (i + 1) * count] for i in range(3)]
        sems = refs[-1]
        arrivals, departures = [], []
        for i in range(count):
            source = sources[i].at[pl.ds(micro, micro)] if i == 0 else sources[i]
            arrivals.append(pltpu.make_async_copy(source, holds[i], sems.at[0, i]))
            departures.append(pltpu.make_async_copy(holds[i], targets[i], sems.at[1, i]))
            arrivals[i].start()
        for i in range(count):
            arrivals[i].wait()
            departures[i].start()
        for copy in departures:
            copy.wait()

    shapes = [jax.ShapeDtypeStruct(value.shape, value.dtype) for value in results]
    shapes[0] = jax.ShapeDtypeStruct((micro,) + results[0].shape[1:], results[0].dtype)
    anywhere = pl.BlockSpec(memory_space=pl.ANY)
    return pl.pallas_call(
        kernel,
        out_shape=tuple(shapes),
        in_specs=[anywhere] * len(results),
        out_specs=[anywhere] * len(results),
        scratch_shapes=[pltpu.VMEM(shape.shape, shape.dtype) for shape in shapes]
        + [pltpu.SemaphoreType.DMA((2, len(results)))],
        compiler_params=pltpu.CompilerParams(vmem_limit_bytes=60 * 1024 * 1024),
    )(*results)


def solution(mesh):
    placed = (
        P("dp", None),
        P("dp", None),
        P("dp", None),
        P("dp", None, None),
        P("section", None, None),
        P("section", None, None),
        P("section", None, None),
        P("section", None, None),
        P("section", None, None),
    )
    return jax.shard_map(
        on_device,
        mesh=mesh,
        in_specs=placed,
        out_specs=(P("section", "dp", None),) * 7,
        check_vma=False,
    )
```

```python
import functools
import math
from types import SimpleNamespace

import jax
import jax.numpy as jnp
from jax import lax
from jax.experimental import pallas as pl
from jax.experimental.pallas import tpu as pltpu
from jax.sharding import PartitionSpec as P

HEADS = 12
TEMB = 128
SHORT = 128
TILE = 256
CHUNK = 64
CORES = 2
DEEP = 4
INNER = (1, 2)
norm_eps = 1e-06
MESH = pl.DeviceIdType.MESH
low = jnp.bfloat16
wide = jnp.float32


def dot_nn(a, b):
    return lax.dot_general(a, b, (((1,), (0,)), ((), ())), preferred_element_type=wide)


def dot_nt(a, b):
    return lax.dot_general(a, b, (((1,), (1,)), ((), ())), preferred_element_type=wide)


def dot_tn(a, b):
    return lax.dot_general(a, b, (((0,), (0,)), ((), ())), preferred_element_type=wide)


def fold(block):
    total = block[0:8]
    for start in range(8, block.shape[0], 8):
        total = total + block[start : start + 8]
    return total


GELU_C = math.sqrt(2.0 / math.pi)


def gelu(u):
    t = jnp.tanh(GELU_C * (u + 0.044715 * (u * u * u)))
    return 0.5 * u * (1.0 + t)


def gelu_both(u):
    square = u * u
    t = jnp.tanh(GELU_C * (u + 0.044715 * (square * u)))
    outer = 0.5 * (1.0 + t)
    slope = outer + 0.5 * u * (1.0 - t * t) * (GELU_C * (1.0 + (3.0 * 0.044715) * square))
    return u * outer, slope


def chain_kernel(names, sections, fused, *refs):
    r = SimpleNamespace(**dict(zip(names, refs)))
    micro, rows, width = r.x.shape
    ff = r.win.shape[1]
    qkv_width = 3 * width
    half_rows = SHORT

    def half_chunks(half):
        return range(half * half_rows, (half + 1) * half_rows, CHUNK)

    halves = rows // half_rows
    section = lax.axis_index("section")
    member = lax.axis_index("dp")
    z_at = lax.div(member, CORES)
    core = lax.rem(member, CORES)
    own = z_at if fused else 0
    right = lax.rem(section + 1, sections)
    left = lax.rem(section + sections - 1, sections)
    is_first = section == 0
    is_last = section == sections - 1

    maps = []
    for k in range(6):
        spot = pl.ds(k % 2 * TEMB, TEMB)
        copy = pltpu.make_async_copy(
            r.ada_h.at[:, pl.ds(k * width, width)], r.z.at[k // 2, spot, :], r.msem.at[k]
        )
        copy.start()
        maps.append(copy)

    loads = []
    for index, (hbm, vmem) in enumerate(
        (
            (r.wqkv_h, r.wa.at[:, 0:qkv_width]),
            (r.wout_h, r.wa.at[:, qkv_width:]),
            (r.win_h, r.win),
            (r.wdown_h, r.wdown),
        )
    ):
        loads.append(pltpu.make_async_copy(hbm, vmem, r.wsem.at[index]))
        if index == 0:
            loads[index].start()

    barrier = pltpu.get_barrier_semaphore()
    partner = (section, z_at * CORES + 1 - core)
    greeted = [(left, member), (right, member), partner]
    if fused:
        for away in range(1, DEEP):
            greeted.append((section, lax.rem(z_at + away, DEEP) * CORES + core))
    for target in greeted:
        pl.semaphore_signal(barrier, inc=1, device_id=target, device_id_type=MESH)
    pl.semaphore_wait(barrier, len(greeted))

    def remote(src, dst, send_sem, recv_sem, target):
        return pltpu.make_async_remote_copy(
            src_ref=src,
            dst_ref=dst,
            send_sem=send_sem,
            recv_sem=recv_sem,
            device_id=target,
            device_id_type=MESH,
        )

    def forward_copy(job, slot, half):
        span = pl.ds(half * half_rows, half_rows)
        landing = pl.ds(
            pl.multiple_of(slot * rows + half * half_rows, half_rows), half_rows
        )
        return remote(
            r.fout.at[job, span, :],
            r.frecv.at[landing, :],
            r.fss.at[job, half],
            r.frs.at[slot, half],
            (right, member),
        )

    def backward_copy(job, half):
        span = pl.ds(half * half_rows, half_rows)
        return remote(
            r.gin.at[job, span, :],
            r.brecv.at[job, span, :],
            r.bss.at[job, half],
            r.brs.at[job, half],
            (left, member),
        )

    def mod_row(mb, half, k):
        return r.mod[mb, half, pl.ds(k, 1), :]

    def mb_rows(mb):
        return pl.ds(pl.multiple_of(mb * rows, rows), rows)

    def mb_span(mb, start):
        return pl.ds(pl.multiple_of(mb * rows + start, CHUNK), CHUNK)

    lane = lax.broadcasted_iota(jnp.int32, (1, 128), 1)
    first_lanes = lane < 64
    masks = [first_lanes.astype(wide).astype(low), (1.0 - first_lanes.astype(wide)).astype(low)]
    scale = (width // HEADS) ** (-0.5)
    ones = jnp.ones((rows, 128), low)

    def spread(buffer, send_sems, recv_sems, mb, wait):
        for k, target in enumerate(INNER):

            @pl.when(z_at != target)
            def _():
                copy = remote(
                    buffer.at[mb, z_at],
                    buffer.at[mb, z_at],
                    send_sems.at[mb, k],
                    recv_sems.at[mb, z_at],
                    (section, target * CORES + core),
                )
                copy.wait_send() if wait else copy.start()

    def await_block(buffer, send_sems, recv_sems, mb, source):
        @pl.when(z_at != source)
        def _():
            remote(
                buffer.at[mb, source],
                buffer.at[mb, source],
                send_sems.at[mb, 0],
                recv_sems.at[mb, source],
                (section, member),
            ).wait_recv()

    def norm_forward(values, mb, half, k_shift, k_scale, n_keep, r_keep, out):
        for start in half_chunks(half):
            span = pl.ds(start, CHUNK)
            v = values(span)
            centered = v - jnp.mean(v, axis=-1, keepdims=True)
            inverse = lax.rsqrt(jnp.mean(centered * centered, axis=-1, keepdims=True) + norm_eps)
            n = centered * inverse
            n_keep[mb_span(mb, start), :] = n.astype(low)
            r_keep[mb, span, :] = inverse
            out[span, :] = (
                n * (1.0 + mod_row(mb, half, k_scale)) + mod_row(mb, half, k_shift)
            ).astype(low)

    r.dmod[...] = jnp.zeros_like(r.dmod)

    for mb in range(micro):
        long_row = (lane * 0 + r.long[0, mb]).astype(wide)
        for half in range(halves):
            here = (lane == 0).astype(wide)
            there = (lane == half).astype(wide)
            in_slot = long_row * here + (1.0 - long_row) * there
            barred = (lane < halves).astype(wide) * (1.0 - in_slot) * -1e30
            span = pl.ds(half * half_rows, half_rows)
            r.tags[0, mb, span, :] = jnp.broadcast_to(in_slot, (half_rows, 128)).astype(low)
            r.tags[1, mb, span, :] = jnp.broadcast_to(barred, (half_rows, 128)).astype(low)

    pairs = [(mb, half) for mb in range(micro) for half in range(halves)]
    row = lax.broadcasted_iota(jnp.int32, (8 * len(pairs), TEMB), 0)
    steps = jnp.zeros((8 * len(pairs), TEMB), jnp.int32)
    for i, (mb, half) in enumerate(pairs):
        flag = r.long[0, mb]
        chosen = flag * r.steps[0, mb, 0] + (1 - flag) * r.steps[0, mb, half]
        steps = jnp.where(row // 8 == i, chosen, steps)
    feature = lax.broadcasted_iota(jnp.int32, (8 * len(pairs), TEMB), 1)
    half_width = TEMB // 2
    position = lax.rem(feature, half_width).astype(wide)
    angles = steps.astype(wide) * 0.1 * jnp.exp(position * (-math.log(10000.0) / half_width))
    features = jnp.where(feature < half_width, jnp.sin(angles), jnp.cos(angles)).astype(low)
    r.feat[...] = features.reshape(micro, 8 * halves, TEMB)
    for copy in maps:
        copy.wait()
    for copy in loads[1:]:
        copy.start()
    for k in range(6):
        spot = pl.ds(k % 2 * TEMB, TEMB)
        found = dot_nn(features, r.z[k // 2, spot, :])
        for i, (mb, half) in enumerate(pairs):
            r.mod[mb, half, k : k + 1, :] = found[8 * i : 8 * i + 1, :]

    def forward_job(job, carry):
        mb = lax.rem(job, micro)
        here = mb_rows(mb)
        opening = jnp.logical_and(is_first, job == 0)

        @pl.when(jnp.logical_and(opening, core == 0))
        def _():
            pl.semaphore_wait(r.turn, 1)

        z_base = 0 if fused else mb * (ff // width)

        def wait_load(index):
            @pl.when(job == 0)
            def _():
                loads[index].wait()

        for half in range(halves):
            span = pl.ds(half * half_rows, half_rows)

            @pl.when(jnp.logical_or(jnp.logical_not(is_first), job >= micro))
            def _():
                forward_copy(job, job, half).wait_recv()

            def entering(part_span):
                begin = part_span.start
                given = pl.ds(pl.multiple_of(job * rows + begin, CHUNK), CHUNK)
                return given

            @pl.when(jnp.logical_and(is_first, job < micro))
            def _():
                def values(at):
                    h = r.x[mb, at, :].astype(wide)
                    r.h[at, :] = h
                    return h

                norm_forward(values, mb, half, 0, 1, r.n1, r.r1, r.a1.at[mb])

            @pl.when(jnp.logical_and(is_first, job >= micro))
            def _():
                def values(at):
                    h = r.x[mb, at, :].astype(wide) + r.frecv[entering(at), :].astype(wide)
                    r.h[at, :] = h
                    return h

                norm_forward(values, mb, half, 0, 1, r.n1, r.r1, r.a1.at[mb])

            @pl.when(jnp.logical_not(is_first))
            def _():
                def values(at):
                    h = r.frecv[entering(at), :].astype(wide)
                    r.h[at, :] = h
                    return h

                norm_forward(values, mb, half, 0, 1, r.n1, r.r1, r.a1.at[mb])

            if half == 0:
                wait_load(0)
            a1 = r.a1[mb, span, :]
            to = pl.ds(pl.multiple_of(mb * rows + half * half_rows, half_rows), half_rows)
            for c in range(0, qkv_width, TILE):
                r.qkvo[to, c : c + TILE] = dot_nn(a1, r.wa[:, c : c + TILE]).astype(low)

        q_tag = r.tags[0, mb]
        k_tag = r.tags[1, mb]

        def scores(c):
            q, k, v = [r.qkvo[here, i * width + c : i * width + c + 128] for i in range(3)]
            k_wide = jnp.concatenate([k, k_tag], axis=1)
            found = [
                dot_nt(jnp.concatenate([q * (mask * scale), q_tag], axis=1), k_wide)
                for mask in masks
            ]
            return found, jnp.concatenate([v, ones], axis=1)

        def mix(c, found, v_wide):
            weights = [jnp.exp(s - jnp.max(s, axis=1, keepdims=True)).astype(low) for s in found]
            mixed = [dot_nn(e, v_wide) for e in weights]
            top = jnp.where(first_lanes, mixed[0][:, 0:128], mixed[1][:, 0:128])
            total = jnp.where(first_lanes, mixed[0][:, 128:], mixed[1][:, 128:])
            r.do[:, c : c + 128] = (top * (1.0 / total)).astype(low)

        ahead = scores(0)
        for c in range(0, width, 128):
            current = ahead
            if c + 128 < width:
                ahead = scores(c + 128)
            mix(c, *current)
        @pl.when(jnp.logical_and(opening, core == 1))
        def _():
            pl.semaphore_signal(r.turn, inc=1, device_id=partner, device_id_type=MESH)

        wait_load(1)
        wait_load(2)
        wait_load(3)
        r.qkvo[here, qkv_width:] = r.do[...]
        for half in range(halves):
            span = pl.ds(half * half_rows, half_rows)
            to = pl.ds(pl.multiple_of(mb * rows + half * half_rows, half_rows), half_rows)
            o = r.do[span, :]
            for c in range(0, width, TILE):
                r.t[span, c : c + TILE] = dot_nn(o, r.wa[:, qkv_width + c : qkv_width + c + TILE])
            def residual(at):
                attn = r.t[at, :]
                r.dattn[mb, at, :] = attn.astype(low)
                m = r.h[at, :] + mod_row(mb, half, 2) * attn
                r.m[at, :] = m
                return m

            norm_forward(residual, mb, half, 3, 4, r.n2, r.r2, r.a2.at[mb, own])
            a2 = r.a2[mb, own, span, :]
            for c in range(0, ff, TILE):
                u = dot_nn(a2, r.win[:, c : c + TILE])
                r.du[to, c : c + TILE] = u.astype(low)
                at = c % width
                r.z[z_base + c // width, span, at : at + TILE] = gelu(u).astype(low)
            z = [r.z[z_base + i, span, :] for i in range(ff // width)]
            for c in range(0, width, TILE):
                y = dot_nn(z[0], r.wdown[0:width, c : c + TILE])
                for i in range(1, ff // width):
                    y = y + dot_nn(z[i], r.wdown[i * width : (i + 1) * width, c : c + TILE])
                r.t[span, c : c + TILE] = y
            for start in half_chunks(half):
                part = pl.ds(start, CHUNK)
                y = r.t[part, :]
                r.y[mb, part, :] = y.astype(low)
                r.fout[job, part, :] = (r.m[part, :] + mod_row(mb, half, 5) * y).astype(low)

            @pl.when(jnp.logical_or(jnp.logical_not(is_last), job < micro))
            def _():
                forward_copy(job, jnp.where(is_last, job + micro, job), half).start()


        if fused:

            @pl.when(job >= micro)
            def _():
                spread(r.a2, r.a2ss, r.a2rs, mb, False)

        return carry

    lax.fori_loop(0, 2 * micro, forward_job, 0)
    if fused:
        pl.semaphore_signal(
            r.done,
            inc=1,
            device_id=partner,
            device_id_type=MESH,
        )

    def norm_backward(mb, k_scale, n_keep, r_keep, base, per_chunk):
        for half in range(halves):
            shift_sum = jnp.zeros((8, width), wide)
            scale_sum = jnp.zeros((8, width), wide)
            gate_sum = jnp.zeros((8, width), wide)
            for start in half_chunks(half):
                span = pl.ds(start, CHUNK)
                da = r.t[span, :]
                n = n_keep[mb_span(mb, start), :].astype(wide)
                inverse = r_keep[mb, span, :]
                shift_sum = shift_sum + fold(da)
                scale_sum = scale_sum + fold(da * n)
                dn = da * (1.0 + mod_row(mb, half, k_scale))
                dv = inverse * (
                    dn
                    - jnp.mean(dn, axis=-1, keepdims=True)
                    - n * jnp.mean(dn * n, axis=-1, keepdims=True)
                )
                extra = per_chunk(span, half, base[span, :] + dv)
                if extra is not None:
                    gate_sum = gate_sum + fold(extra)
            r.dmod[mb, half, k_scale - 1, :] = jnp.sum(shift_sum, axis=0)
            r.dmod[mb, half, k_scale, :] = jnp.sum(scale_sum, axis=0)
            if k_scale == 4:
                r.dmod[mb, half, 2, :] = jnp.sum(gate_sum, axis=0)
            else:

                @pl.when(jnp.logical_not(is_first))
                def _():
                    backward_copy(mb, half).start()

    def backward_job(mb, carry):
        g_s = r.h
        here = mb_rows(mb)
        z_base = 0 if fused else micro * (ff // width)

        for half in range(halves):
            rows_of = pl.ds(half * half_rows, half_rows)

            @pl.when(is_last)
            def _():
                g_s[rows_of, :] = r.cot[mb, rows_of, :].astype(wide)

            @pl.when(jnp.logical_not(is_last))
            def _():
                backward_copy(mb, half).wait_recv()
                g_s[rows_of, :] = r.brecv[mb, rows_of, :].astype(wide)

            gate_sum = jnp.zeros((8, width), wide)
            for start in half_chunks(half):
                span = pl.ds(start, CHUNK)
                g = g_s[span, :]
                gate_sum = gate_sum + fold(g * r.y[mb, span, :].astype(wide))
                r.dy[mb, own, span, :] = (mod_row(mb, half, 5) * g).astype(low)
            r.dmod[mb, half, 5, :] = jnp.sum(gate_sum, axis=0)
        if fused:
            spread(r.dy, r.dyss, r.dyrs, mb, False)
        dy = r.dy[mb, own]
        for c in range(0, ff, TILE):
            dz = dot_nt(dy, r.wdown[c : c + TILE, :])
            u = r.du[mb_rows(mb), c : c + TILE].astype(wide)
            r.du[mb_rows(mb), c : c + TILE] = (gelu_both(u)[1] * dz).astype(low)
        du = r.du[mb_rows(mb), :]
        for c in range(0, width, TILE):
            r.t[:, c : c + TILE] = dot_nt(du, r.win[c : c + TILE, :])

        def after_mlp(span, half, dm):
            r.m[span, :] = dm
            extra = dm * r.dattn[mb, span, :].astype(wide)
            r.dattn[mb, span, :] = (mod_row(mb, half, 2) * dm).astype(low)
            return extra

        norm_backward(mb, 4, r.n2, r.r2, g_s, after_mlp)
        dattn = r.dattn[mb]
        for c in range(0, width, TILE):
            r.do[:, c : c + TILE] = dot_nt(dattn, r.wa[c : c + TILE, qkv_width:]).astype(low)
        q_tag = r.tags[0, mb]
        k_tag = r.tags[1, mb]

        def pulls(c):
            q, k, v = [r.qkvo[here, i * width + c : i * width + c + 128] for i in range(3)]
            do = r.do[:, c : c + 128]
            k_wide = jnp.concatenate([k, k_tag], axis=1)
            found = []
            for mask in masks:
                s = dot_nt(k_wide, jnp.concatenate([q * (mask * scale), q_tag], axis=1))
                found.append((s, dot_nt(v * mask, do)))
            return found, q, k, do

        def push(c, found, q, k, do):
            parts = []
            for s, dp in found:
                e = jnp.exp(s - jnp.max(s, axis=0, keepdims=True))
                p = e * (1.0 / jnp.sum(e, axis=0, keepdims=True))
                inner = jnp.sum(p * dp, axis=0, keepdims=True)
                ds = (p * (dp - inner)).astype(low)
                parts.append((dot_tn(ds, k), dot_nn(ds, q), dot_nn(p.astype(low), do)))
            for i, factor in enumerate((scale, scale, 1.0)):
                both = jnp.where(first_lanes, parts[0][i], parts[1][i])
                r.z[z_base + i, :, c : c + 128] = (both * factor).astype(low)

        ahead = pulls(0)
        for c in range(0, width, 128):
            current = ahead
            if c + 128 < width:
                ahead = pulls(c + 128)
            push(c, *current)
        dqkv = [r.z[z_base + i] for i in range(3)]
        for i in range(3):
            r.qkvo[here, i * width : (i + 1) * width] = dqkv[i]
        for c in range(0, width, TILE):
            pulled = dot_nt(dqkv[0], r.wa[c : c + TILE, 0:width])
            for i in range(1, 3):
                pulled = pulled + dot_nt(
                    dqkv[i], r.wa[c : c + TILE, i * width : (i + 1) * width]
                )
            r.t[:, c : c + TILE] = pulled

        def after_attention(span, half, dh):
            r.gin[mb, span, :] = dh.astype(low)

        norm_backward(mb, 1, r.n1, r.r1, r.m, after_attention)
        return carry

    lax.fori_loop(0, micro, backward_job, 0)

    if fused:
        gradient_tail(r, section, z_at, core, member, remote, spread, await_block)

    for half in range(halves):
        for job in range(2 * micro):

            @pl.when(jnp.logical_or(jnp.logical_not(is_last), job < micro))
            def _():
                forward_copy(job, job, half).wait_send()

        for job in range(micro):

            @pl.when(jnp.logical_not(is_first))
            def _():
                backward_copy(job, half).wait_send()


def gradient_tail(r, section, z_at, core, member, remote, spread, await_block):
    micro, rows, width = r.x.shape
    ff = r.win.shape[1]
    share = width // (DEEP * CORES)
    part = ff // DEEP
    half_part = part // CORES
    other = 1 - core
    partner = (section, z_at * CORES + other)
    qkv_width = 3 * width

    def on_z(z):
        return (section, z * CORES + core)

    for step in (1, -1):

        @pl.when(jnp.logical_and(z_at + step >= 0, z_at + step < DEEP))
        def _():
            pl.semaphore_signal(
                r.free,
                inc=1,
                device_id=on_z(jnp.clip(z_at + step, 0, DEEP - 1)),
                device_id_type=MESH,
            )

    mine = r.ada.at[core, z_at]
    for mb in range(micro):
        sums = r.dmod[mb]
        mine[mb, :, 0:width] = sums.reshape(sums.shape[0] * sums.shape[1], width).astype(low)
        mine[mb, :, width:] = r.feat[mb]

    def ada_copy(away):
        target = lax.rem(z_at + away, DEEP)
        return remote(
            mine, mine, r.adass.at[away - 1], r.adars.at[z_at], (section, target * CORES + core)
        )

    for away in range(1, DEEP):
        ada_copy(away).start()

    def flat(ref):
        block = ref[...]
        return block.reshape(micro * rows, block.shape[-1])

    def share_rows(z, of_core):
        return pl.ds(pl.multiple_of((z * CORES + of_core) * share, share), share)

    def pair_copy(z):
        return remote(
            r.wa.at[share_rows(z, other), :], r.pa.at[z], r.pss.at[z], r.prs.at[z], partner
        )

    a1_t = flat(r.a1).T
    o_t = r.qkvo[:, qkv_width:].T
    dattn = flat(r.dattn)
    both = CORES * share
    for pair in ((0, DEEP - 1), (1, DEEP - 2)):
        a1_rows, o_rows = [
            jnp.concatenate([side[z * both : (z + 1) * both] for z in pair], axis=0)
            for side in (a1_t, o_t)
        ]
        for c in range(0, 4 * width, TILE):
            if c < qkv_width:
                found = dot_nn(a1_rows, r.qkvo[:, c : c + TILE])
            else:
                found = dot_nn(o_rows, dattn[:, c - qkv_width : c - qkv_width + TILE])
            for i, z in enumerate(pair):
                r.wa[z * both : (z + 1) * both, c : c + TILE] = found[
                    i * both : (i + 1) * both
                ].astype(low)
        for z in pair:
            pair_copy(z).start()

    inner = jnp.logical_or(z_at == INNER[0], z_at == INNER[1])
    edge = jnp.where(z_at == INNER[0], 0, DEEP - 1)
    group = 2

    def quarter(turn):
        return jnp.where(turn == 0, edge, z_at)

    def mlp_group(turn, mb, first):
        for step in range(group):

            @pl.when(turn == 0)
            def _():
                await_block(r.a2, r.a2ss, r.a2rs, mb, first + step)
                await_block(r.dy, r.dyss, r.dyrs, mb, first + step)

        tokens = group * rows
        a2 = r.a2[mb, pl.ds(first, group)].reshape(tokens, width)
        dy = r.dy[mb, pl.ds(first, group)].reshape(tokens, width)
        for c in range(0, part, TILE):
            at = pl.ds(pl.multiple_of(quarter(turn) * part + c, TILE), TILE)
            u = dot_nn(a2, r.win[:, at])
            dz = dot_nt(dy, r.wdown[at, :])
            active, slope = gelu_both(u)
            r.z[0:group, :, c : c + TILE] = active.astype(low).reshape(group, rows, TILE)
            r.z[group:, :, c : c + TILE] = (slope * dz).astype(low).reshape(group, rows, TILE)
        z_t = r.z[0:group].reshape(tokens, part).T
        a2_t = a2.T
        for c in range(0, width, TILE):
            r.pdown[:, c : c + TILE] += dot_nn(z_t, dy[:, c : c + TILE])
        for c in range(0, part, TILE):
            up = dot_nn(a2_t, r.z[group:, :, c : c + TILE].reshape(tokens, TILE))
            r.pin[:, c : c + TILE] += up

    def sums(z):
        return r.qkvo.at[z * share : (z + 1) * share, :]

    def sum_pair(z):
        pair_copy(z).wait_recv()
        sums(z)[...] = (r.wa[share_rows(z, core), :].astype(wide) + r.pa[z].astype(wide)).astype(
            low
        )

    def slot_of(z, direction):
        if direction > 0:
            return z - 1
        return DEEP - 1 + z if z < DEEP - 2 else 0

    def slot_ref(z, direction):
        return r.du.at[pl.ds(slot_of(z, direction) * share, share), :]

    def line_copy(z, direction, piece):
        slot = slot_of(z, direction)
        columns = pl.ds(piece * 2 * width, 2 * width)
        return remote(
            sums(z).at[:, columns],
            slot_ref(z, direction).at[:, columns],
            r.lss.at[z, piece],
            r.lrs.at[slot, piece],
            on_z(jnp.clip(z_at + direction, 0, DEEP - 1)),
        )

    def line_pass(z, direction, at, piece):
        @pl.when(z_at == at)
        def _():
            line_copy(z, direction, piece).wait_recv()
            columns = slice(piece * 2 * width, (piece + 1) * 2 * width)
            sums(z)[:, columns] = (
                sums(z)[:, columns].astype(wide)
                + slot_ref(z, direction)[:, columns].astype(wide)
            ).astype(low)
            line_copy(z, direction, piece).start()

    for at in range(DEEP):

        @pl.when(z_at == at)
        def _():
            pl.semaphore_wait(r.free, (at > 0) + (at < DEEP - 1))

    far_first = (0, DEEP - 1, 1, DEEP - 2)

    @pl.when(jnp.logical_not(inner))
    def _():
        for z in far_first:
            sum_pair(z)

        def queue(direction):
            order = [(z, piece) for z in (3, 2, 1) for piece in range(2)]
            if direction < 0:
                order = [(DEEP - 1 - z, piece) for z, piece in order]
            for i, (z, piece) in enumerate(order):
                if i >= 2:
                    before, half = order[i - 2]
                    line_copy(before, direction, half).wait_send()
                line_copy(z, direction, piece).start()

        @pl.when(z_at == 0)
        def _():
            queue(1)

        @pl.when(z_at == DEEP - 1)
        def _():
            queue(-1)

    pl.semaphore_wait(r.done, 1)

    def staged(kind, turn):
        return pl.ds((kind * 2 + turn) * part, part)

    def landing(turn):
        return r.frecv if turn == 0 else r.land2

    def down_copy(turn):
        return remote(
            (r.n1, r.n2)[turn].at[pl.ds(0, half_part), :],
            landing(turn).at[pl.ds(DEEP * share, half_part), :],
            r.mss.at[turn, DEEP],
            r.mrs.at[turn, DEEP],
            partner,
        )

    def up_copy(turn, z):
        return remote(
            r.pa.at[z, :, staged(0, turn)],
            landing(turn).at[pl.ds(z * share, share), :],
            r.mss.at[turn, z],
            r.mrs.at[turn, z],
            partner,
        )

    def column_copy(turn, z):
        return remote(
            r.pa.at[z, :, staged(1, turn)],
            r.land.at[quarter(turn)],
            r.css.at[turn, z],
            r.crs.at[quarter(turn)],
            on_z(z),
        )

    def edge_copy():
        return remote(
            r.slice, r.frecv.at[pl.ds(0, half_part), :], r.ess.at[0], r.ers.at[0], on_z(edge)
        )

    def half_rows_of(which):
        return pl.ds(pl.multiple_of(which * half_part, half_part), half_part)

    def down_rows(z):
        return pl.ds(pl.multiple_of(core * half_part + z * share, share), share)

    def exchange(turn):
        for z in range(DEEP):
            r.pa[z, :, staged(0, turn)] = r.pin[share_rows(z, other), :].astype(low)
            up_copy(turn, z).start()
        (r.n1, r.n2)[turn][0:half_part, :] = r.pdown[half_rows_of(other), :].astype(low)
        down_copy(turn).start()
        for z in range(DEEP):
            r.wa[share_rows(z, core), 0:part] = r.pin[share_rows(z, core), :].astype(low)
            r.wa[share_rows(z, core), part : 2 * part] = r.pdown[down_rows(z), :].astype(low)

    def finish_quarter(turn):
        for z in range(DEEP):
            up_copy(turn, z).wait_recv()
            arrived = landing(turn)[z * share : (z + 1) * share, :].astype(wide)
            total = r.wa[share_rows(z, core), 0:part].astype(wide) + arrived

            @pl.when(z_at == z)
            def _():
                to = pl.ds(pl.multiple_of(quarter(turn) * part, part), part)
                r.g_up[:, to] = total

            @pl.when(z_at != z)
            def _():
                r.pa[z, :, staged(1, turn)] = total.astype(low)
                column_copy(turn, z).start()

        down_copy(turn).wait_recv()
        for z in range(DEEP):
            arrived = landing(turn)[(DEEP + z) * share : (DEEP + z + 1) * share, :].astype(wide)
            total = r.wa[share_rows(z, core), part : 2 * part].astype(wide) + arrived
            if turn == 0:
                r.slice[z * share : (z + 1) * share, :] = total.astype(low)
            else:
                r.g_down[z * share : (z + 1) * share, :] = total
        if turn == 0:
            edge_copy().start()

    def clear():
        r.pdown[...] = jnp.zeros_like(r.pdown)
        r.pin[...] = jnp.zeros_like(r.pin)

    groups = micro * DEEP // group

    def group_step(step, carry):
        turn = lax.div(step, groups)
        at = lax.rem(step, groups)

        @pl.when(step == DEEP // group)
        def _():
            for z in far_first:
                sum_pair(z)

        @pl.when(step == groups)
        def _():
            exchange(0)
            clear()
            line_pass(3, 1, 1, 0)
            line_pass(0, -1, 2, 0)

        @pl.when(step == groups + 1)
        def _():
            finish_quarter(0)
            line_pass(3, 1, 1, 1)
            line_pass(0, -1, 2, 1)

        @pl.when(step == groups + 2)
        def _():
            line_pass(3, 1, 2, 0)
            line_pass(0, -1, 1, 0)
            line_pass(2, 1, 1, 0)
            line_pass(1, -1, 2, 0)

        @pl.when(step == groups + 3)
        def _():
            line_pass(3, 1, 2, 1)
            line_pass(0, -1, 1, 1)
            line_pass(2, 1, 1, 1)
            line_pass(1, -1, 2, 1)

        place = lax.rem(at, DEEP // group) * group
        mlp_group(turn, lax.div(at, DEEP // group), jnp.where(z_at == INNER[0], place, group - place))
        return carry

    @pl.when(inner)
    def _():
        clear()
        lax.fori_loop(0, 2 * groups, group_step, 0)
        exchange(1)

    def ada_pair():
        return remote(
            r.ada.at[core], r.ada.at[core], r.adass.at[DEEP - 1], r.adars.at[DEEP], partner
        )

    def ada_other():
        return remote(
            r.ada.at[other], r.ada.at[other], r.adass.at[DEEP - 1], r.adars.at[DEEP], partner
        )

    for z in range(DEEP):

        @pl.when(z_at != z)
        def _():
            remote(
                r.ada.at[core, z], r.ada.at[core, z], r.adass.at[0], r.adars.at[z], partner
            ).wait_recv()

    ada_pair().start()

    ada_other().wait_recv()
    entries = CORES * DEEP * micro * r.feat.shape[1]
    ada_rows = TEMB // (DEEP * CORES)
    pick = lax.broadcasted_iota(jnp.int32, (ada_rows, TEMB), 1) == (
        lax.broadcasted_iota(jnp.int32, (ada_rows, TEMB), 0) + member * ada_rows
    )
    features = r.ada[:, :, :, :, width:].reshape(entries, TEMB)
    gathered = r.ada[:, :, :, :, 0:width].reshape(entries, width)
    spreads = dot_nt(pick.astype(wide).astype(low), features)
    which = lax.rem(lax.broadcasted_iota(jnp.int32, (ada_rows, entries), 1), 8)
    for k in range(6):
        chosen = jnp.where(which == k, spreads, 0.0).astype(low)
        r.g_ada[:, k * width : (k + 1) * width] = dot_nn(chosen, gathered)

    @pl.when(inner)
    def _():
        finish_quarter(1)

    def finish(z):
        for piece in range(2):
            if z > 0:
                line_copy(z, 1, piece).wait_recv()
            if z < DEEP - 1:
                line_copy(z, -1, piece).wait_recv()
        total = sums(z)[...].astype(wide)
        if z > 0:
            total = total + slot_ref(z, 1)[...].astype(wide)
        if z < DEEP - 1:
            total = total + slot_ref(z, -1)[...].astype(wide)
        r.g_qkv[...] = total[:, 0:qkv_width]
        r.g_out[...] = total[:, qkv_width:]

    for z in range(DEEP):

        @pl.when(z_at == z)
        def _():
            finish(z)

    for q in range(DEEP):

        @pl.when(z_at != INNER[q // 2])
        def _():
            remote(
                r.pa.at[0, :, staged(1, 0)], r.land.at[q], r.css.at[0, 0], r.crs.at[q], partner
            ).wait_recv()
            r.g_up[:, q * part : (q + 1) * part] = r.land[q].astype(wide)

    @pl.when(jnp.logical_not(inner))
    def _():
        edge_copy().wait_recv()
        r.g_down[...] = r.frecv[0:half_part, :].astype(wide)

    for mb in range(micro):
        spread(r.a2, r.a2ss, r.a2rs, mb, True)
        spread(r.dy, r.dyss, r.dyrs, mb, True)
    for away in range(1, DEEP):
        ada_copy(away).wait_send()
    ada_pair().wait_send()
    for z in range(DEEP):
        pair_copy(z).wait_send()

        unsent = inner
        if z in (1, 2):
            unsent = jnp.logical_or(inner, z_at == (0 if z == 1 else DEEP - 1))

        @pl.when(jnp.logical_and(unsent, z_at != z))
        def _():
            for piece in range(2):
                line_copy(z, 1 if z > 0 else -1, piece).wait_send()

    @pl.when(inner)
    def _():
        edge_copy().wait_send()
        for turn in range(2):
            down_copy(turn).wait_send()
            for z in range(DEEP):
                up_copy(turn, z).wait_send()

                @pl.when(z_at != z)
                def _():
                    column_copy(turn, z).wait_send()


def run_chain(x, cot, long_count, timesteps, ada_weight, w_qkv, w_out, w_in, w_down, members):
    micro, rows, width = x.shape
    ff = w_in.shape[1]
    sections = lax.axis_size("section")
    fused = members == DEEP * CORES
    vmem = pl.BlockSpec(memory_space=pltpu.VMEM)
    hbm = pl.BlockSpec(memory_space=pl.ANY)
    dma = pltpu.SemaphoreType.DMA

    def kept(*shape):
        return jax.ShapeDtypeStruct(shape, low)

    def result(*shape):
        return jax.ShapeDtypeStruct(shape, wide)

    halves = rows // SHORT
    smem = pl.BlockSpec(memory_space=pltpu.SMEM)
    names = ["long", "steps", "x", "cot", "ada_h", "wqkv_h", "wout_h", "win_h", "wdown_h"]
    in_specs = [smem] * 2 + [vmem] * 2 + [hbm] * 5
    stored = {
        "dmod": result(micro, halves, 8, width),
        "a1": kept(micro, rows, width),
        "qkvo": kept(micro * rows, 4 * width),
        "dattn": kept(micro, rows, width),
        "a2": kept(micro, DEEP if fused else 1, rows, width),
        "du": kept(micro * rows, ff),
        "z": kept((1 if fused else micro + 1) * (ff // width), rows, width),
        "dy": kept(micro, DEEP if fused else 1, rows, width),
    }
    outs = {"fout": kept(2 * micro, rows, width), "gin": kept(micro, rows, width)}
    share = width // members
    if fused:
        outs["g_qkv"] = result(share, 3 * width)
        outs["g_out"] = result(share, width)
        outs["g_up"] = result(share, ff)
        outs["g_down"] = result(ff // members, width)
        outs["g_ada"] = result(TEMB // members, 6 * width)
    else:
        outs.update(stored)
    scratch = {
        "wa": pltpu.VMEM((width, 4 * width), low),
        "win": pltpu.VMEM((width, ff), low),
        "wdown": pltpu.VMEM((ff, width), low),
        "mod": pltpu.VMEM((micro, halves, 8, width), wide),
        "tags": pltpu.VMEM((2, micro, rows, 128), low),
        "feat": pltpu.VMEM((micro, 8 * halves, TEMB), low),
        "turn": pltpu.SemaphoreType.REGULAR,
        "msem": dma((6,)),
        "h": pltpu.VMEM((rows, width), wide),
        "m": pltpu.VMEM((rows, width), wide),
        "t": pltpu.VMEM((rows, width), wide),
        "do": pltpu.VMEM((rows, width), low),
        "n1": pltpu.VMEM((micro * rows, width), low),
        "n2": pltpu.VMEM((micro * rows, width), low),
        "r1": pltpu.VMEM((micro, rows, 1), wide),
        "r2": pltpu.VMEM((micro, rows, 1), wide),
        "y": pltpu.VMEM((micro, rows, width), low),
        "frecv": pltpu.VMEM((2 * micro * rows, width), low),
        "brecv": pltpu.VMEM((micro, rows, width), low),
        "wsem": dma((4,)),
        "fss": dma((2 * micro, rows // SHORT)),
        "frs": dma((2 * micro, rows // SHORT)),
        "bss": dma((micro, rows // SHORT)),
        "brs": dma((micro, rows // SHORT)),
    }
    if fused:
        part = ff // DEEP
        for name, value in stored.items():
            scratch[name] = pltpu.VMEM(value.shape, value.dtype)
        scratch.update(
            {
                "pa": pltpu.VMEM((DEEP, share, 4 * width), low),
                "pdown": pltpu.VMEM((part, width), wide),
                "pin": pltpu.VMEM((width, part), wide),
                "land2": pltpu.VMEM((DEEP * share + part // CORES, part), low),
                "slice": pltpu.VMEM((part // CORES, width), low),
                "land": pltpu.VMEM((DEEP, share, part), low),
                "ada": pltpu.VMEM((CORES, DEEP, micro, 8 * halves, width + TEMB), low),
                "free": pltpu.SemaphoreType.REGULAR,
                "done": pltpu.SemaphoreType.REGULAR,
                "a2ss": dma((micro, len(INNER))),
                "a2rs": dma((micro, DEEP)),
                "dyss": dma((micro, len(INNER))),
                "dyrs": dma((micro, DEEP)),
                "adass": dma((DEEP,)),
                "adars": dma((DEEP + 1,)),
                "pss": dma((DEEP,)),
                "prs": dma((DEEP,)),
                "lss": dma((DEEP, 2)),
                "lrs": dma((5, 2)),
                "mss": dma((2, DEEP + 1)),
                "mrs": dma((2, DEEP + 1)),
                "ess": dma((1,)),
                "ers": dma((1,)),
                "css": dma((2, DEEP)),
                "crs": dma((DEEP,)),
            }
        )
    names = names + list(outs) + list(scratch)
    values = pl.pallas_call(
        functools.partial(chain_kernel, names, sections, fused),
        out_shape=tuple(outs.values()),
        in_specs=in_specs,
        out_specs=(vmem,) * len(outs),
        scratch_shapes=list(scratch.values()),
        compiler_params=pltpu.CompilerParams(
            collective_id=0, has_side_effects=True, vmem_limit_bytes=60 * 1024 * 1024
        ),
    )(long_count, timesteps, x, cot, ada_weight, w_qkv, w_out, w_in, w_down)
    return SimpleNamespace(**dict(zip(outs, values)))


def time_features(timestep_ids):
    half_width = TEMB // 2
    frequency = jnp.exp(-math.log(10000.0) * jnp.arange(half_width, dtype=wide) / half_width)
    angles = timestep_ids.astype(wide)[:, None] * 0.1 * frequency[None, :]
    return jnp.concatenate([jnp.sin(angles), jnp.cos(angles)], axis=1)


def summed_apart(kept, features, micro, rows, width):
    def product(left, right):
        left = left.reshape(micro * rows, -1)
        right = right.reshape(micro * rows, -1)
        partial = dot_tn(left, right).astype(low)
        return lax.psum_scatter(partial, "dp", scatter_dimension=0, tiled=True).astype(wide)

    sums = kept.dmod[:, :, :6].reshape(features.shape[0], 6 * width)
    features_all = lax.all_gather(features.astype(wide), "dp", tiled=True)
    sums_all = lax.all_gather(sums, "dp", tiled=True)
    share = TEMB // lax.axis_size("dp")
    mine = lax.dynamic_slice_in_dim(features_all, lax.axis_index("dp") * share, share, 1)
    grad_ada = lax.dot_general(
        mine, sums_all, (((0,), (0,)), ((), ())), precision=lax.Precision.HIGHEST
    )
    return (
        product(kept.a1, kept.qkvo[:, : 3 * width]),
        product(kept.qkvo[:, 3 * width :], kept.dattn),
        product(kept.a2, kept.du),
        product(jnp.swapaxes(kept.z.reshape(micro + 1, -1, rows, width)[:micro], 1, 2), kept.dy),
        grad_ada,
    )


def on_device(inputs, cotangent, long_count, timesteps, w_qkv, w_out, w_in, w_down, ada_weight):
    micro = long_count.shape[1]
    width = inputs.shape[1]
    rows = inputs.shape[0] // micro
    halves = rows // SHORT
    members = lax.axis_size("dp")
    kept = run_chain(
        inputs.reshape(micro, rows, width),
        cotangent.reshape(micro, rows, width),
        long_count,
        timesteps,
        ada_weight[0],
        w_qkv[0],
        w_out[0],
        w_in[0],
        w_down[0],
        members,
    )
    if members == DEEP * CORES:
        hidden, grad_in, *grads = handed_over(
            (kept.fout, kept.gin, kept.g_qkv, kept.g_out, kept.g_up, kept.g_down, kept.g_ada)
        )
    else:
        is_long = (long_count[0] == 1)[:, None]
        half_steps = jnp.where(is_long, timesteps[0][:, :1], timesteps[0][:, :halves])
        features = time_features(half_steps.reshape(-1)).astype(low)
        grads = summed_apart(kept, features, micro, rows, width)
        hidden, grad_in = kept.fout[micro:], kept.gin
    hidden_out = hidden.reshape(1, micro * rows, width)
    grad_in = grad_in.reshape(1, micro * rows, width)
    return (hidden_out, grad_in) + tuple(grad[None] for grad in grads)


def handed_over(results):
    micro = results[1].shape[0]

    def kernel(*refs):
        count = len(results)
        sources, targets, holds = [refs[i * count : (i + 1) * count] for i in range(3)]
        sems = refs[-1]
        arrivals, departures = [], []
        for i in range(count):
            source = sources[i].at[pl.ds(micro, micro)] if i == 0 else sources[i]
            arrivals.append(pltpu.make_async_copy(source, holds[i], sems.at[0, i]))
            departures.append(pltpu.make_async_copy(holds[i], targets[i], sems.at[1, i]))
            arrivals[i].start()
        for i in range(count):
            arrivals[i].wait()
            departures[i].start()
        for copy in departures:
            copy.wait()

    shapes = [jax.ShapeDtypeStruct(value.shape, value.dtype) for value in results]
    shapes[0] = jax.ShapeDtypeStruct((micro,) + results[0].shape[1:], results[0].dtype)
    anywhere = pl.BlockSpec(memory_space=pl.ANY)
    return pl.pallas_call(
        kernel,
        out_shape=tuple(shapes),
        in_specs=[anywhere] * len(results),
        out_specs=[anywhere] * len(results),
        scratch_shapes=[pltpu.VMEM(shape.shape, shape.dtype) for shape in shapes]
        + [pltpu.SemaphoreType.DMA((2, len(results)))],
        compiler_params=pltpu.CompilerParams(vmem_limit_bytes=60 * 1024 * 1024),
    )(*results)


def solution(mesh):
    placed = (
        P("dp", None),
        P("dp", None),
        P("dp", None),
        P("dp", None, None),
        P("section", None, None),
        P("section", None, None),
        P("section", None, None),
        P("section", None, None),
        P("section", None, None),
    )
    return jax.shard_map(
        on_device,
        mesh=mesh,
        in_specs=placed,
        out_specs=(P("section", "dp", None),) * 7,
        check_vma=False,
    )
```
